32 devices in a mesh: seq: 16 (over z, y, x), mp: 2 (over core).
Axes of the slice: x: 2, y: 2, z: 4, core: 2. Of those that a mesh axis runs over, the one named last changes fastest.
Arguments:
- tokens: bfloat16 [3, 2048, 2048], P(None, 'seq'), may hold values from -6 to 6
- norm1_gain: float32 [2048], replicated, may hold values from 0.25 to 1.75
- in_weight: bfloat16 [2048, 3, 2048], P(None, None, 'mp'), may hold values from -0.125 to 0.125
- conv_weight: float32 [3, 2048], P(None, 'mp'), may hold values from 0.6 to 1.4
- out_weight: bfloat16 [2048, 2048], P('mp'), may hold values from -0.125 to 0.125
- norm2_gain: float32 [2048], replicated, may hold values from 0.25 to 1.75
- gate_up: bfloat16 [2048, 2, 8192], P(None, None, 'mp'), may hold values from -0.125 to 0.125
- down_weight: bfloat16 [8192, 2048], P('mp'), may hold values from -0.125 to 0.125
- cotangent: bfloat16 [3, 2048, 2048], P(None, 'seq'), may hold values from -6 to 6
Outputs:
- output: bfloat16 [3, 2048, 2048], P(None, 'seq')
- tokens_grad: bfloat16 [3, 2048, 2048], P(None, 'seq')
- norm1_gain_grad: float32 [2048], replicated
- in_weight_grad: float32 [2048, 3, 2048], P('seq', None, 'mp')
- conv_weight_grad: float32 [3, 2048], P(None, 'mp')
- out_weight_grad: float32 [2048, 2048], P('mp', 'seq')
- norm2_gain_grad: float32 [2048], replicated
- gate_up_grad: float32 [2048, 2, 8192], P('seq', None, 'mp')
- down_weight_grad: float32 [8192, 2048], P('mp', 'seq')
The draws below stay inside these ranges and needn't reach their ends.
All inputs are finite; a program needn't handle non-finite values.
Results may differ from the reference program's by a relative error of at most 0.02.
Values may be sent and summed in bfloat16 or wider, within the bound.
No kernel may reach another device: no remote copies, remote signals or barrier semaphores. Data moves between devices by JAX's collectives and lax.ppermute only.
A program may use at most 320 MiB of HBM per device.

```python
import jax
import jax.numpy as jnp
from jax import lax

D = 2048
FF = 8192
SEQS = 3
LEN = 2048


def levels(key, dims, pieces, smallest, largest):
    def one(axis_at, blocks):
        steps = jax.random.uniform(jax.random.fold_in(jax.random.fold_in(key, 6), axis_at), (blocks,), jnp.float32, smallest / len(pieces), largest / len(pieces))
        return jnp.repeat(jnp.exp(steps), dims[axis_at] // blocks).reshape((-1,) + (1,) * (len(dims) - axis_at - 1))

    loudness = one(*pieces[0])
    for cut in pieces[1:]:
        loudness = loudness * one(*cut)
    return loudness


def bell_draw(stream_key, extent, deviation, reach, shards=(), held_as=jnp.bfloat16):
    entries = jax.random.normal(stream_key, extent, jnp.float32) * deviation
    if len(shards) > 0:
        entries = levels(stream_key, extent, shards, -0.22, 0.18) * entries
    return jnp.clip(entries, min=-reach, max=reach).astype(held_as)


def setup_inputs(seed: int = 0) -> dict:
    keys = jax.random.split(jax.random.key(seed), 10)
    tokens = bell_draw(keys[0], (SEQS, LEN, D), 1.0, 6.0, ((1, 16),))
    norm1_gain = jnp.clip(1.0 + 0.15 * jax.random.normal(keys[1], (D,), jnp.float32), 0.25, 1.75)
    in_weight = bell_draw(keys[2], (D, 3, D), D ** -0.5, 0.125, ((2, 2),))
    conv_weight = jnp.clip(0.6 + 0.79999995 * jax.random.uniform(keys[3], (3, D), jnp.float32) ** levels(keys[3], (3, D), ((1, 2),), -0.2, 0.2), 0.6, 1.4)
    out_weight = bell_draw(keys[4], (D, D), D ** -0.5, 0.125, ((0, 2),))
    norm2_gain = jnp.clip(1.0 + 0.15 * jax.random.normal(keys[5], (D,), jnp.float32), 0.25, 1.75)
    gate_up = bell_draw(keys[6], (D, 2, FF), D ** -0.5, 0.125, ((2, 2),))
    down_weight = bell_draw(keys[7], (FF, D), (FF // 4) ** -0.5, 0.125, ((0, 2),))
    cotangent = bell_draw(keys[8], (SEQS, LEN, D), 1.0, 6.0, ((1, 16),))
    return {"tokens": tokens, "norm1_gain": norm1_gain, "in_weight": in_weight, "conv_weight": conv_weight, "out_weight": out_weight, "norm2_gain": norm2_gain, "gate_up": gate_up, "down_weight": down_weight, "cotangent": cotangent}


epsilon = 1e-05

@jax.custom_vjp
def low(v):
    return lax.optimization_barrier(v.astype(jnp.bfloat16)).astype(jnp.float32)

@jax.custom_vjp
def low_back(v):
    return v

def low_keep(v):
    return (low(v), None)

def low_pass(kept, grad):
    return (grad,)

def back_keep(v):
    return (v, None)

def back_low(kept, grad):
    return (low(grad),)
low.defvjp(low_keep, low_pass)
low_back.defvjp(back_keep, back_low)

def rms_norm(values, gain_vec):
    inv_rms = lax.rsqrt(lax.optimization_barrier(jnp.mean(values * values, axis=-1, keepdims=True)) + epsilon)
    return values * inv_rms * gain_vec

def mixer_block(sequence, norm1_gain, in_weight, conv_weight, out_weight, norm2_gain, gate_up, down_weight):
    highest = lax.Precision.HIGHEST
    normed_one = low(rms_norm(sequence, norm1_gain))
    projected = low_back(jnp.einsum('td,dkn->tkn', normed_one, in_weight, precision=highest))
    b_gate = projected[:, 0]
    c_gate = projected[:, 1]
    values = projected[:, 2]
    product = b_gate * values
    padded = jnp.concatenate([jnp.zeros((2, product.shape[1]), jnp.float32), product], axis=0)
    conv_out = conv_weight[0] * padded[:-2] + conv_weight[1] * padded[1:-1] + conv_weight[2] * padded[2:]
    mixed_rows = low(c_gate * conv_out)
    inner_sum = sequence + low_back(jnp.dot(mixed_rows, out_weight, precision=highest))
    normed_two = low(rms_norm(inner_sum, norm2_gain))
    hidden_pre = low_back(jnp.einsum('td,dkf->tkf', normed_two, gate_up, precision=highest))
    activation = low(jax.nn.silu(hidden_pre[:, 0]) * hidden_pre[:, 1])
    return inner_sum + low_back(jnp.dot(activation, down_weight, precision=highest))

def forward(tokens, norm1_gain, in_weight, conv_weight, out_weight, norm2_gain, gate_up, down_weight):

    def one_sequence(carry_value, sequence):
        return (carry_value, mixer_block(sequence, norm1_gain, in_weight, conv_weight, out_weight, norm2_gain, gate_up, down_weight))
    _, outputs = lax.scan(jax.checkpoint(one_sequence), jnp.zeros((), jnp.float32), tokens)
    return outputs

def reference(tokens, norm1_gain, in_weight, conv_weight, out_weight, norm2_gain, gate_up, down_weight, cotangent):
    primals = (tokens.astype(jnp.float32), norm1_gain, in_weight.astype(jnp.float32), conv_weight, out_weight.astype(jnp.float32), norm2_gain, gate_up.astype(jnp.float32), down_weight.astype(jnp.float32))
    outputs, pullback = jax.vjp(forward, *primals)
    grads = pullback(cotangent.astype(jnp.float32))
    return (outputs.astype(jnp.bfloat16), grads[0].astype(jnp.bfloat16), grads[1], grads[2], grads[3], grads[4], grads[5], grads[6], grads[7])
```

```python
import jax
import jax.numpy as jnp
from jax import lax
from jax.sharding import Mesh, PartitionSpec as P

epsilon = 1e-05
low = jnp.bfloat16
full = jnp.float32


def swapped(block, axis):
    return lax.ppermute(block, axis, [(0, 1), (1, 0)])


def passed_along(block, axis, distance):
    devices = range(lax.axis_size(axis))
    route = [(i - distance, i) for i in devices if i - distance in devices]
    return lax.ppermute(block, axis, route)


def turned(block, axis, distance):
    count = lax.axis_size(axis)
    return lax.ppermute(block, axis, [(i, (i + distance) % count) for i in range(count)])


def others(block, axis):
    return [turned(block, axis, step) for step in range(1, lax.axis_size(axis))]


def summed(partial, axis):
    partial = partial.astype(low)
    if lax.axis_size(axis) == 2:
        return partial.astype(full) + swapped(partial, axis).astype(full)
    return lax.psum(partial, axis).astype(full)


def share_of(rows):
    count = rows.shape[0] // lax.axis_size("mp")
    return lax.dynamic_slice_in_dim(rows, lax.axis_index("mp") * count, count, 0)


def cube_gather(mine):
    third = mine.shape[0] // 3
    from_b, from_c, from_d = (swapped(mine, axis) for axis in "bcd")
    from_bc, from_cd, from_bd = swapped(from_b, "c"), swapped(from_c, "d"), swapped(from_d, "b")
    far = [
        swapped(from_bc[:third], "d"),
        swapped(from_cd[third : 2 * third], "b"),
        swapped(from_bd[2 * third :], "c"),
    ]
    pieces = [mine, from_b, from_c, from_d, from_bc, from_cd, from_bd] + far
    gathered = []
    for piece in pieces:
        gathered += [piece] + others(piece, "mp")
    return jnp.concatenate(gathered, axis=0)


def normalize(values, gain_vec):
    inv_rms = lax.rsqrt(jnp.mean(values * values, axis=-1, keepdims=True) + epsilon)
    return (values * inv_rms * gain_vec, inv_rms)


def norm_back(values, inv_rms, gain_vec, upstream):
    scaled = values * inv_rms
    weighted = upstream * gain_vec
    inner_mean = jnp.mean(weighted * scaled, axis=-1, keepdims=True)
    return inv_rms * (weighted - scaled * inner_mean)


def dot(left, right, dims):
    return lax.dot_general(left, right, (dims, ((), ())), preferred_element_type=full)


def hidden_terms(gate_pre, up_pre, activation_grad):
    sigmoid_gate = jax.nn.sigmoid(gate_pre)
    swish_gate = gate_pre * sigmoid_gate
    gate_grad = activation_grad * up_pre * sigmoid_gate * (1.0 + gate_pre * (1.0 - sigmoid_gate))
    return (
        (swish_gate * up_pre).astype(low),
        gate_grad.astype(low),
        (activation_grad * swish_gate).astype(low),
    )


def local(
    tokens,
    norm1_gain,
    in_weight,
    conv_weight,
    out_weight,
    norm2_gain,
    gate_up,
    down_weight,
    cotangent,
):
    seq_count, local_len, width = tokens.shape
    row_total = seq_count * local_len
    channels = in_weight.shape[2]
    hidden = gate_up.shape[2]
    parts = lax.axis_size("a")
    shard = width // (parts * 8)
    blocked = (seq_count, local_len, channels)
    inputs = tokens.reshape(row_total, width).astype(full)
    upstream = cotangent.reshape(row_total, width)
    upstream_all = cube_gather(share_of(upstream))

    normed_full_one, inv_rms_one = normalize(inputs, norm1_gain)
    normed_one = normed_full_one.astype(low)
    b_gate = dot(normed_one, in_weight[:, 0], ((1,), (0,))).reshape(blocked)
    values = dot(normed_one, in_weight[:, 2], ((1,), (0,))).reshape(blocked)
    product = b_gate * values
    carried = passed_along(product[:, local_len - 2 :], ("a", "b", "c", "d"), 1)
    c_gate = dot(normed_one, in_weight[:, 1], ((1,), (0,))).reshape(blocked)
    extended = jnp.concatenate([carried, product], axis=1)
    conv_out = (
        conv_weight[0] * extended[:, :local_len]
        + conv_weight[1] * extended[:, 1 : local_len + 1]
        + conv_weight[2] * extended[:, 2:]
    )
    mixed = (c_gate * conv_out).astype(low).reshape(row_total, channels)
    inner_sum = inputs + summed(dot(mixed, out_weight, ((1,), (0,))), "mp")
    normed_full_two, inv_rms_two = normalize(inner_sum, norm2_gain)
    normed_two = normed_full_two.astype(low)
    normed_two_all = cube_gather(share_of(normed_two))

    gate_weight, up_weight = gate_up[:, 0], gate_up[:, 1]
    activation, gate_grad, up_grad = hidden_terms(
        dot(normed_two, gate_weight, ((1,), (0,))),
        dot(normed_two, up_weight, ((1,), (0,))),
        dot(upstream, down_weight, ((1,), (1,))),
    )
    activation, gate_grad, up_grad = lax.optimization_barrier((activation, gate_grad, up_grad))
    normed_two_grad = summed(
        dot(gate_grad, gate_weight, ((1,), (1,))) + dot(up_grad, up_weight, ((1,), (1,))), "mp"
    )
    output = (inner_sum + summed(dot(activation, down_weight, ((1,), (0,))), "mp")).astype(low)

    place = lax.axis_index(("b", "c", "d"))
    chunk_count = max(1, hidden // 1024)
    strip = hidden // (8 * chunk_count)

    def my_columns(weight):
        strips = weight.reshape(width, chunk_count, 8, strip)
        return lax.dynamic_index_in_dim(strips, place, 2, False).reshape(width, -1)

    my_down = lax.dynamic_index_in_dim(
        down_weight.reshape(chunk_count, 8, strip, width), place, 1, False
    ).reshape(-1, width)
    all_act, all_gate, all_up = lax.optimization_barrier(
        hidden_terms(
            dot(normed_two_all, my_columns(gate_weight), ((1,), (0,))),
            dot(normed_two_all, my_columns(up_weight), ((1,), (0,))),
            dot(upstream_all, my_down, ((1,), (1,))),
        )
    )
    half_width = width // parts
    turn = lax.axis_index("a")

    def columns_for(step):
        start = (turn + step) % parts * half_width
        return [
            lax.dynamic_slice_in_dim(array, start, half_width, 1)
            for array in (normed_two_all, upstream_all)
        ]

    parted = [columns_for(step) for step in range(parts)]
    gate_up_pieces, down_pieces = [], []
    for chunk in range(chunk_count):
        span = slice(chunk * strip, (chunk + 1) * strip)

        def terms(step):
            normed_part, upstream_part = parted[step]
            return jnp.concatenate(
                [
                    dot(normed_part, all_gate[:, span], ((0,), (0,))),
                    dot(normed_part, all_up[:, span], ((0,), (0,))),
                    dot(upstream_part, all_act[:, span], ((0,), (0,))),
                ],
                axis=1,
            )

        arrived = [turned(terms(step).astype(low), "a", step) for step in range(1, parts)]
        total = terms(0)
        for term in arrived:
            total = total + term.astype(full)
        placed = lax.all_to_all(
            total.astype(low).reshape(8, shard, 3 * strip), ("b", "c", "d"), 0, 0, tiled=True
        ).astype(full)
        pair = placed[:, :, : 2 * strip].reshape(8, shard, 2, strip)
        gate_up_pieces.append(pair.transpose(1, 2, 0, 3).reshape(shard, 2, 8 * strip))
        down_pieces.append(placed[:, :, 2 * strip :].transpose(0, 2, 1).reshape(8 * strip, shard))
    gate_up_total = jnp.concatenate(gate_up_pieces, axis=2)
    down_total = jnp.concatenate(down_pieces, axis=0)

    inner_grad = upstream.astype(full) + norm_back(
        inner_sum, inv_rms_two, norm2_gain, normed_two_grad
    )
    gain_two = jnp.sum(share_of(normed_two_grad * inner_sum * inv_rms_two), axis=0)
    branch_grad = inner_grad.astype(low)
    mixed_grad = dot(branch_grad, out_weight, ((1,), (1,))).reshape(blocked)
    conv_grad_in = mixed_grad * c_gate
    later = passed_along(conv_grad_in[:, :2], ("a", "b", "c", "d"), -1)
    c_gate_grad = mixed_grad * conv_out
    grad_extended = jnp.concatenate([conv_grad_in, later], axis=1)
    product_grad = (
        conv_weight[2] * grad_extended[:, :local_len]
        + conv_weight[1] * grad_extended[:, 1 : local_len + 1]
        + conv_weight[0] * grad_extended[:, 2:]
    )
    taps_grad = jnp.stack(
        [
            jnp.sum(conv_grad_in * extended[:, tap : tap + local_len], axis=(0, 1))
            for tap in range(3)
        ]
    )
    projected_grad = [
        grad.astype(low).reshape(row_total, channels)
        for grad in (product_grad * values, c_gate_grad, product_grad * b_gate)
    ]
    normed_one_grad = summed(
        sum(dot(projected_grad[k], in_weight[:, k], ((1,), (1,))) for k in range(3)), "mp"
    )
    tokens_grad = (inner_grad + norm_back(inputs, inv_rms_one, norm1_gain, normed_one_grad)).astype(
        low
    )
    gain_one = jnp.sum(share_of(normed_one_grad * inputs * inv_rms_one), axis=0)

    slices = jnp.stack(
        [array.reshape(row_total, 4, channels // 4) for array in projected_grad + [mixed]], axis=2
    ).transpose(1, 0, 2, 3)
    slices = lax.all_to_all(
        slices.reshape(4, row_total, channels), ("c", "d"), 0, 0, tiled=True
    ).reshape(4 * row_total, channels)
    normed_one_all = lax.all_gather(share_of(normed_one), ("c", "d", "mp"), axis=0, tiled=True)
    branch_all = lax.all_gather(share_of(branch_grad), ("c", "d", "mp"), axis=0, tiled=True)
    cut = 3 * (channels // 4)
    mixer_terms = jnp.concatenate(
        [
            dot(normed_one_all, slices[:, :cut], ((0,), (0,))),
            dot(branch_all, slices[:, cut:], ((0,), (0,))),
        ],
        axis=1,
    ).astype(low)
    mixer_terms = lax.psum_scatter(mixer_terms, ("a", "b"), scatter_dimension=0, tiled=True)
    mixer_terms = lax.all_to_all(
        mixer_terms.reshape(4, shard, channels), ("c", "d"), 0, 0, tiled=True
    ).astype(full)
    in_total = (
        mixer_terms[:, :, :cut]
        .reshape(4, shard, 3, channels // 4)
        .transpose(1, 2, 0, 3)
        .reshape(shard, 3, channels)
    )
    out_total = mixer_terms[:, :, cut:].transpose(0, 2, 1).reshape(channels, shard)

    channel_start = lax.axis_index("mp") * channels
    taps_full = lax.dynamic_update_slice_in_dim(
        jnp.zeros((3, width), full), taps_grad, channel_start, 1
    )
    small = jnp.concatenate([gain_one[None], gain_two[None], taps_full], axis=0)
    for axis in ("d", "c", "b", "a", "mp"):
        arrived = others(small, axis)
        if len(arrived) == 1:
            small = small + arrived[0]
        else:
            small = lax.psum(small, axis)
    taps_total = lax.dynamic_slice_in_dim(small[2:], channel_start, channels, 1)
    return (
        output.reshape(seq_count, local_len, width),
        tokens_grad.reshape(seq_count, local_len, width),
        small[0],
        in_total,
        taps_total,
        out_total,
        small[1],
        gate_up_total,
        down_total,
    )


def solution(mesh):
    seq, mp = mesh.shape["seq"], mesh.shape["mp"]
    fine = Mesh(mesh.devices.reshape(seq // 8, 2, 2, 2, mp), ("a", "b", "c", "d", "mp"))
    by_seq = ("a", "b", "c", "d")
    return jax.shard_map(
        local,
        mesh=fine,
        in_specs=(
            P(None, by_seq, None),
            P(),
            P(None, None, "mp"),
            P(None, "mp"),
            P("mp", None),
            P(),
            P(None, None, "mp"),
            P("mp", None),
            P(None, by_seq, None),
        ),
        out_specs=(
            P(None, by_seq, None),
            P(None, by_seq, None),
            P(),
            P(by_seq, None, "mp"),
            P(None, "mp"),
            P("mp", by_seq),
            P(),
            P(by_seq, None, "mp"),
            P("mp", by_seq),
        ),
        check_vma=False,
    )
```

```python
import functools

import jax
import jax.numpy as jnp
from jax import lax
from jax.experimental import pallas as pl
from jax.experimental.pallas import tpu as pltpu
from jax.sharding import Mesh, PartitionSpec as P

epsilon = 1e-05
low = jnp.bfloat16
full = jnp.float32
plain = ((1,), (0,))
flipped = ((1,), (1,))
params = pltpu.CompilerParams(vmem_limit_bytes=56 * 2**20)


def swapped(block, axis):
    return lax.ppermute(block, axis, [(0, 1), (1, 0)])


def passed_along(block, axis, distance):
    devices = range(lax.axis_size(axis))
    route = [(i - distance, i) for i in devices if i - distance in devices]
    return lax.ppermute(block, axis, route)


def turned(block, axis, distance):
    count = lax.axis_size(axis)
    return lax.ppermute(block, axis, [(i, (i + distance) % count) for i in range(count)])


def others(block, axis):
    return [turned(block, axis, step) for step in range(1, lax.axis_size(axis))]


def summed(partial, axis):
    partial = partial.astype(low)
    if lax.axis_size(axis) == 2:
        return partial.astype(full) + swapped(partial, axis).astype(full)
    return lax.psum(partial, axis).astype(full)


def share_of(rows):
    count = rows.shape[0] // lax.axis_size("mp")
    return lax.dynamic_slice_in_dim(rows, lax.axis_index("mp") * count, count, 0)


def tied(*values):
    return lax.optimization_barrier(values)


def near(mine):
    return [swapped(mine, axis) for axis in "bcd"]


def beyond(from_near):
    from_b, from_c, from_d = from_near
    return [swapped(from_b, "c"), swapped(from_c, "d"), swapped(from_d, "b")]


def far(from_beyond):
    third = from_beyond[0].shape[0] // 3
    return [
        swapped(piece[step * third : (step + 1) * third], axis)
        for step, (piece, axis) in enumerate(zip(from_beyond, "dbc"))
    ]


def both_cores(pieces):
    return [core for piece in pieces for core in [piece] + others(piece, "mp")]


def joined_kernel(spots, place_ref, *refs):
    pieces, (out_ref, arrivals) = refs[: len(spots)], refs[len(spots) :]
    copies = []
    for index, (piece, (unit, mask, step, part, offset)) in enumerate(zip(pieces, spots)):
        chip, core = place_ref[0] ^ mask, lax.rem(place_ref[1] + step, place_ref[2])
        start = pl.multiple_of(chip * unit + core * part + offset, 16)
        target = out_ref.at[pl.ds(start, piece.shape[0])]
        copies.append(pltpu.make_async_copy(piece, target, arrivals.at[index]))
    for copy in copies:
        copy.start()
    for copy in copies:
        copy.wait()


def joined(own, pieces, cores, place):
    unit, width = own.shape
    rows = unit // cores
    masks = [4, 2, 1, 6, 3, 5, 7, 7, 7]
    offsets = [0] * 7 + [rows // 3, 2 * (rows // 3)]
    spots = [(unit, 0, 0, 0, 0)]
    spots += [
        (unit, mask, (cores - step) % cores, rows, offset)
        for mask, offset in zip(masks, offsets)
        for step in range(cores)
    ]
    core = lax.axis_index("mp").astype(jnp.int32) if cores > 1 else jnp.int32(0)
    facts = jnp.stack([place[0], core, jnp.int32(cores)])
    return pl.pallas_call(
        functools.partial(joined_kernel, spots),
        grid_spec=pltpu.PrefetchScalarGridSpec(
            num_scalar_prefetch=1,
            grid=(1,),
            in_specs=[pl.BlockSpec(memory_space=pl.ANY)] * (1 + len(pieces)),
            out_specs=pl.BlockSpec((8 * unit, width), lambda i, p: (0, 0)),
            scratch_shapes=[pltpu.SemaphoreType.DMA((1 + len(pieces),))],
        ),
        out_shape=jax.ShapeDtypeStruct((8 * unit, width), own.dtype),
        compiler_params=params,
        cost_estimate=pl.CostEstimate(
            flops=0, bytes_accessed=32 * unit * width, transcendentals=0
        ),
    )(facts, own, *pieces)


def row_kernel(*refs):
    pieces, (out_ref, arrivals) = refs[:-2], refs[-2:]
    copies, start = [], 0
    for index, piece in enumerate(pieces):
        target = out_ref.at[pl.ds(start, piece.shape[0])]
        copies.append(pltpu.make_async_copy(piece, target, arrivals.at[index]))
        start += piece.shape[0]
    for copy in copies:
        copy.start()
    for copy in copies:
        copy.wait()


def in_a_row(pieces):
    rows, width = sum(piece.shape[0] for piece in pieces), pieces[0].shape[1]
    return pl.pallas_call(
        row_kernel,
        in_specs=[pl.BlockSpec(memory_space=pl.ANY)] * len(pieces),
        out_specs=pl.BlockSpec(memory_space=pltpu.VMEM),
        out_shape=jax.ShapeDtypeStruct((rows, width), pieces[0].dtype),
        scratch_shapes=[pltpu.SemaphoreType.DMA((len(pieces),))],
        compiler_params=params,
        cost_estimate=pl.CostEstimate(flops=0, bytes_accessed=4 * rows * width, transcendentals=0),
    )(*pieces)


def normalize(values, gain_vec):
    inv_rms = lax.rsqrt(jnp.mean(values * values, axis=-1, keepdims=True) + epsilon)
    return (values * inv_rms * gain_vec, inv_rms)


def norm_back(values, inv_rms, gain_vec, upstream):
    scaled = values * inv_rms
    weighted = upstream * gain_vec
    inner_mean = jnp.mean(weighted * scaled, axis=-1, keepdims=True)
    return inv_rms * (weighted - scaled * inner_mean)


def dot(left, right, dims):
    return lax.dot_general(left, right, (dims, ((), ())), preferred_element_type=full)


def hidden_terms(gate_pre, up_pre, activation_grad):
    sigmoid_gate = jax.nn.sigmoid(gate_pre)
    swish_gate = gate_pre * sigmoid_gate
    gate_grad = activation_grad * up_pre * sigmoid_gate * (1.0 + gate_pre * (1.0 - sigmoid_gate))
    return (
        (swish_gate * up_pre).astype(low),
        gate_grad.astype(low),
        (activation_grad * swish_gate).astype(low),
    )


def both_ways_kernel(carried, x_ref, c_ref, top_ref, bottom_ref, down_ref, *refs):
    starts, (out_ref, grad_ref, out_sum, grad_sum) = refs[:carried], refs[carried:]
    step = pl.program_id(0)
    half = top_ref.shape[1]

    @pl.when(step == 0)
    def _():
        for index, total in enumerate((out_sum, grad_sum)):
            total[...] = starts[index][...] if carried else jnp.zeros_like(total)

    def pre(k):
        return dot(x_ref[:, :half], top_ref[k], plain) + dot(x_ref[:, half:], bottom_ref[k], plain)

    activation, gate_grad, up_grad = hidden_terms(
        pre(0), pre(1), dot(c_ref[...], down_ref[...], flipped)
    )
    out_sum[...] += dot(activation, down_ref[...], plain)
    for columns, ref in ((slice(0, half), top_ref), (slice(half, None), bottom_ref)):
        grad_sum[:, columns] += dot(gate_grad, ref[0], flipped) + dot(up_grad, ref[1], flipped)

    @pl.when(step == pl.num_programs(0) - 1)
    def _():
        out_ref[...] = out_sum[...].astype(out_ref.dtype)
        grad_ref[...] = grad_sum[...].astype(grad_ref.dtype)


def both_ways(normed, upstream, top, bottom, down, first, count, sums, dtype):
    rows, width = normed.shape
    tile = count * down.shape[0] // 8
    while tile > 512:
        tile //= 2
    steps = count * down.shape[0] // 8 // tile
    skip = first * down.shape[0] // 8 // tile
    whole = pl.BlockSpec((rows, width), lambda i: (0, 0))
    pair = pl.BlockSpec((2, width // 2, tile), lambda i: (0, 0, skip + i))
    return pl.pallas_call(
        functools.partial(both_ways_kernel, len(sums)),
        grid=(steps,),
        in_specs=[whole, whole, pair, pair, pl.BlockSpec((tile, width), lambda i: (skip + i, 0))]
        + [whole] * len(sums),
        out_specs=[whole, whole],
        out_shape=[jax.ShapeDtypeStruct((rows, width), dtype)] * 2,
        scratch_shapes=[pltpu.VMEM((rows, width), full)] * 2,
        compiler_params=params,
        cost_estimate=pl.CostEstimate(
            flops=12 * rows * width * tile * steps,
            bytes_accessed=6 * width * tile * steps,
            transcendentals=rows * tile * steps,
        ),
    )(normed, upstream, top, bottom, down, *sums)


def hidden_kernel(counts, units, place_ref, *refs):
    x_pieces, c_pieces = refs[: counts[0]], refs[counts[0] : sum(counts)]
    gate_up_ref, down_ref, hidden_ref, x_out, c_out = refs[sum(counts) : sum(counts) + 5]
    x_all, c_all, arrivals, leaving = refs[sum(counts) + 5 :]
    strips = hidden_ref.shape[0]
    strip = hidden_ref.shape[1] // 3
    block = hidden_ref.shape[2]
    step = pl.program_id(0)

    def coming(unit):
        for row, (pieces, target) in enumerate(((x_pieces, x_all), (c_pieces, c_all))):
            place = unit * block
            for index, (piece, start, rows) in enumerate(units[row][unit]):
                yield pltpu.make_async_copy(
                    pieces[piece].at[pl.ds(start, rows)],
                    target.at[pl.ds(place, rows)],
                    arrivals.at[row, unit, index],
                )
                place += rows

    def going(unit):
        rows = pl.ds(unit * block, block)
        return [
            pltpu.make_async_copy(x_all.at[rows], x_out.at[rows], leaving.at[0, unit]),
            pltpu.make_async_copy(c_all.at[rows], c_out.at[rows], leaving.at[1, unit]),
        ]

    @pl.when(step == 0)
    def _():
        for unit in range(8):
            for copy in coming(unit):
                copy.start()

    for unit in range(8):

        @pl.when(step == unit)
        def _(unit=unit):
            for copy in coming(unit):
                copy.wait()
            for copy in going(unit):
                copy.start()

    rows = pl.ds(step * block, block)
    activation, gate_grad, up_grad = hidden_terms(
        dot(x_all[rows], gate_up_ref[0], plain),
        dot(x_all[rows], gate_up_ref[1], plain),
        dot(c_all[rows], down_ref[...], flipped),
    )
    for n, term in enumerate((gate_grad, up_grad, activation)):
        on_side = term.T
        for k in range(strips):
            hidden_ref[k, n * strip : (n + 1) * strip] = on_side[k * strip : (k + 1) * strip]

    @pl.when(step == 7)
    def _():
        for unit in range(8):
            for copy in going(unit):
                copy.wait()


def hidden_of_all(x_pieces, c_pieces, units, gate_up, down, place, strips):
    width = down.shape[1]
    block = sum(rows for _, _, rows in units[0][0])
    own = down.shape[0] // 8
    anywhere = pl.BlockSpec(memory_space=pl.ANY)
    counts = (len(x_pieces), len(c_pieces))
    most = max(len(unit) for row in units for unit in row)
    joined_shape = jax.ShapeDtypeStruct((8 * block, width), low)
    return pl.pallas_call(
        functools.partial(hidden_kernel, counts, units),
        grid_spec=pltpu.PrefetchScalarGridSpec(
            num_scalar_prefetch=1,
            grid=(8,),
            in_specs=[anywhere] * sum(counts)
            + [
                pl.BlockSpec((2, width, own), lambda i, p: (0, 0, 0)),
                pl.BlockSpec((own, width), lambda i, p: (p[0], 0)),
            ],
            out_specs=[
                pl.BlockSpec((strips, 3 * own // strips, block), lambda i, p: (0, 0, i)),
                anywhere,
                anywhere,
            ],
            scratch_shapes=[
                pltpu.VMEM((8 * block, width), low),
                pltpu.VMEM((8 * block, width), low),
                pltpu.SemaphoreType.DMA((2, 8, most)),
                pltpu.SemaphoreType.DMA((2, 8)),
            ],
        ),
        out_shape=[
            jax.ShapeDtypeStruct((strips, 3 * own // strips, 8 * block), low),
            joined_shape,
            joined_shape,
        ],
        compiler_params=params,
        cost_estimate=pl.CostEstimate(
            flops=48 * block * width * own,
            bytes_accessed=64 * block * width,
            transcendentals=8 * block * own,
        ),
    )(place, *x_pieces, *c_pieces, gate_up, down)


def weight_kernel(part_ref, hidden_ref, x_ref, c_ref, out_ref):
    strip = hidden_ref.shape[1] // 3
    shard = out_ref.shape[3]
    for k in range(hidden_ref.shape[0]):
        pair = dot(hidden_ref[k, : 2 * strip], x_ref[...], plain).astype(low)
        single = dot(hidden_ref[k, 2 * strip :], c_ref[...], plain).astype(low)
        for j in range(out_ref.shape[0]):
            out_ref[j, k, : 2 * strip] = pair[:, j * shard : (j + 1) * shard]
            out_ref[j, k, 2 * strip :] = single[:, j * shard : (j + 1) * shard]


def weight_terms(hidden, normed, upstream, part, parts, first, count):
    three, rows = hidden.shape[1:]
    width = normed.shape[1]
    shard, half = width // (8 * parts), width // parts
    tile = max(256, shard)
    tiles = half // tile
    columns = pl.BlockSpec((rows, tile), lambda i, p: (0, p[0] * tiles + i))
    return pl.pallas_call(
        weight_kernel,
        grid_spec=pltpu.PrefetchScalarGridSpec(
            num_scalar_prefetch=1,
            grid=(tiles,),
            in_specs=[
                pl.BlockSpec((count, three, rows), lambda i, p: (first // count, 0, 0)),
                columns,
                columns,
            ],
            out_specs=pl.BlockSpec((tile // shard, count, three, shard), lambda i, p: (i, 0, 0, 0)),
        ),
        out_shape=jax.ShapeDtypeStruct((8, count, three, shard), low),
        compiler_params=params,
        cost_estimate=pl.CostEstimate(
            flops=2 * rows * half * three * count,
            bytes_accessed=4 * rows * half + 2 * rows * three * count,
            transcendentals=0,
        ),
    )(part, hidden, normed, upstream)


def local(
    tokens,
    norm1_gain,
    in_weight,
    conv_weight,
    out_weight,
    norm2_gain,
    gate_up,
    down_weight,
    cotangent,
):
    seq_count, local_len, width = tokens.shape
    row_total = seq_count * local_len
    channels = in_weight.shape[2]
    hidden = gate_up.shape[2]
    parts = lax.axis_size("a")
    shard = width // (parts * 8)
    blocked = (seq_count, local_len, channels)
    inputs = tokens.reshape(row_total, width).astype(full)
    upstream = cotangent.reshape(row_total, width)
    place = lax.axis_index(("b", "c", "d")).astype(jnp.int32).reshape(1)
    turn = lax.axis_index("a").astype(jnp.int32).reshape(1)
    chunk_count = max(1, hidden // 1024)
    strip = hidden // (8 * chunk_count)
    own = hidden // 8
    half_hidden = hidden // 2

    cores = lax.axis_size("mp")
    half_width = width // 2

    upstream_mine = share_of(upstream)
    upstream_near = near(upstream_mine)
    normed_full_one, inv_rms_one = normalize(inputs, norm1_gain)
    normed_one = normed_full_one.astype(low)
    b_gate = dot(normed_one, in_weight[:, 0], plain).reshape(blocked)
    values = dot(normed_one, in_weight[:, 2], plain).reshape(blocked)
    product = b_gate * values
    carried = passed_along(product[:, local_len - 2 :], ("a", "b", "c", "d"), 1)
    c_gate = dot(normed_one, in_weight[:, 1], plain).reshape(blocked)
    extended = jnp.concatenate([carried, product], axis=1)
    conv_out = (
        conv_weight[0] * extended[:, :local_len]
        + conv_weight[1] * extended[:, 1 : local_len + 1]
        + conv_weight[2] * extended[:, 2:]
    )
    mixed = (c_gate * conv_out).astype(low).reshape(row_total, channels)
    mixer_part = dot(mixed, out_weight, plain).astype(low)
    mixer_part, *upstream_near = tied(mixer_part, *upstream_near)
    upstream_beyond = beyond(upstream_near)
    inner_sum = inputs + summed(mixer_part, "mp")
    normed_full_two, inv_rms_two = normalize(inner_sum, norm2_gain)
    normed_two = normed_full_two.astype(low)

    def apart(block):
        return lax.optimization_barrier(jnp.transpose(block, (1, 0, 2)))

    normed_mine = share_of(normed_two)
    gate_up, normed_mine = tied(gate_up, normed_mine)
    from_c, from_d = swapped(normed_mine, "c"), swapped(normed_mine, "d")
    top = apart(gate_up[:half_width])
    top, gate_up, normed_mine, *upstream_beyond = tied(top, gate_up, normed_mine, *upstream_beyond)
    from_b = swapped(normed_mine, "b")
    upstream_far = far(upstream_beyond)
    bottom = apart(gate_up[half_width:])
    pair_own = apart(lax.dynamic_slice_in_dim(gate_up, place[0] * own, own, 2))
    top, bottom, pair_own, *arrived = tied(
        top, bottom, pair_own, from_b, from_c, from_d, *upstream_far
    )
    normed_near, upstream_far = arrived[:3], arrived[3:]
    normed_beyond = beyond(normed_near)
    upstream_row = in_a_row(upstream_near + upstream_beyond + upstream_far)
    upstream_rows = both_cores([upstream_row])
    sums = both_ways(normed_two, upstream, top, bottom, down_weight, 0, 4, (), full)
    normed_pieces = both_cores(normed_near)
    out_sum, grad_sum, *normed_beyond = tied(*sums, *normed_beyond)
    sums = (out_sum, grad_sum)
    normed_far = far(normed_beyond)
    normed_pieces += both_cores(normed_beyond)
    sums = both_ways(normed_two, upstream, top, bottom, down_weight, 4, 2, sums, full)
    out_sum, grad_sum, *normed_far = tied(*sums, *normed_far)
    sums = (out_sum, grad_sum)
    normed_pieces += both_cores(normed_far)
    output_part, normed_two_part = both_ways(
        normed_two, upstream, top, bottom, down_weight, 6, 2, sums, low
    )
    pair_own, normed_two_part = tied(pair_own, normed_two_part)
    normed_two_grad = summed(normed_two_part, "mp")

    rows = row_total // cores
    third = rows // 3
    x_units = [[(0, 0, row_total)]]
    x_units += [
        [(1 + unit * cores + core, 0, rows) for core in range(cores)] for unit in range(6)
    ]
    x_units += [
        [(1 + (6 + part) * cores + core, 0, third) for core in range(cores) for part in range(3)]
    ]
    c_units = [[(0, 0, row_total)]]
    c_units += [
        [(1 + core, unit * rows, rows) for core in range(cores)] for unit in range(7)
    ]
    hidden_all, normed_all, upstream_all = hidden_of_all(
        [normed_two] + normed_pieces,
        [upstream] + upstream_rows,
        (x_units, c_units),
        pair_own,
        down_weight,
        place,
        chunk_count,
    )
    one_near = near(share_of(tied(normed_one, hidden_all)[0]))

    def terms(step, first, count, hidden_rows):
        part = (turn + step) % parts
        return weight_terms(hidden_rows, normed_all, upstream_all, part, parts, first, count)

    def sent(chunk, hidden_rows):
        return [terms(step, chunk, 1, hidden_rows) for step in range(1, parts)]

    def on_way(blocks):
        return [turned(block, "a", step + 1) for step, block in enumerate(blocks)]

    arrived = []
    for chunk in range(chunk_count):
        blocks = sent(chunk, hidden_all)
        arrived.append(on_way(blocks))
        if chunk + 1 < chunk_count:
            hidden_all, *_ = tied(hidden_all, *blocks)
    normed_two_grad, inner_sum, *rest = tied(normed_two_grad, inner_sum, *one_near, *blocks)
    one_near = rest[:3]
    one_beyond = beyond(one_near)
    mixed_near = near(mixed)
    output = (inner_sum + summed(output_part, "mp")).astype(low)

    inner_grad = upstream.astype(full) + norm_back(
        inner_sum, inv_rms_two, norm2_gain, normed_two_grad
    )
    gain_two = jnp.sum(share_of(normed_two_grad * inner_sum * inv_rms_two), axis=0)
    branch_grad = inner_grad.astype(low)
    branch_columns = lax.all_to_all(
        branch_grad.reshape(row_total, parts, 8, shard)
        .transpose(2, 0, 1, 3)
        .reshape(8, row_total, parts * shard),
        ("b", "c", "d"),
        0,
        0,
        tiled=True,
    )
    branch_grad, *rest = tied(branch_grad, *one_beyond, *mixed_near)
    one_beyond, mixed_near = rest[:3], rest[3:]
    one_far = far(one_beyond)
    mixed_beyond = beyond(mixed_near)
    mixed_grad = dot(branch_grad, out_weight, flipped).reshape(blocked)
    conv_grad_in = mixed_grad * c_gate
    later = passed_along(conv_grad_in[:, :2], ("a", "b", "c", "d"), -1)
    c_gate_grad = mixed_grad * conv_out
    grad_extended = jnp.concatenate([conv_grad_in, later], axis=1)
    product_grad = (
        conv_weight[2] * grad_extended[:, :local_len]
        + conv_weight[1] * grad_extended[:, 1 : local_len + 1]
        + conv_weight[0] * grad_extended[:, 2:]
    )
    taps_grad = jnp.stack(
        [
            jnp.sum(conv_grad_in * extended[:, tap : tap + local_len], axis=(0, 1))
            for tap in range(3)
        ]
    )
    projected_grad = [
        grad.astype(low).reshape(row_total, channels)
        for grad in (product_grad * values, c_gate_grad, product_grad * b_gate)
    ]
    slices = jnp.stack(
        [grad.reshape(row_total, 8, channels // 8) for grad in projected_grad], axis=2
    ).transpose(1, 0, 2, 3)
    slices = lax.all_to_all(
        slices.reshape(8, row_total, 3 * channels // 8), ("b", "c", "d"), 0, 0, tiled=True
    )
    projected_grad[0], *mixed_beyond = tied(projected_grad[0], *mixed_beyond)
    mixed_far = far(mixed_beyond)
    normed_one_grad = summed(
        sum(dot(projected_grad[k], in_weight[:, k], flipped) for k in range(3)), "mp"
    )
    tokens_grad = (inner_grad + norm_back(inputs, inv_rms_one, norm1_gain, normed_one_grad)).astype(
        low
    )
    gain_one = jnp.sum(share_of(normed_one_grad * inputs * inv_rms_one), axis=0)

    pair_count = min(2, chunk_count)
    hidden_all, normed_one_grad = tied(hidden_all, normed_one_grad)
    kept = [
        terms(0, first, pair_count, hidden_all) for first in range(0, chunk_count, pair_count)
    ]

    def settled(kept_block, arrived_blocks):
        total = kept_block.astype(full)
        for block in arrived_blocks:
            total = total + block[:, 0].astype(full)
        return lax.all_to_all(total.astype(low), ("b", "c", "d"), 0, 0, tiled=True)

    placed = [
        settled(kept[chunk // pair_count][:, chunk % pair_count], arrived[chunk])
        for chunk in range(chunk_count)
    ]
    placed = jnp.stack(placed, axis=1).astype(full).reshape(8, chunk_count, 3, strip, shard)
    gate_up_total = placed[:, :, :2].transpose(4, 2, 0, 1, 3).reshape(shard, 2, hidden)
    down_total = placed[:, :, 2].reshape(hidden, shard)

    one_all = joined(normed_one, both_cores(one_near + one_beyond + one_far), cores, place)
    mixed_all = joined(mixed, mixed_near + mixed_beyond + mixed_far, 1, place)
    slices = slices.reshape(8 * row_total, -1).T[None]

    def in_terms(step):
        part = (turn + step) % parts
        return weight_terms(slices, one_all, one_all, part, parts, 0, 1)

    in_arrived = on_way([in_terms(step) for step in range(1, parts)])
    in_placed = settled(in_terms(0)[:, 0], in_arrived).astype(full)
    in_total = (
        in_placed.reshape(8, 3, channels // 8, shard)
        .transpose(3, 1, 0, 2)
        .reshape(shard, 3, channels)
    )
    branch_columns = branch_columns.reshape(8 * row_total, parts, shard)

    def out_terms(step):
        columns = lax.dynamic_index_in_dim(branch_columns, (turn[0] + step) % parts, 1, False)
        return dot(mixed_all, columns, ((0,), (0,))).astype(low)

    out_total = out_terms(0).astype(full)
    for block in on_way([out_terms(step) for step in range(1, parts)]):
        out_total = out_total + block.astype(full)

    channel_start = lax.axis_index("mp") * channels
    taps_full = lax.dynamic_update_slice_in_dim(
        jnp.zeros((3, width), full), taps_grad, channel_start, 1
    )
    small = jnp.concatenate([gain_one[None], gain_two[None], taps_full], axis=0)
    for axis in ("d", "c", "b", "a", "mp"):
        arrived = others(small, axis)
        if len(arrived) == 1:
            small = small + arrived[0]
        else:
            small = lax.psum(small, axis)
    taps_total = lax.dynamic_slice_in_dim(small[2:], channel_start, channels, 1)
    return (
        output.reshape(seq_count, local_len, width),
        tokens_grad.reshape(seq_count, local_len, width),
        small[0],
        in_total,
        taps_total,
        out_total,
        small[1],
        gate_up_total,
        down_total,
    )


def solution(mesh):
    seq, mp = mesh.shape["seq"], mesh.shape["mp"]
    fine = Mesh(mesh.devices.reshape(seq // 8, 2, 2, 2, mp), ("a", "b", "c", "d", "mp"))
    by_seq = ("a", "b", "c", "d")
    return jax.shard_map(
        local,
        mesh=fine,
        in_specs=(
            P(None, by_seq, None),
            P(),
            P(None, None, "mp"),
            P(None, "mp"),
            P("mp", None),
            P(),
            P(None, None, "mp"),
            P("mp", None),
            P(None, by_seq, None),
        ),
        out_specs=(
            P(None, by_seq, None),
            P(None, by_seq, None),
            P(),
            P(by_seq, None, "mp"),
            P(None, "mp"),
            P("mp", by_seq),
            P(),
            P(by_seq, None, "mp"),
            P("mp", by_seq),
        ),
        check_vma=False,
    )
```

```python
import functools

import jax
import jax.numpy as jnp
from jax import lax
from jax.experimental import pallas as pl
from jax.experimental.pallas import tpu as pltpu
from jax.sharding import Mesh, PartitionSpec as P

epsilon = 1e-05
low = jnp.bfloat16
full = jnp.float32
plain = ((1,), (0,))
flipped = ((1,), (1,))
params = pltpu.CompilerParams(vmem_limit_bytes=56 * 2**20)


brief = pl.CostEstimate(flops=1000, bytes_accessed=1000, transcendentals=0)


def swapped(block, axis):
    return lax.ppermute(block, axis, [(0, 1), (1, 0)])


def passed_along(block, axis, distance):
    devices = range(lax.axis_size(axis))
    route = [(i - distance, i) for i in devices if i - distance in devices]
    return lax.ppermute(block, axis, route)


def turned(block, axis, distance):
    count = lax.axis_size(axis)
    return lax.ppermute(block, axis, [(i, (i + distance) % count) for i in range(count)])


def others(block, axis):
    return [turned(block, axis, step) for step in range(1, lax.axis_size(axis))]


def both_parts(partial):
    if lax.axis_size("mp") == 2:
        return [partial, swapped(partial, "mp")]
    return [lax.psum(partial, "mp")]


def summed(partial):
    return sum(part.astype(full) for part in both_parts(partial.astype(low)))


def share_of(rows):
    count = rows.shape[0] // lax.axis_size("mp")
    return lax.dynamic_slice_in_dim(rows, lax.axis_index("mp") * count, count, 0)


def tied(*values):
    return lax.optimization_barrier(values)


def near(mine):
    return [swapped(mine, axis) for axis in "bcd"]


def beyond(from_near, axes="cdb"):
    return [swapped(piece, axis) for piece, axis in zip(from_near, axes)]


def opposite(mine):
    return lax.ppermute(mine, ("b", "c", "d"), [(i, 7 - i) for i in range(8)])


def row_kernel(makings, *refs):
    for place, making in enumerate(makings):
        out_ref, row = refs[len(refs) - len(makings) + place], 0
        for part in making:
            index, start, rows = part if isinstance(part, tuple) else (part, 0, None)
            rows = refs[index].shape[0] if rows is None else rows
            out_ref[row : row + rows] = refs[index][start : start + rows]
            row += rows


def in_rows(arrays, makings):
    width = arrays[0].shape[1]

    def rows(making):
        return sum(
            part[2] if isinstance(part, tuple) else arrays[part].shape[0] for part in making
        )

    whole = pl.BlockSpec(memory_space=pltpu.VMEM)
    return pl.pallas_call(
        functools.partial(row_kernel, makings),
        in_specs=[whole] * len(arrays),
        out_specs=[whole] * len(makings),
        out_shape=[jax.ShapeDtypeStruct((rows(making), width), low) for making in makings],
        compiler_params=params,
        cost_estimate=brief,
    )(*arrays)


def shared_out(blocks, axes):
    return lax.all_to_all(blocks, axes, 0, 0, tiled=True)


def shown_to_all(mine, axes):
    return shared_out(jnp.broadcast_to(mine, (lax.axis_size(axes),) + mine.shape), axes)


def normalize(values, gain_vec):
    inv_rms = lax.rsqrt(jnp.mean(values * values, axis=-1, keepdims=True) + epsilon)
    return (values * inv_rms * gain_vec, inv_rms)


def norm_back(values, inv_rms, gain_vec, upstream):
    scaled = values * inv_rms
    weighted = upstream * gain_vec
    inner_mean = jnp.mean(weighted * scaled, axis=-1, keepdims=True)
    return inv_rms * (weighted - scaled * inner_mean)


def dot(left, right, dims):
    return lax.dot_general(left, right, (dims, ((), ())), preferred_element_type=full)


def hidden_terms(gate_pre, up_pre, activation_grad):
    sigmoid_gate = jax.nn.sigmoid(gate_pre)
    swish_gate = gate_pre * sigmoid_gate
    gate_grad = activation_grad * up_pre * sigmoid_gate * (1.0 + gate_pre * (1.0 - sigmoid_gate))
    return (
        (swish_gate * up_pre).astype(low),
        gate_grad.astype(low),
        (activation_grad * swish_gate).astype(low),
    )


def both_ways_kernel(x_ref, c_ref, pair_ref, down_ref, act_ref, grad_ref, grad_sum):
    step = pl.program_id(0)

    @pl.when(step == 0)
    def _():
        grad_sum[...] = jnp.zeros_like(grad_sum)

    activation, gate_grad, up_grad = hidden_terms(
        dot(x_ref[...], pair_ref[0], plain),
        dot(x_ref[...], pair_ref[1], plain),
        dot(c_ref[...], down_ref[...], flipped),
    )
    act_ref[...] = activation
    grad_sum[...] += dot(gate_grad, pair_ref[0], flipped) + dot(up_grad, pair_ref[1], flipped)

    @pl.when(step == pl.num_programs(0) - 1)
    def _():
        grad_ref[...] = grad_sum[...].astype(low)


def both_ways(normed, upstream, pair, down):
    rows, width = normed.shape
    hidden = down.shape[0]
    tile = min(512, hidden)
    whole = pl.BlockSpec((rows, width), lambda i: (0, 0))
    return pl.pallas_call(
        both_ways_kernel,
        grid=(hidden // tile,),
        in_specs=[
            whole,
            whole,
            pl.BlockSpec((2, width, tile), lambda i: (0, 0, i)),
            pl.BlockSpec((tile, width), lambda i: (i, 0)),
        ],
        out_specs=[pl.BlockSpec((rows, tile), lambda i: (0, i)), whole],
        out_shape=[
            jax.ShapeDtypeStruct((rows, hidden), low),
            jax.ShapeDtypeStruct((rows, width), low),
        ],
        scratch_shapes=[pltpu.VMEM((rows, width), full)],
        compiler_params=params,
        cost_estimate=brief,
    )(normed, upstream, pair, down)


def write_hidden(x, c, weights, hidden_ref):
    strips, strip = hidden_ref.shape[1], hidden_ref.shape[2] // 3
    for core, (gate_ref, up_ref, down_ref) in enumerate(weights):
        activation, gate_grad, up_grad = hidden_terms(
            dot(x, gate_ref[0, 0], plain),
            dot(x, up_ref[0, 0], plain),
            dot(c, down_ref[0], flipped),
        )
        for n, term in enumerate((gate_grad, up_grad, activation)):
            on_side = term.T
            for k in range(strips):
                hidden_ref[core, k, n * strip : (n + 1) * strip] = on_side[
                    k * strip : (k + 1) * strip
                ]


def threes(refs):
    return [refs[start : start + 3] for start in range(0, len(refs), 3)]


def first_hidden_kernel(counts, spots, unit, *refs):
    pieces = refs[: counts[0]], refs[counts[0] : sum(counts)]
    *weights, hidden_ref, x_out, c_out, x_all, c_all, arrivals, leaving = refs[sum(counts) :]
    both = (x_all, x_out), (c_all, c_out)
    count = len(spots[0])
    block = hidden_ref.shape[3]
    together = block // unit
    step = pl.program_id(0)

    def coming(index):
        rows = pl.ds(index * unit, unit)
        copies = []
        for n in range(2):
            piece, start = spots[n][index]
            source = pieces[n][piece].at[pl.ds(start, unit)]
            copies.append(
                pltpu.make_async_copy(source, both[n][0].at[rows], arrivals.at[n, index])
            )
        return copies

    def going(index):
        rows = pl.ds(index * block, block)
        return [
            pltpu.make_async_copy(here.at[rows], there.at[rows], leaving.at[n, index])
            for n, (here, there) in enumerate(both)
        ]

    @pl.when(step == 0)
    def _():
        for index in range(count):
            for copy in coming(index):
                copy.start()

    for index in range(count // together):

        @pl.when(step == index)
        def _(index=index):
            for piece in range(index * together, (index + 1) * together):
                for copy in coming(piece):
                    copy.wait()
            for copy in going(index):
                copy.start()

    rows = pl.ds(step * block, block)
    write_hidden(x_all[rows], c_all[rows], threes(weights), hidden_ref)

    @pl.when(step == pl.num_programs(0) - 1)
    def _():
        for index in range(count // together):
            for copy in going(index):
                copy.wait()


def next_hidden_kernel(x_ref, c_ref, *refs):
    write_hidden(x_ref[...], c_ref[...], threes(refs[:-1]), refs[-1])


def weight_operands(pairs, downs, index):
    _, _, width, part = pairs[0].shape
    specs, arrays = [], []
    for pair, down in zip(pairs, downs):
        specs += [
            pl.BlockSpec((1, 1, width, part), lambda i, k=k: (index, k, 0, 0)) for k in range(2)
        ]
        specs.append(pl.BlockSpec((1, part, width), lambda i: (index, 0, 0)))
        arrays += [pair, pair, down]
    return specs, arrays


def first_hidden(x_pieces, c_pieces, unit, pairs, downs, strips):
    width = downs[0].shape[2]
    arrays, spots = [], []
    for row in (x_pieces, c_pieces):
        known = []
        for array, _ in row:
            if not any(array is other for other in known):
                known.append(array)
        arrays.append(known)
        spots.append(
            [
                (next(n for n, other in enumerate(known) if other is array), start)
                for array, start in row
            ]
        )
    counts = tuple(len(known) for known in arrays)
    count, own, cores = len(x_pieces), downs[0].shape[1], len(downs)
    block, rows = max(1, 384 // unit) * unit, count * unit
    anywhere = pl.BlockSpec(memory_space=pl.ANY)
    row_shape = jax.ShapeDtypeStruct((rows, width), low)
    three = 3 * own // strips
    specs, weights = weight_operands(pairs, downs, 0)
    return pl.pallas_call(
        functools.partial(first_hidden_kernel, counts, spots, unit),
        grid=(rows // block,),
        in_specs=[anywhere] * sum(counts) + specs,
        out_specs=[
            pl.BlockSpec((cores, strips, three, block), lambda i: (0, 0, 0, i)),
            anywhere,
            anywhere,
        ],
        scratch_shapes=[
            pltpu.VMEM((rows, width), low),
            pltpu.VMEM((rows, width), low),
            pltpu.SemaphoreType.DMA((2, count)),
            pltpu.SemaphoreType.DMA((2, rows // block)),
        ],
        out_shape=[
            jax.ShapeDtypeStruct((cores, strips, three, rows), low),
            row_shape,
            row_shape,
        ],
        compiler_params=params,
        cost_estimate=brief,
    )(*arrays[0], *arrays[1], *weights)


def next_hidden(x_all, c_all, pairs, downs, strips, index):
    rows, width = x_all.shape
    own, cores = downs[0].shape[1], len(downs)
    block = min(384, rows)
    three = 3 * own // strips
    tokens = pl.BlockSpec((block, width), lambda i: (i, 0))
    specs, weights = weight_operands(pairs, downs, index)
    return pl.pallas_call(
        next_hidden_kernel,
        grid=(rows // block,),
        in_specs=[tokens, tokens] + specs,
        out_specs=pl.BlockSpec((cores, strips, three, block), lambda i: (0, 0, 0, i)),
        out_shape=jax.ShapeDtypeStruct((cores, strips, three, rows), low),
        compiler_params=params,
        cost_estimate=brief,
    )(x_all, c_all, *weights)


def weight_kernel(hidden_ref, x_ref, c_ref, *refs):
    arrived, out_ref = refs[:-1], refs[-1]
    strip = hidden_ref.shape[2] // 3
    shard = out_ref.shape[3]
    for k in range(out_ref.shape[1]):
        pair = dot(hidden_ref[0, k, : 2 * strip], x_ref[...], plain)
        single = dot(hidden_ref[0, k, 2 * strip :], c_ref[...], plain)
        for j in range(out_ref.shape[0]):
            columns = slice(j * shard, (j + 1) * shard)
            for rows, term in ((slice(0, 2 * strip), pair), (slice(2 * strip, None), single)):
                total = term[:, columns]
                for ref in arrived:
                    total = total + ref[j, k, rows].astype(full)
                out_ref[j, k, rows] = total.astype(low)


def weight_terms(hidden, normed, upstream, shard, core, arrived=()):
    count, three, rows = hidden.shape[1:]
    width = normed.shape[1]
    tile = max(256, shard)
    columns = pl.BlockSpec((rows, tile), lambda i: (0, i))
    out_block = pl.BlockSpec((tile // shard, count, three, shard), lambda i: (i, 0, 0, 0))
    return pl.pallas_call(
        weight_kernel,
        grid=(width // tile,),
        in_specs=[
            pl.BlockSpec((1, count, three, rows), lambda i: (core, 0, 0, 0)),
            columns,
            columns,
        ]
        + [out_block] * len(arrived),
        out_specs=out_block,
        out_shape=jax.ShapeDtypeStruct((width // shard, count, three, shard), low),
        compiler_params=params,
        cost_estimate=brief,
    )(hidden, normed, upstream, *arrived)


def mixing_kernel(facts, x_ref, weight_ref, taps_ref, mixed_ref, kept_ref, line):
    seqs, length, gap = facts
    own, side = seqs * length, 2 * seqs
    x = x_ref[...]
    b_gate, c_gate, values = (dot(x, weight_ref[k], plain) for k in range(3))
    product = b_gate * values
    conv_out = [None] * (2 * seqs)
    for seq in range(seqs):
        before, after = own + side + 2 * seq, own + 2 * seq
        line[seq, 0:2] = product[before : before + 2]
        line[seq, 2 : length + 2] = product[seq * length : (seq + 1) * length]
        line[seq, length + 2 : length + 4] = product[after : after + 2]
        conv = sum(taps_ref[tap] * line[seq, tap : tap + length + 2] for tap in range(3))
        kept_ref[3, seq * length : (seq + 1) * length] = conv[:length]
        kept_ref[3, after : after + 2] = conv[length:]
    kept_ref[3, own + side :] = jnp.zeros_like(product[own + side :])
    kept_ref[0], kept_ref[1], kept_ref[2] = b_gate, c_gate, values
    mixed_ref[...] = (c_gate * kept_ref[3]).astype(low)


def mixing(normed, weight, taps, seqs, length):
    rows, width = normed.shape
    channels = weight.shape[2]
    tile = channels // 4
    return pl.pallas_call(
        functools.partial(mixing_kernel, (seqs, length, 0)),
        grid=(4,),
        in_specs=[
            pl.BlockSpec((rows, width), lambda i: (0, 0)),
            pl.BlockSpec((3, width, tile), lambda i: (0, 0, i)),
            pl.BlockSpec((3, tile), lambda i: (0, i)),
        ],
        out_specs=[
            pl.BlockSpec((rows, tile), lambda i: (0, i)),
            pl.BlockSpec((4, rows, tile), lambda i: (0, 0, i)),
        ],
        out_shape=[
            jax.ShapeDtypeStruct((rows, channels), low),
            jax.ShapeDtypeStruct((4, rows, channels), full),
        ],
        scratch_shapes=[pltpu.VMEM((seqs, length + 8, tile), full)],
        compiler_params=params,
        cost_estimate=brief,
    )(normed, weight, taps)


def unmixing_kernel(
    facts, spot_ref, grad_ref, weight_ref, kept_ref, taps_ref, sent_ref, sums_ref, line, past
):
    seqs, length, deep, shard = facts
    own, side = seqs * length, 2 * seqs
    tile = weight_ref.shape[0]
    mixed_grad = dot(grad_ref[...], weight_ref[...], flipped)
    conv_grad = mixed_grad * kept_ref[1]
    for seq in range(seqs):
        rows = slice(seq * length, (seq + 1) * length)
        before, after = own + side + 2 * seq, own + 2 * seq
        line[seq, 0:length] = conv_grad[rows]
        line[seq, length : length + 2] = conv_grad[after : after + 2]
        product_grad = sum(taps_ref[2 - tap] * line[seq, tap : tap + length] for tap in range(3))
        b_gate, values = kept_ref[0, rows], kept_ref[2, rows]
        sent_ref[0, rows, :tile] = (product_grad * values).astype(low)
        sent_ref[0, rows, tile : 2 * tile] = (mixed_grad[rows] * kept_ref[3, rows]).astype(low)
        sent_ref[0, rows, 2 * tile : 3 * tile] = (product_grad * b_gate).astype(low)
        past[seq, 0:2] = kept_ref[0, before : before + 2] * kept_ref[2, before : before + 2]
        past[seq, 2 : length + 2] = b_gate * values
    for tap in range(3):
        sums_ref[tap : tap + 1] = sum(
            jnp.sum(line[seq, 0:length] * past[seq, tap : tap + length], axis=0, keepdims=True)
            for seq in range(seqs)
        )
    for part in range(4):

        @pl.when(pl.program_id(0) == part)
        def _(part=part):
            for far in range(deep):
                start = (far * 4 + part) * shard
                sent_ref[0, :, 3 * tile + far * shard : 3 * tile + (far + 1) * shard] = grad_ref[
                    0:own, start : start + shard
                ]


def unmixing(grad, weight, kept, taps, seqs, length, shard, spot):
    rows, width = grad.shape
    channels = weight.shape[0]
    tile, deep = channels // 4, width // (4 * shard)
    wide = 3 * tile + deep * shard
    return pl.pallas_call(
        functools.partial(unmixing_kernel, (seqs, length, deep, shard)),
        grid_spec=pltpu.PrefetchScalarGridSpec(
            num_scalar_prefetch=1,
            grid=(4,),
            in_specs=[
                pl.BlockSpec((rows, width), lambda i, p: (0, 0)),
                pl.BlockSpec((tile, width), lambda i, p: (i, 0)),
                pl.BlockSpec((4, rows, tile), lambda i, p: (0, 0, i)),
                pl.BlockSpec((3, tile), lambda i, p: (0, i)),
            ],
            out_specs=[
                pl.BlockSpec((1, seqs * length, wide), lambda i, p: (i ^ p[0], 0, 0)),
                pl.BlockSpec((3, tile), lambda i, p: (0, i)),
            ],
            scratch_shapes=[pltpu.VMEM((seqs, length + 8, tile), full)] * 2,
        ),
        out_shape=[
            jax.ShapeDtypeStruct((4, seqs * length, wide), low),
            jax.ShapeDtypeStruct((3, channels), full),
        ],
        compiler_params=params,
        cost_estimate=brief,
    )(spot, grad, weight, kept, taps)


def unprojected_kernel(spot_ref, sent_ref, weight_ref, out_ref, total):
    step = pl.program_id(0)
    tile = weight_ref.shape[2]
    term = sum(
        dot(sent_ref[0, :, k * tile : (k + 1) * tile], weight_ref[k], flipped) for k in range(3)
    )

    @pl.when(step == 0)
    def _():
        total[...] = term

    @pl.when(step > 0)
    def _():
        total[...] += term

    @pl.when(step == pl.num_programs(0) - 1)
    def _():
        out_ref[...] = total[...].astype(low)


def unprojected(sent, weight, spot):
    rows = sent.shape[1]
    width, channels = weight.shape[1:]
    tile = channels // 4
    return pl.pallas_call(
        unprojected_kernel,
        grid_spec=pltpu.PrefetchScalarGridSpec(
            num_scalar_prefetch=1,
            grid=(4,),
            in_specs=[
                pl.BlockSpec((1, rows, 3 * tile), lambda i, p: (i, 0, 0)),
                pl.BlockSpec((3, width, tile), lambda i, p: (0, 0, i ^ p[0])),
            ],
            out_specs=pl.BlockSpec((rows, width), lambda i, p: (0, 0)),
            scratch_shapes=[pltpu.VMEM((rows, width), full)],
        ),
        out_shape=jax.ShapeDtypeStruct((rows, width), low),
        compiler_params=params,
        cost_estimate=brief,
    )(spot, sent, weight)


def mixer_kernel(cores, facts_ref, *refs):
    sent, (mixed_ref, *refs) = refs[:4], refs[4:]
    rights, out_ref = refs[:cores], refs[cores]
    gathered, turned_rows, turned_mixed, columns = refs[cores + 1 :]
    chips, rows, channels = mixed_ref.shape
    count = turned_rows.shape[1]
    share = rows // cores
    shard = out_ref.shape[2]
    step = pl.program_id(0)

    @pl.when(step == 0)
    def _():
        for index in range(cores):
            core = lax.rem(facts_ref[1] + cores - index, cores)
            start = pl.multiple_of(core * share, 16)
            for mask, ref in enumerate(sent):
                place = pl.multiple_of((facts_ref[0] ^ mask) * share, 16)
                gathered[pl.ds(place, share)] = ref[0, pl.ds(start, share), :count]
            turned_rows[index] = gathered[...].T
        turned_mixed[...] = mixed_ref[...].reshape(chips * rows, channels).T
        for mask, ref in enumerate(sent):
            place = pl.multiple_of((facts_ref[0] ^ mask) * rows, 16)
            for far in range(columns.shape[0]):
                start = count + far * shard
                columns[far, pl.ds(place, rows)] = ref[0, :, start : start + shard]

    total = sum(
        dot(turned_rows[index], rights[index][...].reshape(chips * share, chips * shard), plain)
        for index in range(cores)
    )
    for j in range(chips):
        out_ref[0, j * count : (j + 1) * count] = total[:, j * shard : (j + 1) * shard].astype(low)
    out_ref[0, chips * count :] = dot(turned_mixed[...], columns[step], plain).astype(low)


def mixer_terms(sent, count, rights, shown, channels, shard, spot):
    rows, wide = sent[0].shape[1:]
    cores = len(rights)
    chips, _, share, half = rights[0].shape
    tile = chips * shard
    tiles = half // tile
    deep = 2 * tiles
    facts = jnp.concatenate([spot, lax.axis_index("mp").astype(jnp.int32).reshape(1)])
    right = pl.BlockSpec((chips, 1, share, tile), lambda i, p: (0, i // tiles, 0, i % tiles))
    tall = chips * count + channels
    return pl.pallas_call(
        functools.partial(mixer_kernel, cores),
        grid_spec=pltpu.PrefetchScalarGridSpec(
            num_scalar_prefetch=1,
            grid=(deep,),
            in_specs=[pl.BlockSpec((1, rows, wide), lambda i, p: (0, 0, 0))] * chips
            + [pl.BlockSpec((chips, rows, channels), lambda i, p: (0, 0, 0))]
            + [right] * cores,
            out_specs=pl.BlockSpec((1, tall, shard), lambda i, p: (i, 0, 0)),
            scratch_shapes=[
                pltpu.VMEM((chips * share, count), low),
                pltpu.VMEM((cores, count, chips * share), low),
                pltpu.VMEM((channels, chips * rows), low),
                pltpu.VMEM((deep, chips * rows, shard), low),
            ],
        ),
        out_shape=jax.ShapeDtypeStruct((deep, tall, shard), low),
        compiler_params=params,
        cost_estimate=brief,
    )(facts, *sent, shown, *rights)


def placing_kernel(parts, *refs):
    placed_ref, pair_ref, down_ref = refs[0], refs[-2], refs[-1]
    chips, count, three, _ = placed_ref.shape
    chips //= parts
    strip = three // 3
    for chip in range(chips):
        for k in range(count):
            block = sum(placed_ref[part * chips + chip, k].astype(full) for part in range(parts))
            start = (chip * count + k) * strip
            pair_ref[:, 0, start : start + strip] = block[:strip].T
            pair_ref[:, 1, start : start + strip] = block[strip : 2 * strip].T
            down_ref[start : start + strip] = block[2 * strip :]


def put_in_place(placed, parts, index, groups, before):
    chips, count, three, shard = placed.shape
    columns = chips // parts * count * three // 3
    return pl.pallas_call(
        functools.partial(placing_kernel, parts),
        grid=(1,),
        in_specs=[pl.BlockSpec(placed.shape, lambda i: (0, 0, 0, 0))]
        + [pl.BlockSpec(memory_space=pl.ANY)] * len(before),
        out_specs=[
            pl.BlockSpec((shard, 2, columns), lambda i: (0, 0, index)),
            pl.BlockSpec((columns, shard), lambda i: (index, 0)),
        ],
        out_shape=[
            jax.ShapeDtypeStruct((shard, 2, groups * columns), full),
            jax.ShapeDtypeStruct((groups * columns, shard), full),
        ],
        input_output_aliases={1 + n: n for n in range(len(before))},
        compiler_params=params,
        cost_estimate=brief,
    )(placed, *before)


def product_kernel(left_ref, right_ref, out_ref, total):
    step = pl.program_id(0)
    term = dot(left_ref[...], right_ref[...], plain)

    @pl.when(step == 0)
    def _():
        total[...] = term

    @pl.when(step > 0)
    def _():
        total[...] += term

    @pl.when(step == pl.num_programs(0) - 1)
    def _():
        out_ref[...] = total[...].astype(low)


def product_of(left, right):
    rows, depth = left.shape
    width = right.shape[1]
    tile = min(512, depth)
    return pl.pallas_call(
        product_kernel,
        grid=(depth // tile,),
        in_specs=[
            pl.BlockSpec((rows, tile), lambda i: (0, i)),
            pl.BlockSpec((tile, width), lambda i: (i, 0)),
        ],
        out_specs=pl.BlockSpec((rows, width), lambda i: (0, 0)),
        out_shape=jax.ShapeDtypeStruct((rows, width), low),
        scratch_shapes=[pltpu.VMEM((rows, width), full)],
        compiler_params=params,
        cost_estimate=brief,
    )(left, right)


def tokens_grad_kernel(core_ref, values_ref, inv_ref, gain_ref, inner_ref, *refs):
    parts, (out_ref, sums_ref) = refs[:-2], refs[-2:]
    upstream = sum(ref[...].astype(full) for ref in parts)
    scaled = values_ref[...] * inv_ref[...]
    weighted = upstream * gain_ref[...]
    inner_mean = jnp.mean(weighted * scaled, axis=-1, keepdims=True)
    out_ref[...] = (inner_ref[...] + inv_ref[...] * (weighted - scaled * inner_mean)).astype(low)

    @pl.when(pl.program_id(0) == core_ref[0])
    def _():
        sums_ref[...] = jnp.sum(upstream * scaled, axis=0, keepdims=True)


def tokens_grad_of(values, inv_rms, gain_vec, inner_grad, parts, rows, cores):
    width = values.shape[1]
    share = rows // cores
    core = lax.axis_index("mp").astype(jnp.int32).reshape(1)
    block = pl.BlockSpec((share, width), lambda i, p: (i, 0))
    line = pl.BlockSpec((1, width), lambda i, p: (0, 0))
    return pl.pallas_call(
        tokens_grad_kernel,
        grid_spec=pltpu.PrefetchScalarGridSpec(
            num_scalar_prefetch=1,
            grid=(cores,),
            in_specs=[block, pl.BlockSpec((share, 1), lambda i, p: (i, 0)), line, block]
            + [block] * len(parts),
            out_specs=[block, line],
        ),
        out_shape=[
            jax.ShapeDtypeStruct((rows, width), low),
            jax.ShapeDtypeStruct((1, width), full),
        ],
        compiler_params=params,
        cost_estimate=brief,
    )(core, values, inv_rms, gain_vec.reshape(1, -1), inner_grad, *parts)


def local(
    tokens,
    norm1_gain,
    in_weight,
    conv_weight,
    out_weight,
    norm2_gain,
    gate_up,
    down_weight,
    cotangent,
):
    seq_count, local_len, width = tokens.shape
    row_total = seq_count * local_len
    channels = in_weight.shape[2]
    hidden = gate_up.shape[2]
    parts = lax.axis_size("a")
    cores = lax.axis_size("mp")
    shard = width // (parts * 8)
    deep = width // (4 * shard)
    quarter = channels // 4
    cube, plane, column = ("b", "c", "d"), ("c", "d"), ("a", "b")
    place = lax.axis_index(cube).astype(jnp.int32).reshape(1)
    own = hidden // 8
    chunk_count = max(1, hidden // 1024)
    in_parts = jnp.transpose(in_weight, (1, 0, 2))

    after = passed_along(
        jnp.stack([tokens[:, :2], cotangent[:, :2]]), column + plane, -1
    ).reshape(2, -1, width)
    before = passed_along(tokens[:, local_len - 2 :], column + plane, 1).reshape(-1, width)
    side = before.shape[0]
    padding = jnp.zeros((2 * side + (-2 * side) % 16, width), low)
    before, upstream_mine = tied(before, share_of(cotangent.reshape(row_total, width)))
    inputs = jnp.concatenate(
        [tokens.reshape(row_total, width), after[0], before, padding[2 * side :]]
    ).astype(full)
    upstream = jnp.concatenate([cotangent.reshape(row_total, width), after[1], padding[side:]])
    normed_full_one, inv_rms_one = normalize(inputs, norm1_gain)
    normed_one = normed_full_one.astype(low)
    upstream_opposite = opposite(upstream_mine)
    mixed, mixer_state = mixing(normed_one, in_parts, conv_weight, seq_count, local_len)
    mixed, upstream_opposite = tied(mixed, upstream_opposite)
    inner_sum = inputs + summed(dot(mixed, out_weight, plain))
    normed_full_two, inv_rms_two = normalize(inner_sum, norm2_gain)
    normed_two = normed_full_two.astype(low)

    group = min(2, chunk_count)
    groups = chunk_count // group
    half_width = width // 2
    part = own // groups
    unit = row_total // cores
    normed_mine = share_of(normed_two[:row_total])
    together = in_rows([normed_mine, upstream_mine], [(0, 1)])[0]
    from_near = near(together)
    firsts = [(index * 8 + place[0]) * part for index in range(groups)]
    down_own = jnp.stack(
        [lax.dynamic_slice_in_dim(down_weight, first, part, 0) for first in firsts]
    )
    downs = [down_own] + others(down_own, "mp")
    gate_up, together = tied(gate_up, together)
    pair_weight = lax.optimization_barrier(jnp.transpose(gate_up, (1, 0, 2)))
    pair_weight, normed_mine, *arrived = tied(
        pair_weight, normed_mine, *from_near, *downs[1:]
    )
    from_near, downs[1:] = arrived[:3], arrived[3:]
    from_beyond = beyond(from_near, "cdb")
    normed_opposite = opposite(normed_mine)
    pair_own = jnp.stack(
        [lax.dynamic_slice_in_dim(pair_weight, first, part, 2) for first in firsts]
    )
    pairs = [pair_own] + others(pair_own, "mp")
    pair_weight, pairs[0] = tied(pair_weight, pairs[0])
    activation, normed_two_part = both_ways(normed_two, upstream, pair_weight, down_weight)
    activation, normed_two_part, normed_opposite, *arrived = tied(
        activation, normed_two_part, normed_opposite, *from_beyond, *pairs[1:]
    )
    from_beyond, pairs[1:] = arrived[:3], arrived[3:]
    latest = []

    def in_turn(*values):
        values = tied(*values, *latest)[: len(values)]
        return values if len(values) > 1 else values[0]

    def over(*values):
        latest[:] = values

    over(normed_two_part, activation)
    one_mine = share_of(normed_one[:row_total])
    shown = jnp.stack([one_mine[:, :half_width], one_mine[:, half_width:]])
    spare = ((0, 0), (0, half_width - channels))
    shown = jnp.concatenate([jnp.pad(mixed[:row_total], spare), shown.reshape(-1, half_width)])
    shown = lax.all_gather(in_turn(shown), plane)
    normed_two_grad = summed(normed_two_part)

    gathered = [together] + from_near + from_beyond
    hidden_rows, normed_all, upstream_all = first_hidden(
        [(rows, 0) for rows in gathered] + [(normed_opposite, 0)],
        [(rows, unit) for rows in gathered] + [(upstream_opposite, 0)],
        unit,
        [in_turn(pairs[0])] + pairs[1:],
        downs,
        group,
    )
    over(hidden_rows)

    def of_others(rows):
        blocks = []
        for core in range(1, cores):
            blocks.append(weight_terms(in_turn(rows), normed_all, upstream_all, shard, core))
            over(blocks[-1])
        return [turned(block, "mp", -core - 1) for core, block in enumerate(blocks)]

    def of_mine(rows, received):
        block = weight_terms(in_turn(rows), normed_all, upstream_all, shard, 0, received)
        over(block)
        return block

    received = of_others(hidden_rows)
    next_rows = None
    if groups > 1:
        next_rows = next_hidden(in_turn(normed_all), upstream_all, pairs, downs, group, 1)
        over(next_rows)
    block = of_mine(hidden_rows, received)
    placed = shared_out(block, column + plane)

    normed_two_grad = in_turn(normed_two_grad)
    inner_grad = upstream.astype(full) + norm_back(
        inner_sum, inv_rms_two, norm2_gain, normed_two_grad
    )
    branch_grad = inner_grad.astype(low)
    spot = lax.axis_index(plane).astype(jnp.int32).reshape(1)
    sent, taps_grad = unmixing(
        branch_grad, out_weight, mixer_state, conv_weight, seq_count, local_len, shard, spot
    )
    over(sent)
    side_blocks = [swapped(sent[1:2], "d"), swapped(sent[2:3], "c")]
    one_all = [shown[:, row_total:].reshape(4, 2, unit, half_width)]
    if groups > 1:
        received = of_others(next_rows)
    over(*latest, *side_blocks)
    across = lax.ppermute(in_turn(sent)[3:4], plane, [(i, 3 - i) for i in range(4)])
    one_all[0] = in_turn(one_all[0])
    one_all += others(one_all[0], "mp")
    if groups > 1:
        next_block = of_mine(next_rows, received)
    over(*latest, across, *one_all[1:])
    terms = mixer_terms(
        [in_turn(sent)] + side_blocks + [across], 3 * quarter, one_all, shown, channels, shard, spot
    )
    over(terms)
    terms = lax.psum_scatter(terms, column, scatter_dimension=0)
    normed_one_part = unprojected(in_turn(sent), in_parts, spot)
    over(normed_one_part)
    if groups > 1:
        next_block, placed = in_turn(next_block, placed)
        next_placed = shared_out(next_block, column + plane)
        over(placed)
    parts_one = both_parts(in_turn(normed_one_part))
    output_part = product_of(in_turn(activation[:row_total]), down_weight)
    over(output_part)
    totals = put_in_place(in_turn(placed), parts, 0, groups, ())
    over(*totals)
    tokens_grad, gain_one = tokens_grad_of(
        in_turn(inputs), inv_rms_one, norm1_gain, inner_grad, parts_one, row_total, cores
    )
    over(tokens_grad)
    output = (inner_sum[:row_total] + summed(in_turn(output_part))).astype(low)
    gain_two = jnp.sum(
        share_of((normed_two_grad * inner_sum * inv_rms_two)[:row_total]), axis=0
    )
    channel_start = lax.axis_index("mp") * channels
    taps_full = lax.dynamic_update_slice_in_dim(
        jnp.zeros((3, width), full), taps_grad, channel_start, 1
    )
    small = in_turn(jnp.concatenate([gain_one, gain_two[None], taps_full], axis=0))
    for axis in ("d", "c", "b", "a", "mp"):
        if lax.axis_size(axis) == 2:
            small = small + swapped(small, axis)
        else:
            small = lax.psum(small, axis)
    deep_rows = 12 * quarter
    in_total = terms[:deep_rows].reshape(4, 3 * quarter, shard)
    out_total = terms[deep_rows:].astype(full)
    if groups > 1:
        next_placed, in_total = tied(next_placed, in_total)
        totals = put_in_place(next_placed, parts, 1, groups, totals)
    in_total = shared_out(in_total, plane)
    gate_up_total, down_total = totals
    in_total = (
        in_total.astype(full)
        .reshape(4, 3, quarter, shard)
        .transpose(3, 1, 0, 2)
        .reshape(shard, 3, channels)
    )
    taps_total = lax.dynamic_slice_in_dim(small[2:], channel_start, channels, 1)
    return (
        output.reshape(seq_count, local_len, width),
        tokens_grad.reshape(seq_count, local_len, width),
        small[0],
        in_total,
        taps_total,
        out_total,
        small[1],
        gate_up_total,
        down_total,
    )


def solution(mesh):
    seq, mp = mesh.shape["seq"], mesh.shape["mp"]
    fine = Mesh(mesh.devices.reshape(seq // 8, 2, 2, 2, mp), ("a", "b", "c", "d", "mp"))
    by_seq = ("a", "b", "c", "d")
    return jax.shard_map(
        local,
        mesh=fine,
        in_specs=(
            P(None, by_seq, None),
            P(),
            P(None, None, "mp"),
            P(None, "mp"),
            P("mp", None),
            P(),
            P(None, None, "mp"),
            P("mp", None),
            P(None, by_seq, None),
        ),
        out_specs=(
            P(None, by_seq, None),
            P(None, by_seq, None),
            P(),
            P(by_seq, None, "mp"),
            P(None, "mp"),
            P("mp", by_seq),
            P(),
            P(by_seq, None, "mp"),
            P("mp", by_seq),
        ),
        check_vma=False,
    )
```

```python
import functools

import jax
import jax.numpy as jnp
from jax import lax
from jax.experimental import pallas as pl
from jax.experimental.pallas import tpu as pltpu
from jax.sharding import Mesh, PartitionSpec as P

epsilon = 1e-05
low = jnp.bfloat16
full = jnp.float32
plain = ((1,), (0,))
flipped = ((1,), (1,))
params = pltpu.CompilerParams(vmem_limit_bytes=56 * 2**20)


brief = pl.CostEstimate(flops=1000, bytes_accessed=1000, transcendentals=0)


def swapped(block, axis):
    return lax.ppermute(block, axis, [(0, 1), (1, 0)])


def passed_along(block, axis, distance):
    devices = range(lax.axis_size(axis))
    route = [(i - distance, i) for i in devices if i - distance in devices]
    return lax.ppermute(block, axis, route)


def turned(block, axis, distance):
    count = lax.axis_size(axis)
    return lax.ppermute(block, axis, [(i, (i + distance) % count) for i in range(count)])


def others(block, axis):
    return [turned(block, axis, step) for step in range(1, lax.axis_size(axis))]


def both_parts(partial):
    if lax.axis_size("mp") == 2:
        return [partial, swapped(partial, "mp")]
    return [lax.psum(partial, "mp")]


def summed(partial):
    return sum(part.astype(full) for part in both_parts(partial.astype(low)))


def over_all(values, axes):
    count = lax.axis_size(axes)
    near_by, *rest = [
        lax.ppermute(values, axes, [(i, i ^ mask) for i in range(count)]) for mask in range(1, count)
    ]
    total = values + near_by
    return total + (rest[0] + rest[1]) if rest else total


def share_of(rows):
    count = rows.shape[0] // lax.axis_size("mp")
    return lax.dynamic_slice_in_dim(rows, lax.axis_index("mp") * count, count, 0)


def tied(*values):
    return lax.optimization_barrier(values)


def near(mine):
    return [swapped(mine, axis) for axis in "bcd"]


def beyond(from_near, axes="cdb"):
    return [swapped(piece, axis) for piece, axis in zip(from_near, axes)]


def opposite(mine):
    return lax.ppermute(mine, ("b", "c", "d"), [(i, 7 - i) for i in range(8)])


def row_kernel(makings, *refs):
    for place, making in enumerate(makings):
        out_ref, row = refs[len(refs) - len(makings) + place], 0
        for part in making:
            index, start, rows = part if isinstance(part, tuple) else (part, 0, None)
            rows = refs[index].shape[0] if rows is None else rows
            out_ref[row : row + rows] = refs[index][start : start + rows]
            row += rows


def in_rows(arrays, makings):
    width = arrays[0].shape[1]

    def rows(making):
        return sum(
            part[2] if isinstance(part, tuple) else arrays[part].shape[0] for part in making
        )

    whole = pl.BlockSpec(memory_space=pltpu.VMEM)
    return pl.pallas_call(
        functools.partial(row_kernel, makings),
        in_specs=[whole] * len(arrays),
        out_specs=[whole] * len(makings),
        out_shape=[jax.ShapeDtypeStruct((rows(making), width), low) for making in makings],
        compiler_params=params,
        cost_estimate=brief,
    )(*arrays)


def shared_out(blocks, axes):
    return lax.all_to_all(blocks, axes, 0, 0, tiled=True)


def shown_to_all(mine, axes):
    return shared_out(jnp.broadcast_to(mine, (lax.axis_size(axes),) + mine.shape), axes)


def normalize(values, gain_vec):
    inv_rms = lax.rsqrt(jnp.mean(values * values, axis=-1, keepdims=True) + epsilon)
    return (values * inv_rms * gain_vec, inv_rms)


def norm_back(values, inv_rms, gain_vec, upstream):
    scaled = values * inv_rms
    weighted = upstream * gain_vec
    inner_mean = jnp.mean(weighted * scaled, axis=-1, keepdims=True)
    return inv_rms * (weighted - scaled * inner_mean)


def dot(left, right, dims):
    return lax.dot_general(left, right, (dims, ((), ())), preferred_element_type=full)


def hidden_terms(gate_pre, up_pre, activation_grad):
    sigmoid_gate = jax.nn.sigmoid(gate_pre)
    swish_gate = gate_pre * sigmoid_gate
    gate_grad = activation_grad * up_pre * sigmoid_gate * (1.0 + gate_pre * (1.0 - sigmoid_gate))
    return (
        (swish_gate * up_pre).astype(low),
        gate_grad.astype(low),
        (activation_grad * swish_gate).astype(low),
    )


def both_ways_kernel(
    x_ref, own_ref, after_ref, pair_ref, down_ref, act_ref, grad_ref, grad_sum, c_ref
):
    step = pl.program_id(0)
    own = own_ref.shape[0]

    @pl.when(step == 0)
    def _():
        grad_sum[...] = jnp.zeros_like(grad_sum)
        c_ref[:own] = own_ref[...]
        c_ref[own:] = after_ref[...]

    activation, gate_grad, up_grad = hidden_terms(
        dot(x_ref[...], pair_ref[0], plain),
        dot(x_ref[...], pair_ref[1], plain),
        dot(c_ref[...], down_ref[...], flipped),
    )
    act_ref[...] = activation
    grad_sum[...] += dot(gate_grad, pair_ref[0], flipped) + dot(up_grad, pair_ref[1], flipped)

    @pl.when(step == pl.num_programs(0) - 1)
    def _():
        grad_ref[...] = grad_sum[...].astype(low)


def both_ways(normed, upstream, after, pair, down):
    rows, width = normed.shape
    hidden = down.shape[0]
    tile = min(512, hidden)
    whole = pl.BlockSpec((rows, width), lambda i: (0, 0))
    return pl.pallas_call(
        both_ways_kernel,
        grid=(hidden // tile,),
        in_specs=[
            whole,
            pl.BlockSpec(upstream.shape, lambda i: (0, 0)),
            pl.BlockSpec(after.shape, lambda i: (0, 0)),
            pl.BlockSpec((2, width, tile), lambda i: (0, 0, i)),
            pl.BlockSpec((tile, width), lambda i: (i, 0)),
        ],
        out_specs=[pl.BlockSpec((rows, tile), lambda i: (0, i)), whole],
        out_shape=[
            jax.ShapeDtypeStruct((rows, hidden), low),
            jax.ShapeDtypeStruct((rows, width), low),
        ],
        scratch_shapes=[pltpu.VMEM((rows, width), full), pltpu.VMEM((rows, width), low)],
        compiler_params=params,
        cost_estimate=brief,
    )(normed, upstream, after, pair, down)


def copy_kernel(place_ref, from_ref, to_ref):
    to_ref[...] = from_ref[...]


def own_columns(pair, place, part, group):
    _, width, _ = pair.shape
    return pl.pallas_call(
        copy_kernel,
        grid_spec=pltpu.PrefetchScalarGridSpec(
            num_scalar_prefetch=1,
            grid=(2,),
            in_specs=[pl.BlockSpec((1, width, part), lambda k, p: (k, 0, 8 * group + p[0]))],
            out_specs=pl.BlockSpec((1, width, part), lambda k, p: (k, 0, 0)),
        ),
        out_shape=jax.ShapeDtypeStruct((2, width, part), low),
        compiler_params=params,
        cost_estimate=brief,
    )(place, pair)


def write_hidden(x, c, weights, hidden_ref):
    part = hidden_ref.shape[1] // 3
    for core, (gate_ref, up_ref, down_ref) in enumerate(weights):
        activation, gate_grad, up_grad = hidden_terms(
            dot(x, gate_ref[0], plain),
            dot(x, up_ref[0], plain),
            dot(c, down_ref[0], flipped),
        )
        for n, term in enumerate((gate_grad, up_grad, activation)):
            hidden_ref[core, n * part : (n + 1) * part] = term.T


def threes(refs):
    return [refs[start : start + 3] for start in range(0, len(refs), 3)]


def first_hidden_kernel(counts, spots, unit, *refs):
    pieces = refs[: counts[0]], refs[counts[0] : sum(counts)]
    *weights, hidden_ref, x_out, c_out, x_all, c_all, arrivals, leaving = refs[sum(counts) :]
    both = (x_all, x_out), (c_all, c_out)
    count = len(spots[0])
    block = hidden_ref.shape[2]
    together = block // unit
    step = pl.program_id(0)

    def coming(index):
        rows = pl.ds(index * unit, unit)
        copies = []
        for n in range(2):
            piece, start = spots[n][index]
            source = pieces[n][piece].at[pl.ds(start, unit)]
            copies.append(
                pltpu.make_async_copy(source, both[n][0].at[rows], arrivals.at[n, index])
            )
        return copies

    def going(index):
        rows = pl.ds(index * block, block)
        return [
            pltpu.make_async_copy(here.at[rows], there.at[rows], leaving.at[n, index])
            for n, (here, there) in enumerate(both)
        ]

    @pl.when(step == 0)
    def _():
        for index in range(count):
            for copy in coming(index):
                copy.start()

    for index in range(count // together):

        @pl.when(step == index)
        def _(index=index):
            for piece in range(index * together, (index + 1) * together):
                for copy in coming(piece):
                    copy.wait()
            for copy in going(index):
                copy.start()

    rows = pl.ds(step * block, block)
    write_hidden(x_all[rows], c_all[rows], threes(weights), hidden_ref)

    @pl.when(step == pl.num_programs(0) - 1)
    def _():
        for index in range(count // together):
            for copy in going(index):
                copy.wait()


def next_hidden_kernel(x_ref, c_ref, *refs):
    write_hidden(x_ref[...], c_ref[...], threes(refs[:-1]), refs[-1])


def weight_operands(pairs, downs, index):
    _, width, part = pairs[0].shape
    specs, arrays = [], []
    for pair, down in zip(pairs, downs):
        specs += [
            pl.BlockSpec((1, width, part), lambda i, k=k: (k, 0, 0)) for k in range(2)
        ]
        specs.append(pl.BlockSpec((1, part, width), lambda i: (index, 0, 0)))
        arrays += [pair, pair, down]
    return specs, arrays


def first_hidden(x_pieces, c_pieces, unit, pairs, downs):
    width = downs[0].shape[2]
    arrays, spots = [], []
    for row in (x_pieces, c_pieces):
        known = []
        for array, _ in row:
            if not any(array is other for other in known):
                known.append(array)
        arrays.append(known)
        spots.append(
            [
                (next(n for n, other in enumerate(known) if other is array), start)
                for array, start in row
            ]
        )
    counts = tuple(len(known) for known in arrays)
    count, own, cores = len(x_pieces), downs[0].shape[1], len(downs)
    block, rows = max(1, 384 // unit) * unit, count * unit
    anywhere = pl.BlockSpec(memory_space=pl.ANY)
    row_shape = jax.ShapeDtypeStruct((rows, width), low)
    specs, weights = weight_operands(pairs, downs, 0)
    return pl.pallas_call(
        functools.partial(first_hidden_kernel, counts, spots, unit),
        grid=(rows // block,),
        in_specs=[anywhere] * sum(counts) + specs,
        out_specs=[
            pl.BlockSpec((cores, 3 * own, block), lambda i: (0, 0, i)),
            anywhere,
            anywhere,
        ],
        scratch_shapes=[
            pltpu.VMEM((rows, width), low),
            pltpu.VMEM((rows, width), low),
            pltpu.SemaphoreType.DMA((2, count)),
            pltpu.SemaphoreType.DMA((2, rows // block)),
        ],
        out_shape=[
            jax.ShapeDtypeStruct((cores, 3 * own, rows), low),
            row_shape,
            row_shape,
        ],
        compiler_params=params,
        cost_estimate=brief,
    )(*arrays[0], *arrays[1], *weights)


def next_hidden(x_all, c_all, pairs, downs, index):
    rows, width = x_all.shape
    own, cores = downs[0].shape[1], len(downs)
    block = min(384, rows)
    tokens = pl.BlockSpec((block, width), lambda i: (i, 0))
    specs, weights = weight_operands(pairs, downs, index)
    return pl.pallas_call(
        next_hidden_kernel,
        grid=(rows // block,),
        in_specs=[tokens, tokens] + specs,
        out_specs=pl.BlockSpec((cores, 3 * own, block), lambda i: (0, 0, i)),
        out_shape=jax.ShapeDtypeStruct((cores, 3 * own, rows), low),
        compiler_params=params,
        cost_estimate=brief,
    )(x_all, c_all, *weights)


def weight_kernel(hidden_ref, x_ref, c_ref, *refs):
    arrived, out_ref = refs[:-1], refs[-1]
    two = 2 * hidden_ref.shape[1] // 3
    shard = out_ref.shape[2]
    pair = dot(hidden_ref[0, :two], x_ref[...], plain)
    single = dot(hidden_ref[0, two:], c_ref[...], plain)
    for j in range(out_ref.shape[0]):
        columns = slice(j * shard, (j + 1) * shard)
        for rows, term in ((slice(0, two), pair), (slice(two, None), single)):
            total = term[:, columns]
            for ref in arrived:
                total = total + ref[j, rows].astype(full)
            out_ref[j, rows] = total.astype(low)


def weight_terms(hidden, normed, upstream, shard, core, arrived=()):
    three, rows = hidden.shape[1:]
    width = normed.shape[1]
    tile = max(512, shard)
    columns = pl.BlockSpec((rows, tile), lambda i: (0, i))
    out_block = pl.BlockSpec((tile // shard, three, shard), lambda i: (i, 0, 0))
    return pl.pallas_call(
        weight_kernel,
        grid=(width // tile,),
        in_specs=[pl.BlockSpec((1, three, rows), lambda i: (core, 0, 0)), columns, columns]
        + [out_block] * len(arrived),
        out_specs=out_block,
        out_shape=jax.ShapeDtypeStruct((width // shard, three, shard), low),
        compiler_params=params,
        cost_estimate=brief,
    )(hidden, normed, upstream, *arrived)


def mixing_kernel(facts, x_ref, weight_ref, taps_ref, mixed_ref, kept_ref, line):
    seqs, length, gap = facts
    own, side = seqs * length, 2 * seqs
    x = x_ref[...]
    b_gate, c_gate, values = (dot(x, weight_ref[k], plain) for k in range(3))
    product = b_gate * values
    conv_out = [None] * (2 * seqs)
    for seq in range(seqs):
        before, after = own + side + 2 * seq, own + 2 * seq
        line[seq, 0:2] = product[before : before + 2]
        line[seq, 2 : length + 2] = product[seq * length : (seq + 1) * length]
        line[seq, length + 2 : length + 4] = product[after : after + 2]
        conv = sum(taps_ref[tap] * line[seq, tap : tap + length + 2] for tap in range(3))
        kept_ref[3, seq * length : (seq + 1) * length] = conv[:length]
        kept_ref[3, after : after + 2] = conv[length:]
    kept_ref[3, own + side :] = jnp.zeros_like(product[own + side :])
    kept_ref[0], kept_ref[1], kept_ref[2] = b_gate, c_gate, values
    mixed_ref[...] = (c_gate * kept_ref[3]).astype(low)


def mixing(normed, weight, taps, seqs, length):
    rows, width = normed.shape
    channels = weight.shape[2]
    tile = channels // 4
    return pl.pallas_call(
        functools.partial(mixing_kernel, (seqs, length, 0)),
        grid=(4,),
        in_specs=[
            pl.BlockSpec((rows, width), lambda i: (0, 0)),
            pl.BlockSpec((3, width, tile), lambda i: (0, 0, i)),
            pl.BlockSpec((3, tile), lambda i: (0, i)),
        ],
        out_specs=[
            pl.BlockSpec((rows, tile), lambda i: (0, i)),
            pl.BlockSpec((4, rows, tile), lambda i: (0, 0, i)),
        ],
        out_shape=[
            jax.ShapeDtypeStruct((rows, channels), low),
            jax.ShapeDtypeStruct((4, rows, channels), full),
        ],
        scratch_shapes=[pltpu.VMEM((seqs, length + 8, tile), full)],
        compiler_params=params,
        cost_estimate=brief,
    )(normed, weight, taps)


def unmixing_kernel(facts, spot_ref, grad_ref, weight_ref, kept_ref, taps_ref, *refs):
    *sent, sums_ref, line, past = refs
    seqs, length, deep, shard = facts
    own, side = seqs * length, 2 * seqs
    tile = weight_ref.shape[0]
    mixed_grad = dot(grad_ref[...], weight_ref[...], flipped)
    conv_grad = mixed_grad * kept_ref[1]
    blocks = []
    for seq in range(seqs):
        rows = slice(seq * length, (seq + 1) * length)
        before, after = own + side + 2 * seq, own + 2 * seq
        line[seq, 0:length] = conv_grad[rows]
        line[seq, length : length + 2] = conv_grad[after : after + 2]
        product_grad = sum(taps_ref[2 - tap] * line[seq, tap : tap + length] for tap in range(3))
        b_gate, values = kept_ref[0, rows], kept_ref[2, rows]
        grads = (product_grad * values, mixed_grad[rows] * kept_ref[3, rows], product_grad * b_gate)
        blocks.append((rows, [grad.astype(low) for grad in grads]))
        past[seq, 0:2] = kept_ref[0, before : before + 2] * kept_ref[2, before : before + 2]
        past[seq, 2 : length + 2] = b_gate * values
    for tap in range(3):
        sums_ref[tap : tap + 1] = sum(
            jnp.sum(line[seq, 0:length] * past[seq, tap : tap + length], axis=0, keepdims=True)
            for seq in range(seqs)
        )
    for mask, sent_ref in enumerate(sent):

        @pl.when(pl.program_id(0) == mask)
        def _(mask=mask, sent_ref=sent_ref):
            for rows, grads in blocks:
                for k, grad in enumerate(grads):
                    sent_ref[rows, k * tile : (k + 1) * tile] = grad
            for part in range(4):

                @pl.when(spot_ref[0] == part ^ mask)
                def _(part=part):
                    for far in range(deep):
                        start = (far * 4 + part) * shard
                        to = 3 * tile + far * shard
                        sent_ref[:, to : to + shard] = grad_ref[0:own, start : start + shard]


def unmixing(grad, weight, kept, taps, seqs, length, shard, spot):
    rows, width = grad.shape
    channels = weight.shape[0]
    tile, deep = channels // 4, width // (4 * shard)
    wide = 3 * tile + deep * shard
    block = pl.BlockSpec((seqs * length, wide), lambda i, p: (0, 0))
    return pl.pallas_call(
        functools.partial(unmixing_kernel, (seqs, length, deep, shard)),
        grid_spec=pltpu.PrefetchScalarGridSpec(
            num_scalar_prefetch=1,
            grid=(4,),
            in_specs=[
                pl.BlockSpec((rows, width), lambda i, p: (0, 0)),
                pl.BlockSpec((tile, width), lambda i, p: (i ^ p[0], 0)),
                pl.BlockSpec((4, rows, tile), lambda i, p: (0, 0, i ^ p[0])),
                pl.BlockSpec((3, tile), lambda i, p: (0, i ^ p[0])),
            ],
            out_specs=[block] * 4 + [pl.BlockSpec((3, tile), lambda i, p: (0, i ^ p[0]))],
            scratch_shapes=[pltpu.VMEM((seqs, length + 8, tile), full)] * 2,
        ),
        out_shape=[jax.ShapeDtypeStruct((seqs * length, wide), low)] * 4
        + [jax.ShapeDtypeStruct((3, channels), full)],
        compiler_params=params,
        cost_estimate=brief,
    )(spot, grad, weight, kept, taps)


def unprojected_kernel(spot_ref, *refs):
    *sent, weight_ref, out_ref, total = refs
    step = pl.program_id(0)
    tile = weight_ref.shape[2]
    for mask, sent_ref in enumerate(sent):

        @pl.when(step == mask)
        def _(mask=mask, sent_ref=sent_ref):
            term = sum(
                dot(sent_ref[:, k * tile : (k + 1) * tile], weight_ref[k], flipped)
                for k in range(3)
            )
            total[...] = term if mask == 0 else total[...] + term

    @pl.when(step == len(sent) - 1)
    def _():
        out_ref[...] = total[...].astype(low)


def unprojected(sent, weight, spot):
    rows = sent[0].shape[0]
    width, channels = weight.shape[1:]
    tile = channels // 4
    return pl.pallas_call(
        unprojected_kernel,
        grid_spec=pltpu.PrefetchScalarGridSpec(
            num_scalar_prefetch=1,
            grid=(4,),
            in_specs=[pl.BlockSpec((rows, 3 * tile), lambda i, p: (0, 0))] * 4
            + [pl.BlockSpec((3, width, tile), lambda i, p: (0, 0, i ^ p[0]))],
            out_specs=pl.BlockSpec((rows, width), lambda i, p: (0, 0)),
            scratch_shapes=[pltpu.VMEM((rows, width), full)],
        ),
        out_shape=jax.ShapeDtypeStruct((rows, width), low),
        compiler_params=params,
        cost_estimate=brief,
    )(spot, *sent, weight)


def mixer_kernel(cores, facts_ref, *refs):
    sent, (mixed_ref, *refs) = refs[:4], refs[4:]
    rights, in_ref, out_ref = refs[:cores], refs[cores], refs[cores + 1]
    gathered, turned_rows, turned_mixed, columns = refs[cores + 2 :]
    chips, rows, channels = mixed_ref.shape
    count = turned_rows.shape[1]
    share = rows // cores
    shard = out_ref.shape[2]
    step = pl.program_id(0)

    @pl.when(step == 0)
    def _():
        for index in range(cores):
            core = lax.rem(facts_ref[1] + cores - index, cores)
            start = pl.multiple_of(core * share, 16)
            for mask, ref in enumerate(sent):
                place = pl.multiple_of((facts_ref[0] ^ mask) * share, 16)
                gathered[pl.ds(place, share)] = ref[pl.ds(start, share), :count]
            turned_rows[index] = gathered[...].T
        turned_mixed[...] = mixed_ref[...].reshape(chips * rows, channels).T
        for mask, ref in enumerate(sent):
            place = pl.multiple_of((facts_ref[0] ^ mask) * rows, 16)
            for far in range(columns.shape[0]):
                start = count + far * shard
                columns[far, pl.ds(place, rows)] = ref[:, start : start + shard]

    total = sum(
        dot(turned_rows[index], rights[index][...].reshape(chips * share, chips * shard), plain)
        for index in range(cores)
    )
    for j in range(chips):
        in_ref[j] = total[:, j * shard : (j + 1) * shard].astype(low)
    out_ref[0] = dot(turned_mixed[...], columns[step], plain).astype(low)


def mixer_terms(sent, count, rights, shown, channels, shard, spot):
    rows, wide = sent[0].shape
    cores = len(rights)
    chips, _, share, half = rights[0].shape
    tile = chips * shard
    tiles = half // tile
    deep = 2 * tiles
    facts = [spot[0], lax.axis_index("mp").astype(jnp.int32)]
    right = pl.BlockSpec((chips, 1, share, tile), lambda i, p: (0, i // tiles, 0, i % tiles))
    return pl.pallas_call(
        functools.partial(mixer_kernel, cores),
        grid_spec=pltpu.PrefetchScalarGridSpec(
            num_scalar_prefetch=1,
            grid=(deep,),
            in_specs=[pl.BlockSpec((rows, wide), lambda i, p: (0, 0))] * chips
            + [pl.BlockSpec((chips, rows, channels), lambda i, p: (0, 0, 0))]
            + [right] * cores,
            out_specs=[
                pl.BlockSpec((chips, count, shard), lambda i, p: (i, 0, 0)),
                pl.BlockSpec((1, channels, shard), lambda i, p: (i, 0, 0)),
            ],
            scratch_shapes=[
                pltpu.VMEM((chips * share, count), low),
                pltpu.VMEM((cores, count, chips * share), low),
                pltpu.VMEM((channels, chips * rows), low),
                pltpu.VMEM((deep, chips * rows, shard), low),
            ],
        ),
        out_shape=[
            jax.ShapeDtypeStruct((deep * chips, count, shard), low),
            jax.ShapeDtypeStruct((deep, channels, shard), low),
        ],
        compiler_params=params,
        cost_estimate=brief,
    )(jnp.stack(facts), *sent, shown, *rights)


def placing_kernel(parts, *refs):
    placed_ref, pair_ref, down_ref = refs[0], refs[-2], refs[-1]
    chips, three, _ = placed_ref.shape
    chips //= parts
    own = three // 3
    for chip in range(chips):
        block = sum(placed_ref[part * chips + chip].astype(full) for part in range(parts))
        rows = slice(chip * own, (chip + 1) * own)
        pair_ref[:, 0, rows] = block[:own].T
        pair_ref[:, 1, rows] = block[own : 2 * own].T
        down_ref[rows] = block[2 * own :]


def put_in_place(placed, parts, index, groups, before):
    chips, three, shard = placed.shape
    columns = chips // parts * three // 3
    return pl.pallas_call(
        functools.partial(placing_kernel, parts),
        grid=(1,),
        in_specs=[pl.BlockSpec(placed.shape, lambda i: (0, 0, 0))]
        + [pl.BlockSpec(memory_space=pl.ANY)] * len(before),
        out_specs=[
            pl.BlockSpec((shard, 2, columns), lambda i: (0, 0, index)),
            pl.BlockSpec((columns, shard), lambda i: (index, 0)),
        ],
        out_shape=[
            jax.ShapeDtypeStruct((shard, 2, groups * columns), full),
            jax.ShapeDtypeStruct((groups * columns, shard), full),
        ],
        input_output_aliases={1 + n: n for n in range(len(before))},
        compiler_params=params,
        cost_estimate=brief,
    )(placed, *before)


def product_kernel(left_ref, right_ref, out_ref, total):
    step = pl.program_id(0)
    term = dot(left_ref[...], right_ref[...], plain)

    @pl.when(step == 0)
    def _():
        total[...] = term

    @pl.when(step > 0)
    def _():
        total[...] += term

    @pl.when(step == pl.num_programs(0) - 1)
    def _():
        out_ref[...] = total[...].astype(low)


def product_of(left, right):
    rows, depth = left.shape
    width = right.shape[1]
    tile = min(1024, depth)
    return pl.pallas_call(
        product_kernel,
        grid=(depth // tile,),
        in_specs=[
            pl.BlockSpec((rows, tile), lambda i: (0, i)),
            pl.BlockSpec((tile, width), lambda i: (i, 0)),
        ],
        out_specs=pl.BlockSpec((rows, width), lambda i: (0, 0)),
        out_shape=jax.ShapeDtypeStruct((rows, width), low),
        scratch_shapes=[pltpu.VMEM((rows, width), full)],
        compiler_params=params,
        cost_estimate=brief,
    )(left, right)


def tokens_grad_kernel(core_ref, values_ref, inv_ref, gain_ref, inner_ref, *refs):
    parts, (out_ref, sums_ref) = refs[:-2], refs[-2:]
    upstream = sum(ref[...].astype(full) for ref in parts)
    scaled = values_ref[...] * inv_ref[...]
    weighted = upstream * gain_ref[...]
    inner_mean = jnp.mean(weighted * scaled, axis=-1, keepdims=True)
    out_ref[...] = (inner_ref[...] + inv_ref[...] * (weighted - scaled * inner_mean)).astype(low)

    @pl.when(pl.program_id(0) == core_ref[0])
    def _():
        sums_ref[...] = jnp.sum(upstream * scaled, axis=0, keepdims=True)


def tokens_grad_of(values, inv_rms, gain_vec, inner_grad, parts, rows, cores):
    width = values.shape[1]
    share = rows // cores
    core = lax.axis_index("mp").astype(jnp.int32).reshape(1)
    block = pl.BlockSpec((share, width), lambda i, p: (i, 0))
    line = pl.BlockSpec((1, width), lambda i, p: (0, 0))
    return pl.pallas_call(
        tokens_grad_kernel,
        grid_spec=pltpu.PrefetchScalarGridSpec(
            num_scalar_prefetch=1,
            grid=(cores,),
            in_specs=[block, pl.BlockSpec((share, 1), lambda i, p: (i, 0)), line, block]
            + [block] * len(parts),
            out_specs=[block, line],
        ),
        out_shape=[
            jax.ShapeDtypeStruct((rows, width), low),
            jax.ShapeDtypeStruct((1, width), full),
        ],
        compiler_params=params,
        cost_estimate=brief,
    )(core, values, inv_rms, gain_vec.reshape(1, -1), inner_grad, *parts)


def local(
    tokens,
    norm1_gain,
    in_weight,
    conv_weight,
    out_weight,
    norm2_gain,
    gate_up,
    down_weight,
    cotangent,
):
    seq_count, local_len, width = tokens.shape
    row_total = seq_count * local_len
    channels = in_weight.shape[2]
    hidden = gate_up.shape[2]
    parts = lax.axis_size("a")
    cores = lax.axis_size("mp")
    shard = width // (parts * 8)
    deep = width // (4 * shard)
    quarter = channels // 4
    cube, plane, column = ("b", "c", "d"), ("c", "d"), ("a", "b")
    place = lax.axis_index(cube).astype(jnp.int32).reshape(1)
    own = hidden // 8
    in_parts = jnp.transpose(in_weight, (1, 0, 2))

    after = passed_along(
        jnp.stack([tokens[:, :2], cotangent[:, :2]]), column + plane, -1
    ).reshape(2, -1, width)
    before = passed_along(tokens[:, local_len - 2 :], column + plane, 1).reshape(-1, width)
    side = before.shape[0]
    padding = jnp.zeros((2 * side + (-2 * side) % 16, width), low)
    before, upstream_mine = tied(before, share_of(cotangent.reshape(row_total, width)))
    inputs = jnp.concatenate(
        [tokens.reshape(row_total, width), after[0], before, padding[2 * side :]]
    ).astype(full)
    upstream_own = cotangent.reshape(row_total, width)
    upstream_after = jnp.concatenate([after[1], padding[side:]])
    upstream_grad = jnp.concatenate([upstream_own, upstream_after]).astype(full)
    normed_full_one, inv_rms_one = normalize(inputs, norm1_gain)
    normed_one = normed_full_one.astype(low)
    upstream_opposite = opposite(upstream_mine)
    mixed, mixer_state = mixing(normed_one, in_parts, conv_weight, seq_count, local_len)
    mixed, upstream_opposite = tied(mixed, upstream_opposite)
    inner_sum = inputs + summed(dot(mixed, out_weight, plain))
    normed_full_two, inv_rms_two = normalize(inner_sum, norm2_gain)
    normed_two = normed_full_two.astype(low)

    groups = 2 if own > 256 else 1
    half_width = width // 2
    part = own // groups
    unit = row_total // cores
    normed_mine = share_of(normed_two[:row_total])
    together = in_rows([normed_mine, upstream_mine], [(0, 1)])[0]
    from_near = near(together)
    firsts = [(index * 8 + place[0]) * part for index in range(groups)]
    down_own = jnp.stack(
        [lax.dynamic_slice_in_dim(down_weight, first, part, 0) for first in firsts]
    )
    downs = [down_own] + others(down_own, "mp")
    gate_up, together = tied(gate_up, together)
    pair_weight = lax.optimization_barrier(jnp.transpose(gate_up, (1, 0, 2)))
    pair_weight, normed_mine, *arrived = tied(
        pair_weight, normed_mine, *from_near, *downs[1:]
    )
    from_near, downs[1:] = arrived[:3], arrived[3:]
    from_beyond = beyond(from_near, "cdb")
    normed_opposite = opposite(normed_mine)
    pairs = [own_columns(pair_weight, place, part, 0)]
    pairs[0] = [pairs[0]] + others(pairs[0], "mp")
    pair_weight, pairs[0][0] = tied(pair_weight, pairs[0][0])
    activation, normed_two_part = both_ways(
        normed_two, upstream_own, upstream_after, pair_weight, down_weight
    )
    activation, normed_two_part, normed_opposite, *arrived = tied(
        activation, normed_two_part, normed_opposite, *from_beyond, *pairs[0][1:]
    )
    from_beyond, pairs[0][1:] = arrived[:3], arrived[3:]
    latest = []

    def in_turn(*values):
        values = tied(*values, *latest)[: len(values)]
        return values if len(values) > 1 else values[0]

    def over(*values):
        latest[:] = values

    over(normed_two_part, activation)
    one_mine = share_of(normed_one[:row_total])
    shown = jnp.stack([one_mine[:, :half_width], one_mine[:, half_width:]])
    spare = ((0, 0), (0, half_width - channels))
    shown = jnp.concatenate([jnp.pad(mixed[:row_total], spare), shown.reshape(-1, half_width)])
    shown = lax.all_gather(in_turn(shown), plane)
    normed_two_grad = summed(normed_two_part)

    gathered = [together] + from_near + from_beyond
    hidden_rows, normed_all, upstream_all = first_hidden(
        [(rows, 0) for rows in gathered] + [(normed_opposite, 0)],
        [(rows, unit) for rows in gathered] + [(upstream_opposite, 0)],
        unit,
        [in_turn(pairs[0][0])] + pairs[0][1:],
        downs,
    )
    def of_others(rows):
        blocks = []
        for core in range(1, cores):
            blocks.append(weight_terms(in_turn(rows), normed_all, upstream_all, shard, core))
            over(blocks[-1])
        return [turned(block, "mp", -core - 1) for core, block in enumerate(blocks)]

    def of_mine(rows, received):
        block = weight_terms(in_turn(rows), normed_all, upstream_all, shard, 0, received)
        over(block)
        return block

    over(hidden_rows)
    if groups > 1:
        next_pair = own_columns(in_turn(pair_weight), place, part, 1)
        over(next_pair)
        pairs.append([next_pair] + others(next_pair, "mp"))
    received = of_others(hidden_rows)
    normed_two_grad = in_turn(normed_two_grad)
    inner_grad = upstream_grad + norm_back(inner_sum, inv_rms_two, norm2_gain, normed_two_grad)
    branch_grad = inner_grad.astype(low)
    over(branch_grad)
    block = of_mine(hidden_rows, received)
    placed = shared_out(block, column + plane)
    if groups > 1:
        next_rows = next_hidden(in_turn(normed_all), upstream_all, pairs[1], downs, 1)
        over(next_rows)
        received = of_others(next_rows)
    spot = lax.axis_index(plane).astype(jnp.int32).reshape(1)
    *sent, taps_grad = unmixing(
        in_turn(branch_grad), out_weight, mixer_state, conv_weight, seq_count, local_len, shard, spot
    )
    over(*sent)
    seen = [sent[0], swapped(in_turn(sent[1]), "d"), swapped(in_turn(sent[2]), "c")]
    if groups > 1:
        next_block = of_mine(next_rows, received)
    over(*latest, *seen, shown, placed)
    if groups > 1:
        next_placed = shared_out(in_turn(next_block), column + plane)
    one_all = [in_turn(shown)[:, row_total:].reshape(4, 2, unit, half_width)]
    one_all += others(one_all[0], "mp")
    normed_one_part = unprojected([in_turn(sent[0])] + sent[1:], in_parts, spot)
    over(normed_one_part, *one_all[1:])
    seen.append(lax.ppermute(in_turn(sent[3]), plane, [(i, 3 - i) for i in range(4)]))
    output_part = product_of(in_turn(activation), down_weight)
    over(output_part, seen[3])
    seen[0] = in_turn(seen[0])
    in_terms, out_terms = mixer_terms(seen, 3 * quarter, one_all, shown, channels, shard, spot)
    if groups > 1:
        over(in_terms, next_placed)
    in_total = shared_out(in_turn(in_terms), column + plane)
    out_total = lax.psum_scatter(out_terms, column, scatter_dimension=0).astype(full)
    totals = put_in_place(placed, parts, 0, groups, ())
    if groups > 1:
        totals = put_in_place(next_placed, parts, 1, groups, totals)
    gate_up_total, down_total = totals
    parts_one = both_parts(in_turn(normed_one_part))
    tokens_grad, gain_one = tokens_grad_of(
        inputs, inv_rms_one, norm1_gain, inner_grad, parts_one, row_total, cores
    )
    gain_two = jnp.sum(
        share_of((normed_two_grad * inner_sum * inv_rms_two)[:row_total]), axis=0
    )
    channel_start = lax.axis_index("mp") * channels
    taps_full = lax.dynamic_update_slice_in_dim(
        jnp.zeros((3, width), full), taps_grad, channel_start, 1
    )
    small = jnp.concatenate([gain_one, gain_two[None], taps_full], axis=0)
    for axes in (("mp",), plane, column):
        if lax.axis_size(axes) <= 4:
            small = over_all(small, axes)
        else:
            small = lax.psum(small, axes)
    output = (inner_sum + summed(output_part))[:row_total].astype(low)
    in_total = (
        jnp.sum(in_total.astype(full).reshape(-1, 4, 3, quarter, shard), axis=0)
        .transpose(3, 1, 0, 2)
        .reshape(shard, 3, channels)
    )
    taps_total = lax.dynamic_slice_in_dim(small[2:], channel_start, channels, 1)
    return (
        output.reshape(seq_count, local_len, width),
        tokens_grad.reshape(seq_count, local_len, width),
        small[0],
        in_total,
        taps_total,
        out_total,
        small[1],
        gate_up_total,
        down_total,
    )


def solution(mesh):
    seq, mp = mesh.shape["seq"], mesh.shape["mp"]
    fine = Mesh(mesh.devices.reshape(seq // 8, 2, 2, 2, mp), ("a", "b", "c", "d", "mp"))
    by_seq = ("a", "b", "c", "d")
    return jax.shard_map(
        local,
        mesh=fine,
        in_specs=(
            P(None, by_seq, None),
            P(),
            P(None, None, "mp"),
            P(None, "mp"),
            P("mp", None),
            P(),
            P(None, None, "mp"),
            P("mp", None),
            P(None, by_seq, None),
        ),
        out_specs=(
            P(None, by_seq, None),
            P(None, by_seq, None),
            P(),
            P(by_seq, None, "mp"),
            P(None, "mp"),
            P("mp", by_seq),
            P(),
            P(by_seq, None, "mp"),
            P("mp", by_seq),
        ),
        check_vma=False,
    )
```

```python
import functools

import jax
import jax.numpy as jnp
from jax import lax
from jax.experimental import pallas as pl
from jax.experimental.pallas import tpu as pltpu
from jax.sharding import Mesh, PartitionSpec as P

epsilon = 1e-05
low = jnp.bfloat16
full = jnp.float32
plain = ((1,), (0,))
flipped = ((1,), (1,))
params = pltpu.CompilerParams(vmem_limit_bytes=56 * 2**20)


brief = pl.CostEstimate(flops=1000, bytes_accessed=1000, transcendentals=0)


def swapped(block, axis):
    return lax.ppermute(block, axis, [(0, 1), (1, 0)])


def passed_along(block, axis, distance):
    devices = range(lax.axis_size(axis))
    route = [(i - distance, i) for i in devices if i - distance in devices]
    return lax.ppermute(block, axis, route)


def turned(block, axis, distance):
    count = lax.axis_size(axis)
    return lax.ppermute(block, axis, [(i, (i + distance) % count) for i in range(count)])


def others(block, axis):
    return [turned(block, axis, step) for step in range(1, lax.axis_size(axis))]


def both_parts(partial):
    if lax.axis_size("mp") == 2:
        return [partial, swapped(partial, "mp")]
    return [lax.psum(partial, "mp")]


def summed(partial):
    return sum(part.astype(full) for part in both_parts(partial.astype(low)))


def over_all(values, axes):
    count = lax.axis_size(axes)
    near_by, *rest = [
        lax.ppermute(values, axes, [(i, i ^ mask) for i in range(count)]) for mask in range(1, count)
    ]
    total = values + near_by
    return total + (rest[0] + rest[1]) if rest else total


def share_of(rows):
    count = rows.shape[0] // lax.axis_size("mp")
    return lax.dynamic_slice_in_dim(rows, lax.axis_index("mp") * count, count, 0)


def tied(*values):
    return lax.optimization_barrier(values)


def near(mine):
    return [swapped(mine, axis) for axis in "bcd"]


def beyond(from_near, axes="cdb"):
    return [swapped(piece, axis) for piece, axis in zip(from_near, axes)]


def opposite(mine):
    return lax.ppermute(mine, ("b", "c", "d"), [(i, 7 - i) for i in range(8)])


def row_kernel(makings, *refs):
    for place, making in enumerate(makings):
        out_ref, row = refs[len(refs) - len(makings) + place], 0
        for part in making:
            index, start, rows = part if isinstance(part, tuple) else (part, 0, None)
            rows = refs[index].shape[0] if rows is None else rows
            out_ref[row : row + rows] = refs[index][start : start + rows]
            row += rows


def in_rows(arrays, makings):
    width = arrays[0].shape[1]

    def rows(making):
        return sum(
            part[2] if isinstance(part, tuple) else arrays[part].shape[0] for part in making
        )

    whole = pl.BlockSpec(memory_space=pltpu.VMEM)
    return pl.pallas_call(
        functools.partial(row_kernel, makings),
        in_specs=[whole] * len(arrays),
        out_specs=[whole] * len(makings),
        out_shape=[jax.ShapeDtypeStruct((rows(making), width), low) for making in makings],
        compiler_params=params,
        cost_estimate=brief,
    )(*arrays)


def shared_out(blocks, axes):
    return lax.all_to_all(blocks, axes, 0, 0, tiled=True)


def shown_to_all(mine, axes):
    return shared_out(jnp.broadcast_to(mine, (lax.axis_size(axes),) + mine.shape), axes)


def normalize(values, gain_vec):
    inv_rms = lax.rsqrt(jnp.mean(values * values, axis=-1, keepdims=True) + epsilon)
    return (values * inv_rms * gain_vec, inv_rms)


def norm_back(values, inv_rms, gain_vec, upstream):
    scaled = values * inv_rms
    weighted = upstream * gain_vec
    inner_mean = jnp.mean(weighted * scaled, axis=-1, keepdims=True)
    return inv_rms * (weighted - scaled * inner_mean)


def dot(left, right, dims):
    return lax.dot_general(left, right, (dims, ((), ())), preferred_element_type=full)


def hidden_terms(gate_pre, up_pre, activation_grad):
    sigmoid_gate = jax.nn.sigmoid(gate_pre)
    swish_gate = gate_pre * sigmoid_gate
    gate_grad = activation_grad * up_pre * sigmoid_gate * (1.0 + gate_pre * (1.0 - sigmoid_gate))
    return (
        (swish_gate * up_pre).astype(low),
        gate_grad.astype(low),
        (activation_grad * swish_gate).astype(low),
    )


def both_ways_kernel(
    x_ref, own_ref, after_ref, pair_ref, down_ref, act_ref, grad_ref, grad_sum, c_ref
):
    step = pl.program_id(0)
    own = own_ref.shape[0]

    @pl.when(step == 0)
    def _():
        grad_sum[...] = jnp.zeros_like(grad_sum)
        c_ref[:own] = own_ref[...]
        c_ref[own:] = after_ref[...]

    activation, gate_grad, up_grad = hidden_terms(
        dot(x_ref[...], pair_ref[0], plain),
        dot(x_ref[...], pair_ref[1], plain),
        dot(c_ref[...], down_ref[...], flipped),
    )
    act_ref[...] = activation
    grad_sum[...] += dot(gate_grad, pair_ref[0], flipped) + dot(up_grad, pair_ref[1], flipped)

    @pl.when(step == pl.num_programs(0) - 1)
    def _():
        grad_ref[...] = grad_sum[...].astype(low)


def both_ways(normed, upstream, after, pair, down):
    rows, width = normed.shape
    hidden = down.shape[0]
    tile = min(512, hidden)
    whole = pl.BlockSpec((rows, width), lambda i: (0, 0))
    return pl.pallas_call(
        both_ways_kernel,
        grid=(hidden // tile,),
        in_specs=[
            whole,
            pl.BlockSpec(upstream.shape, lambda i: (0, 0)),
            pl.BlockSpec(after.shape, lambda i: (0, 0)),
            pl.BlockSpec((2, width, tile), lambda i: (0, 0, i)),
            pl.BlockSpec((tile, width), lambda i: (i, 0)),
        ],
        out_specs=[pl.BlockSpec((rows, tile), lambda i: (0, i)), whole],
        out_shape=[
            jax.ShapeDtypeStruct((rows, hidden), low),
            jax.ShapeDtypeStruct((rows, width), low),
        ],
        scratch_shapes=[pltpu.VMEM((rows, width), full), pltpu.VMEM((rows, width), low)],
        compiler_params=params,
        cost_estimate=brief,
    )(normed, upstream, after, pair, down)


def copy_kernel(place_ref, from_ref, to_ref):
    to_ref[...] = from_ref[...]


def own_columns(pair, place, part, group):
    _, width, _ = pair.shape
    return pl.pallas_call(
        copy_kernel,
        grid_spec=pltpu.PrefetchScalarGridSpec(
            num_scalar_prefetch=1,
            grid=(2,),
            in_specs=[pl.BlockSpec((1, width, part), lambda k, p: (k, 0, 8 * group + p[0]))],
            out_specs=pl.BlockSpec((1, width, part), lambda k, p: (k, 0, 0)),
        ),
        out_shape=jax.ShapeDtypeStruct((2, width, part), low),
        compiler_params=params,
        cost_estimate=brief,
    )(place, pair)


def write_hidden(x, c, weights, hidden_ref):
    part = hidden_ref.shape[1] // 3
    for core, (gate_ref, up_ref, down_ref) in enumerate(weights):
        activation, gate_grad, up_grad = hidden_terms(
            dot(x, gate_ref[0], plain),
            dot(x, up_ref[0], plain),
            dot(c, down_ref[0], flipped),
        )
        for n, term in enumerate((gate_grad, up_grad, activation)):
            hidden_ref[core, n * part : (n + 1) * part] = term.T


def threes(refs):
    return [refs[start : start + 3] for start in range(0, len(refs), 3)]


def first_hidden_kernel(counts, spots, unit, *refs):
    pieces = refs[: counts[0]], refs[counts[0] : sum(counts)]
    *weights, hidden_ref, x_out, c_out, x_all, c_all, arrivals, leaving = refs[sum(counts) :]
    both = (x_all, x_out), (c_all, c_out)
    count = len(spots[0])
    block = hidden_ref.shape[2]
    together = block // unit
    step = pl.program_id(0)

    def coming(index):
        rows = pl.ds(index * unit, unit)
        copies = []
        for n in range(2):
            piece, start = spots[n][index]
            source = pieces[n][piece].at[pl.ds(start, unit)]
            copies.append(
                pltpu.make_async_copy(source, both[n][0].at[rows], arrivals.at[n, index])
            )
        return copies

    def going(index):
        rows = pl.ds(index * block, block)
        return [
            pltpu.make_async_copy(here.at[rows], there.at[rows], leaving.at[n, index])
            for n, (here, there) in enumerate(both)
        ]

    @pl.when(step == 0)
    def _():
        for index in range(count):
            for copy in coming(index):
                copy.start()

    for index in range(count // together):

        @pl.when(step == index)
        def _(index=index):
            for piece in range(index * together, (index + 1) * together):
                for copy in coming(piece):
                    copy.wait()
            for copy in going(index):
                copy.start()

    rows = pl.ds(step * block, block)
    write_hidden(x_all[rows], c_all[rows], threes(weights), hidden_ref)

    @pl.when(step == pl.num_programs(0) - 1)
    def _():
        for index in range(count // together):
            for copy in going(index):
                copy.wait()


def next_hidden_kernel(x_ref, c_ref, *refs):
    write_hidden(x_ref[...], c_ref[...], threes(refs[:-1]), refs[-1])


def weight_operands(pairs, downs, index):
    _, width, part = pairs[0].shape
    specs, arrays = [], []
    for pair, down in zip(pairs, downs):
        specs += [
            pl.BlockSpec((1, width, part), lambda i, k=k: (k, 0, 0)) for k in range(2)
        ]
        specs.append(pl.BlockSpec((1, part, width), lambda i: (index, 0, 0)))
        arrays += [pair, pair, down]
    return specs, arrays


def first_hidden(x_pieces, c_pieces, unit, pairs, downs):
    width = downs[0].shape[2]
    arrays, spots = [], []
    for row in (x_pieces, c_pieces):
        known = []
        for array, _ in row:
            if not any(array is other for other in known):
                known.append(array)
        arrays.append(known)
        spots.append(
            [
                (next(n for n, other in enumerate(known) if other is array), start)
                for array, start in row
            ]
        )
    counts = tuple(len(known) for known in arrays)
    count, own, cores = len(x_pieces), downs[0].shape[1], len(downs)
    block, rows = max(1, 384 // unit) * unit, count * unit
    anywhere = pl.BlockSpec(memory_space=pl.ANY)
    row_shape = jax.ShapeDtypeStruct((rows, width), low)
    specs, weights = weight_operands(pairs, downs, 0)
    return pl.pallas_call(
        functools.partial(first_hidden_kernel, counts, spots, unit),
        grid=(rows // block,),
        in_specs=[anywhere] * sum(counts) + specs,
        out_specs=[
            pl.BlockSpec((cores, 3 * own, block), lambda i: (0, 0, i)),
            anywhere,
            anywhere,
        ],
        scratch_shapes=[
            pltpu.VMEM((rows, width), low),
            pltpu.VMEM((rows, width), low),
            pltpu.SemaphoreType.DMA((2, count)),
            pltpu.SemaphoreType.DMA((2, rows // block)),
        ],
        out_shape=[
            jax.ShapeDtypeStruct((cores, 3 * own, rows), low),
            row_shape,
            row_shape,
        ],
        compiler_params=params,
        cost_estimate=brief,
    )(*arrays[0], *arrays[1], *weights)


def next_hidden(x_all, c_all, pairs, downs, index):
    rows, width = x_all.shape
    own, cores = downs[0].shape[1], len(downs)
    block = min(384, rows)
    tokens = pl.BlockSpec((block, width), lambda i: (i, 0))
    specs, weights = weight_operands(pairs, downs, index)
    return pl.pallas_call(
        next_hidden_kernel,
        grid=(rows // block,),
        in_specs=[tokens, tokens] + specs,
        out_specs=pl.BlockSpec((cores, 3 * own, block), lambda i: (0, 0, i)),
        out_shape=jax.ShapeDtypeStruct((cores, 3 * own, rows), low),
        compiler_params=params,
        cost_estimate=brief,
    )(x_all, c_all, *weights)


def weight_kernel(hidden_ref, x_ref, c_ref, *refs):
    arrived, out_ref = refs[:-1], refs[-1]
    two = 2 * hidden_ref.shape[1] // 3
    shard = out_ref.shape[2]
    pair = dot(hidden_ref[0, :two], x_ref[...], plain)
    single = dot(hidden_ref[0, two:], c_ref[...], plain)
    for j in range(out_ref.shape[0]):
        columns = slice(j * shard, (j + 1) * shard)
        for rows, term in ((slice(0, two), pair), (slice(two, None), single)):
            total = term[:, columns]
            for ref in arrived:
                total = total + ref[j, rows].astype(full)
            out_ref[j, rows] = total.astype(low)


def weight_terms(hidden, normed, upstream, shard, core, arrived=()):
    three, rows = hidden.shape[1:]
    width = normed.shape[1]
    tile = max(512, shard)
    columns = pl.BlockSpec((rows, tile), lambda i: (0, i))
    out_block = pl.BlockSpec((tile // shard, three, shard), lambda i: (i, 0, 0))
    return pl.pallas_call(
        weight_kernel,
        grid=(width // tile,),
        in_specs=[pl.BlockSpec((1, three, rows), lambda i: (core, 0, 0)), columns, columns]
        + [out_block] * len(arrived),
        out_specs=out_block,
        out_shape=jax.ShapeDtypeStruct((width // shard, three, shard), low),
        compiler_params=params,
        cost_estimate=brief,
    )(hidden, normed, upstream, *arrived)


def mixing_kernel(facts, x_ref, weight_ref, taps_ref, mixed_ref, kept_ref, line):
    seqs, length, gap = facts
    own, side = seqs * length, 2 * seqs
    x = x_ref[...]
    b_gate, c_gate, values = (dot(x, weight_ref[k], plain) for k in range(3))
    product = b_gate * values
    conv_out = [None] * (2 * seqs)
    for seq in range(seqs):
        before, after = own + side + 2 * seq, own + 2 * seq
        line[seq, 0:2] = product[before : before + 2]
        line[seq, 2 : length + 2] = product[seq * length : (seq + 1) * length]
        line[seq, length + 2 : length + 4] = product[after : after + 2]
        conv = sum(taps_ref[tap] * line[seq, tap : tap + length + 2] for tap in range(3))
        kept_ref[3, seq * length : (seq + 1) * length] = conv[:length]
        kept_ref[3, after : after + 2] = conv[length:]
    kept_ref[3, own + side :] = jnp.zeros_like(product[own + side :])
    kept_ref[0], kept_ref[1], kept_ref[2] = b_gate, c_gate, values
    mixed_ref[...] = (c_gate * kept_ref[3]).astype(low)


def mixing(normed, weight, taps, seqs, length):
    rows, width = normed.shape
    channels = weight.shape[2]
    tile = channels // 4
    return pl.pallas_call(
        functools.partial(mixing_kernel, (seqs, length, 0)),
        grid=(4,),
        in_specs=[
            pl.BlockSpec((rows, width), lambda i: (0, 0)),
            pl.BlockSpec((3, width, tile), lambda i: (0, 0, i)),
            pl.BlockSpec((3, tile), lambda i: (0, i)),
        ],
        out_specs=[
            pl.BlockSpec((rows, tile), lambda i: (0, i)),
            pl.BlockSpec((4, rows, tile), lambda i: (0, 0, i)),
        ],
        out_shape=[
            jax.ShapeDtypeStruct((rows, channels), low),
            jax.ShapeDtypeStruct((4, rows, channels), full),
        ],
        scratch_shapes=[pltpu.VMEM((seqs, length + 8, tile), full)],
        compiler_params=params,
        cost_estimate=brief,
    )(normed, weight, taps)


def unmixing_kernel(facts, spot_ref, grad_ref, weight_ref, kept_ref, taps_ref, *refs):
    *sent, sums_ref, line, past = refs
    seqs, length, deep, shard = facts
    own, side = seqs * length, 2 * seqs
    tile = weight_ref.shape[0]
    mixed_grad = dot(grad_ref[...], weight_ref[...], flipped)
    conv_grad = mixed_grad * kept_ref[1]
    blocks = []
    for seq in range(seqs):
        rows = slice(seq * length, (seq + 1) * length)
        before, after = own + side + 2 * seq, own + 2 * seq
        line[seq, 0:length] = conv_grad[rows]
        line[seq, length : length + 2] = conv_grad[after : after + 2]
        product_grad = sum(taps_ref[2 - tap] * line[seq, tap : tap + length] for tap in range(3))
        b_gate, values = kept_ref[0, rows], kept_ref[2, rows]
        grads = (product_grad * values, mixed_grad[rows] * kept_ref[3, rows], product_grad * b_gate)
        blocks.append((rows, [grad.astype(low) for grad in grads]))
        past[seq, 0:2] = kept_ref[0, before : before + 2] * kept_ref[2, before : before + 2]
        past[seq, 2 : length + 2] = b_gate * values
    for tap in range(3):
        sums_ref[tap : tap + 1] = sum(
            jnp.sum(line[seq, 0:length] * past[seq, tap : tap + length], axis=0, keepdims=True)
            for seq in range(seqs)
        )
    for mask, sent_ref in enumerate(sent):

        @pl.when(pl.program_id(0) == mask)
        def _(mask=mask, sent_ref=sent_ref):
            for rows, grads in blocks:
                for k, grad in enumerate(grads):
                    sent_ref[rows, k * tile : (k + 1) * tile] = grad
            for part in range(4):

                @pl.when(spot_ref[0] == part ^ mask)
                def _(part=part):
                    for far in range(deep):
                        start = (far * 4 + part) * shard
                        to = 3 * tile + far * shard
                        sent_ref[:, to : to + shard] = grad_ref[0:own, start : start + shard]


def unmixing(grad, weight, kept, taps, seqs, length, shard, spot):
    rows, width = grad.shape
    channels = weight.shape[0]
    tile, deep = channels // 4, width // (4 * shard)
    wide = 3 * tile + deep * shard
    block = pl.BlockSpec((seqs * length, wide), lambda i, p: (0, 0))
    return pl.pallas_call(
        functools.partial(unmixing_kernel, (seqs, length, deep, shard)),
        grid_spec=pltpu.PrefetchScalarGridSpec(
            num_scalar_prefetch=1,
            grid=(4,),
            in_specs=[
                pl.BlockSpec((rows, width), lambda i, p: (0, 0)),
                pl.BlockSpec((tile, width), lambda i, p: (i ^ p[0], 0)),
                pl.BlockSpec((4, rows, tile), lambda i, p: (0, 0, i ^ p[0])),
                pl.BlockSpec((3, tile), lambda i, p: (0, i ^ p[0])),
            ],
            out_specs=[block] * 4 + [pl.BlockSpec((3, tile), lambda i, p: (0, i ^ p[0]))],
            scratch_shapes=[pltpu.VMEM((seqs, length + 8, tile), full)] * 2,
        ),
        out_shape=[jax.ShapeDtypeStruct((seqs * length, wide), low)] * 4
        + [jax.ShapeDtypeStruct((3, channels), full)],
        compiler_params=params,
        cost_estimate=brief,
    )(spot, grad, weight, kept, taps)


def unprojected_kernel(spot_ref, *refs):
    *sent, weight_ref, out_ref, total = refs
    step = pl.program_id(0)
    tile = weight_ref.shape[2]
    for mask, sent_ref in enumerate(sent):

        @pl.when(step == mask)
        def _(mask=mask, sent_ref=sent_ref):
            term = sum(
                dot(sent_ref[:, k * tile : (k + 1) * tile], weight_ref[k], flipped)
                for k in range(3)
            )
            total[...] = term if mask == 0 else total[...] + term

    @pl.when(step == len(sent) - 1)
    def _():
        out_ref[...] = total[...].astype(low)


def unprojected(sent, weight, spot):
    rows = sent[0].shape[0]
    width, channels = weight.shape[1:]
    tile = channels // 4
    return pl.pallas_call(
        unprojected_kernel,
        grid_spec=pltpu.PrefetchScalarGridSpec(
            num_scalar_prefetch=1,
            grid=(4,),
            in_specs=[pl.BlockSpec((rows, 3 * tile), lambda i, p: (0, 0))] * 4
            + [pl.BlockSpec((3, width, tile), lambda i, p: (0, 0, i ^ p[0]))],
            out_specs=pl.BlockSpec((rows, width), lambda i, p: (0, 0)),
            scratch_shapes=[pltpu.VMEM((rows, width), full)],
        ),
        out_shape=jax.ShapeDtypeStruct((rows, width), low),
        compiler_params=params,
        cost_estimate=brief,
    )(spot, *sent, weight)


def in_terms_kernel(cores, facts_ref, *refs):
    sent, rights, (out_ref, gathered, turned_rows) = refs[:4], refs[4 : 4 + cores], refs[4 + cores :]
    chips, count, shard = out_ref.shape
    rows = sent[0].shape[0]
    share = rows // cores

    @pl.when(pl.program_id(0) == 0)
    def _():
        for index in range(cores):
            core = lax.rem(facts_ref[1] + cores - index, cores)
            start = pl.multiple_of(core * share, 16)
            for mask, ref in enumerate(sent):
                place = pl.multiple_of((facts_ref[0] ^ mask) * share, 16)
                gathered[pl.ds(place, share)] = ref[pl.ds(start, share), :]
            turned_rows[index] = gathered[...].T

    total = sum(
        dot(turned_rows[index], rights[index][...].reshape(chips * share, chips * shard), plain)
        for index in range(cores)
    )
    for j in range(chips):
        out_ref[j] = total[:, j * shard : (j + 1) * shard].astype(low)


def in_weight_terms(sent, count, rights, shard, spot):
    rows = sent[0].shape[0]
    cores = len(rights)
    chips, _, share, half = rights[0].shape
    tile = chips * shard
    tiles = half // tile
    facts = jnp.concatenate([spot, lax.axis_index("mp").astype(jnp.int32).reshape(1)])
    right = pl.BlockSpec((chips, 1, share, tile), lambda i, p: (0, i // tiles, 0, i % tiles))
    return pl.pallas_call(
        functools.partial(in_terms_kernel, cores),
        grid_spec=pltpu.PrefetchScalarGridSpec(
            num_scalar_prefetch=1,
            grid=(2 * tiles,),
            in_specs=[pl.BlockSpec((rows, count), lambda i, p: (0, 0))] * chips + [right] * cores,
            out_specs=pl.BlockSpec((chips, count, shard), lambda i, p: (i, 0, 0)),
            scratch_shapes=[
                pltpu.VMEM((chips * share, count), low),
                pltpu.VMEM((cores, count, chips * share), low),
            ],
        ),
        out_shape=jax.ShapeDtypeStruct((2 * tiles * chips, count, shard), low),
        compiler_params=params,
        cost_estimate=brief,
    )(facts, *sent, *rights)


def out_terms_kernel(facts_ref, *refs):
    *sent, mixed_ref, out_ref, columns = refs
    chips, rows, channels = mixed_ref.shape
    shard = out_ref.shape[2]
    deep = out_ref.shape[0]
    first = sent[0].shape[1] - deep * shard
    for mask, ref in enumerate(sent):
        place = pl.multiple_of((facts_ref[0] ^ mask) * rows, 16)
        columns[pl.ds(place, rows)] = ref[:, first:]
    total = dot(mixed_ref[...].reshape(chips * rows, channels).T, columns[...], plain)
    for far in range(deep):
        out_ref[far] = total[:, far * shard : (far + 1) * shard].astype(low)


def out_weight_terms(sent, count, shown, channels, shard, spot):
    rows, wide = sent[0].shape
    chips = shown.shape[0]
    deep = (wide - count) // shard
    return pl.pallas_call(
        out_terms_kernel,
        grid_spec=pltpu.PrefetchScalarGridSpec(
            num_scalar_prefetch=1,
            grid=(1,),
            in_specs=[pl.BlockSpec((rows, wide), lambda i, p: (0, 0))] * chips
            + [pl.BlockSpec((chips, rows, channels), lambda i, p: (0, 0, 0))],
            out_specs=pl.BlockSpec((deep, channels, shard), lambda i, p: (0, 0, 0)),
            scratch_shapes=[pltpu.VMEM((chips * rows, deep * shard), low)],
        ),
        out_shape=jax.ShapeDtypeStruct((deep, channels, shard), low),
        compiler_params=params,
        cost_estimate=brief,
    )(spot, *sent, shown)


def placing_kernel(parts, *refs):
    placed_ref, pair_ref, down_ref = refs[0], refs[-2], refs[-1]
    chips, three, _ = placed_ref.shape
    chips //= parts
    own = three // 3
    for chip in range(chips):
        block = sum(placed_ref[part * chips + chip].astype(full) for part in range(parts))
        rows = slice(chip * own, (chip + 1) * own)
        pair_ref[:, 0, rows] = block[:own].T
        pair_ref[:, 1, rows] = block[own : 2 * own].T
        down_ref[rows] = block[2 * own :]


def put_in_place(placed, parts, index, groups, before):
    chips, three, shard = placed.shape
    columns = chips // parts * three // 3
    return pl.pallas_call(
        functools.partial(placing_kernel, parts),
        grid=(1,),
        in_specs=[pl.BlockSpec(placed.shape, lambda i: (0, 0, 0))]
        + [pl.BlockSpec(memory_space=pl.ANY)] * len(before),
        out_specs=[
            pl.BlockSpec((shard, 2, columns), lambda i: (0, 0, index)),
            pl.BlockSpec((columns, shard), lambda i: (index, 0)),
        ],
        out_shape=[
            jax.ShapeDtypeStruct((shard, 2, groups * columns), full),
            jax.ShapeDtypeStruct((groups * columns, shard), full),
        ],
        input_output_aliases={1 + n: n for n in range(len(before))},
        compiler_params=params,
        cost_estimate=brief,
    )(placed, *before)


def product_kernel(left_ref, right_ref, out_ref, total):
    step = pl.program_id(0)
    term = dot(left_ref[...], right_ref[...], plain)

    @pl.when(step == 0)
    def _():
        total[...] = term

    @pl.when(step > 0)
    def _():
        total[...] += term

    @pl.when(step == pl.num_programs(0) - 1)
    def _():
        out_ref[...] = total[...].astype(low)


def product_of(left, right):
    rows, depth = left.shape
    width = right.shape[1]
    tile = min(1024, depth)
    return pl.pallas_call(
        product_kernel,
        grid=(depth // tile,),
        in_specs=[
            pl.BlockSpec((rows, tile), lambda i: (0, i)),
            pl.BlockSpec((tile, width), lambda i: (i, 0)),
        ],
        out_specs=pl.BlockSpec((rows, width), lambda i: (0, 0)),
        out_shape=jax.ShapeDtypeStruct((rows, width), low),
        scratch_shapes=[pltpu.VMEM((rows, width), full)],
        compiler_params=params,
        cost_estimate=brief,
    )(left, right)


def tokens_grad_kernel(core_ref, values_ref, inv_ref, gain_ref, inner_ref, *refs):
    parts, (out_ref, sums_ref) = refs[:-2], refs[-2:]
    upstream = sum(ref[...].astype(full) for ref in parts)
    scaled = values_ref[...] * inv_ref[...]
    weighted = upstream * gain_ref[...]
    inner_mean = jnp.mean(weighted * scaled, axis=-1, keepdims=True)
    out_ref[...] = (inner_ref[...] + inv_ref[...] * (weighted - scaled * inner_mean)).astype(low)

    @pl.when(pl.program_id(0) == core_ref[0])
    def _():
        sums_ref[...] = jnp.sum(upstream * scaled, axis=0, keepdims=True)


def tokens_grad_of(values, inv_rms, gain_vec, inner_grad, parts, rows, cores):
    width = values.shape[1]
    share = rows // cores
    core = lax.axis_index("mp").astype(jnp.int32).reshape(1)
    block = pl.BlockSpec((share, width), lambda i, p: (i, 0))
    line = pl.BlockSpec((1, width), lambda i, p: (0, 0))
    return pl.pallas_call(
        tokens_grad_kernel,
        grid_spec=pltpu.PrefetchScalarGridSpec(
            num_scalar_prefetch=1,
            grid=(cores,),
            in_specs=[block, pl.BlockSpec((share, 1), lambda i, p: (i, 0)), line, block]
            + [block] * len(parts),
            out_specs=[block, line],
        ),
        out_shape=[
            jax.ShapeDtypeStruct((rows, width), low),
            jax.ShapeDtypeStruct((1, width), full),
        ],
        compiler_params=params,
        cost_estimate=brief,
    )(core, values, inv_rms, gain_vec.reshape(1, -1), inner_grad, *parts)


def local(
    tokens,
    norm1_gain,
    in_weight,
    conv_weight,
    out_weight,
    norm2_gain,
    gate_up,
    down_weight,
    cotangent,
):
    seq_count, local_len, width = tokens.shape
    row_total = seq_count * local_len
    channels = in_weight.shape[2]
    hidden = gate_up.shape[2]
    parts = lax.axis_size("a")
    cores = lax.axis_size("mp")
    shard = width // (parts * 8)
    deep = width // (4 * shard)
    quarter = channels // 4
    cube, plane, column = ("b", "c", "d"), ("c", "d"), ("a", "b")
    place = lax.axis_index(cube).astype(jnp.int32).reshape(1)
    own = hidden // 8
    in_parts = jnp.transpose(in_weight, (1, 0, 2))

    after = passed_along(
        jnp.stack([tokens[:, :2], cotangent[:, :2]]), column + plane, -1
    ).reshape(2, -1, width)
    before = passed_along(tokens[:, local_len - 2 :], column + plane, 1).reshape(-1, width)
    side = before.shape[0]
    padding = jnp.zeros((2 * side + (-2 * side) % 16, width), low)
    before, upstream_mine = tied(before, share_of(cotangent.reshape(row_total, width)))
    inputs = jnp.concatenate(
        [tokens.reshape(row_total, width), after[0], before, padding[2 * side :]]
    ).astype(full)
    upstream_own = cotangent.reshape(row_total, width)
    upstream_after = jnp.concatenate([after[1], padding[side:]])
    upstream_grad = jnp.concatenate([upstream_own, upstream_after]).astype(full)
    normed_full_one, inv_rms_one = normalize(inputs, norm1_gain)
    normed_one = normed_full_one.astype(low)
    upstream_opposite = opposite(upstream_mine)
    mixed, mixer_state = mixing(normed_one, in_parts, conv_weight, seq_count, local_len)
    mixed, upstream_opposite = tied(mixed, upstream_opposite)
    inner_sum = inputs + summed(dot(mixed, out_weight, plain))
    normed_full_two, inv_rms_two = normalize(inner_sum, norm2_gain)
    normed_two = normed_full_two.astype(low)

    groups = 2 if own > 256 else 1
    half_width = width // 2
    part = own // groups
    unit = row_total // cores
    normed_mine = share_of(normed_two[:row_total])
    together = in_rows([normed_mine, upstream_mine], [(0, 1)])[0]
    from_near = near(together)
    firsts = [(index * 8 + place[0]) * part for index in range(groups)]
    down_own = jnp.stack(
        [lax.dynamic_slice_in_dim(down_weight, first, part, 0) for first in firsts]
    )
    downs = [down_own] + others(down_own, "mp")
    gate_up, together = tied(gate_up, together)
    pair_weight = lax.optimization_barrier(jnp.transpose(gate_up, (1, 0, 2)))
    pair_weight, normed_mine, *arrived = tied(
        pair_weight, normed_mine, *from_near, *downs[1:]
    )
    from_near, downs[1:] = arrived[:3], arrived[3:]
    from_beyond = beyond(from_near, "cdb")
    normed_opposite = opposite(normed_mine)
    pairs = [own_columns(pair_weight, place, part, 0)]
    pairs[0] = [pairs[0]] + others(pairs[0], "mp")
    pair_weight, pairs[0][0] = tied(pair_weight, pairs[0][0])
    activation, normed_two_part = both_ways(
        normed_two, upstream_own, upstream_after, pair_weight, down_weight
    )
    activation, normed_two_part, normed_opposite, *arrived = tied(
        activation, normed_two_part, normed_opposite, *from_beyond, *pairs[0][1:]
    )
    from_beyond, pairs[0][1:] = arrived[:3], arrived[3:]
    latest = []

    def in_turn(*values):
        values = tied(*values, *latest)[: len(values)]
        return values if len(values) > 1 else values[0]

    def over(*values):
        latest[:] = values

    over(normed_two_part, activation)
    normed_one, mixed = in_turn(normed_one, mixed)
    one_mine = share_of(normed_one[:row_total])
    shown = jnp.stack([one_mine[:, :half_width], one_mine[:, half_width:]])
    spare = ((0, 0), (0, half_width - channels))
    shown = jnp.concatenate([jnp.pad(mixed[:row_total], spare), shown.reshape(-1, half_width)])
    shown = lax.all_gather(in_turn(shown), plane)
    normed_two_grad = summed(normed_two_part)

    gathered = [together] + from_near + from_beyond
    hidden_rows, normed_all, upstream_all = first_hidden(
        [(rows, 0) for rows in gathered] + [(normed_opposite, 0)],
        [(rows, unit) for rows in gathered] + [(upstream_opposite, 0)],
        unit,
        [in_turn(pairs[0][0])] + pairs[0][1:],
        downs,
    )
    def of_others(rows):
        blocks = []
        for core in range(1, cores):
            blocks.append(weight_terms(in_turn(rows), normed_all, upstream_all, shard, core))
            over(blocks[-1])
        return [turned(block, "mp", -core - 1) for core, block in enumerate(blocks)]

    def of_mine(rows, received):
        block = weight_terms(in_turn(rows), normed_all, upstream_all, shard, 0, received)
        over(block)
        return block

    over(hidden_rows)
    if groups > 1:
        next_pair = own_columns(in_turn(pair_weight), place, part, 1)
        over(next_pair)
        pairs.append([next_pair] + others(next_pair, "mp"))
    received = of_others(hidden_rows)
    normed_two_grad = in_turn(normed_two_grad)
    inner_grad = upstream_grad + norm_back(inner_sum, inv_rms_two, norm2_gain, normed_two_grad)
    branch_grad = inner_grad.astype(low)
    over(branch_grad)
    block = of_mine(hidden_rows, received)
    placed = shared_out(block, column + plane)
    if groups > 1:
        next_rows = next_hidden(in_turn(normed_all), upstream_all, pairs[1], downs, 1)
        over(next_rows)
        received = of_others(next_rows)
    spot = lax.axis_index(plane).astype(jnp.int32).reshape(1)
    *sent, taps_grad = unmixing(
        in_turn(branch_grad), out_weight, mixer_state, conv_weight, seq_count, local_len, shard, spot
    )
    over(*sent)
    seen = [sent[0], swapped(in_turn(sent[1]), "d"), swapped(in_turn(sent[2]), "c")]
    if groups > 1:
        next_block = of_mine(next_rows, received)
    over(*latest, *seen, shown, placed)
    if groups > 1:
        next_placed = shared_out(in_turn(next_block), column + plane)
    one_all = [in_turn(shown)[:, row_total:].reshape(4, 2, unit, half_width)]
    one_all += others(one_all[0], "mp")
    seen.append(lax.ppermute(in_turn(sent[3]), plane, [(i, 3 - i) for i in range(4)]))
    normed_one_part = unprojected([in_turn(sent[0])] + sent[1:], in_parts, spot)
    over(normed_one_part, *one_all[1:], seen[3])
    seen[0] = in_turn(seen[0])
    in_terms = in_weight_terms(seen, 3 * quarter, one_all, shard, spot)
    over(in_terms)
    if groups > 1:
        over(in_terms, next_placed)
    in_total = shared_out(in_turn(in_terms), column + plane)
    out_terms = out_weight_terms(
        [in_turn(seen[0])] + seen[1:], 3 * quarter, shown, channels, shard, spot
    )
    over(out_terms)
    out_total = lax.psum_scatter(out_terms, column, scatter_dimension=0).astype(full)
    totals = put_in_place(placed, parts, 0, groups, ())
    if groups > 1:
        totals = put_in_place(next_placed, parts, 1, groups, totals)
    gate_up_total, down_total = totals
    parts_one = both_parts(in_turn(normed_one_part))
    tokens_grad, gain_one = tokens_grad_of(
        inputs, inv_rms_one, norm1_gain, inner_grad, parts_one, row_total, cores
    )
    gain_two = jnp.sum(
        share_of((normed_two_grad * inner_sum * inv_rms_two)[:row_total]), axis=0
    )
    channel_start = lax.axis_index("mp") * channels
    taps_full = lax.dynamic_update_slice_in_dim(
        jnp.zeros((3, width), full), taps_grad, channel_start, 1
    )
    small = jnp.concatenate([gain_one, gain_two[None], taps_full], axis=0)
    for axes in (("mp",), plane, column):
        if lax.axis_size(axes) <= 4:
            small = over_all(small, axes)
        else:
            small = lax.psum(small, axes)
    output_part = product_of(in_turn(activation), down_weight)
    output = (inner_sum + summed(output_part))[:row_total].astype(low)
    in_total = (
        jnp.sum(in_total.astype(full).reshape(-1, 4, 3, quarter, shard), axis=0)
        .transpose(3, 1, 0, 2)
        .reshape(shard, 3, channels)
    )
    taps_total = lax.dynamic_slice_in_dim(small[2:], channel_start, channels, 1)
    return (
        output.reshape(seq_count, local_len, width),
        tokens_grad.reshape(seq_count, local_len, width),
        small[0],
        in_total,
        taps_total,
        out_total,
        small[1],
        gate_up_total,
        down_total,
    )


def solution(mesh):
    seq, mp = mesh.shape["seq"], mesh.shape["mp"]
    fine = Mesh(mesh.devices.reshape(seq // 8, 2, 2, 2, mp), ("a", "b", "c", "d", "mp"))
    by_seq = ("a", "b", "c", "d")
    return jax.shard_map(
        local,
        mesh=fine,
        in_specs=(
            P(None, by_seq, None),
            P(),
            P(None, None, "mp"),
            P(None, "mp"),
            P("mp", None),
            P(),
            P(None, None, "mp"),
            P("mp", None),
            P(None, by_seq, None),
        ),
        out_specs=(
            P(None, by_seq, None),
            P(None, by_seq, None),
            P(),
            P(by_seq, None, "mp"),
            P(None, "mp"),
            P("mp", by_seq),
            P(),
            P(by_seq, None, "mp"),
            P("mp", by_seq),
        ),
        check_vma=False,
    )
```

```python
import functools

import jax
import jax.numpy as jnp
from jax import lax
from jax.experimental import pallas as pl
from jax.experimental.pallas import tpu as pltpu
from jax.sharding import Mesh, PartitionSpec as P

epsilon = 1e-05
low = jnp.bfloat16
full = jnp.float32
plain = ((1,), (0,))
flipped = ((1,), (1,))
params = pltpu.CompilerParams(vmem_limit_bytes=56 * 2**20)


brief = pl.CostEstimate(flops=1000, bytes_accessed=1000, transcendentals=0)


def swapped(block, axis):
    return lax.ppermute(block, axis, [(0, 1), (1, 0)])


def passed_along(block, axis, distance):
    devices = range(lax.axis_size(axis))
    route = [(i - distance, i) for i in devices if i - distance in devices]
    return lax.ppermute(block, axis, route)


def turned(block, axis, distance):
    count = lax.axis_size(axis)
    return lax.ppermute(block, axis, [(i, (i + distance) % count) for i in range(count)])


def others(block, axis):
    return [turned(block, axis, step) for step in range(1, lax.axis_size(axis))]


def both_parts(partial):
    if lax.axis_size("mp") == 2:
        return [partial, swapped(partial, "mp")]
    return [lax.psum(partial, "mp")]


def summed(partial):
    return sum(part.astype(full) for part in both_parts(partial.astype(low)))


def over_all(values, axes):
    count = lax.axis_size(axes)
    near_by, *rest = [
        lax.ppermute(values, axes, [(i, i ^ mask) for i in range(count)]) for mask in range(1, count)
    ]
    total = values + near_by
    return total + (rest[0] + rest[1]) if rest else total


def share_of(rows):
    count = rows.shape[0] // lax.axis_size("mp")
    return lax.dynamic_slice_in_dim(rows, lax.axis_index("mp") * count, count, 0)


def tied(*values):
    return lax.optimization_barrier(values)


def near(mine):
    return [swapped(mine, axis) for axis in "bcd"]


def beyond(from_near, axes="cdb"):
    return [swapped(piece, axis) for piece, axis in zip(from_near, axes)]


def opposite(mine):
    return lax.ppermute(mine, ("b", "c", "d"), [(i, 7 - i) for i in range(8)])


def row_kernel(makings, *refs):
    for place, making in enumerate(makings):
        out_ref, row = refs[len(refs) - len(makings) + place], 0
        for part in making:
            index, start, rows = part if isinstance(part, tuple) else (part, 0, None)
            rows = refs[index].shape[0] if rows is None else rows
            out_ref[row : row + rows] = refs[index][start : start + rows]
            row += rows


def in_rows(arrays, makings):
    width = arrays[0].shape[1]

    def rows(making):
        return sum(
            part[2] if isinstance(part, tuple) else arrays[part].shape[0] for part in making
        )

    whole = pl.BlockSpec(memory_space=pltpu.VMEM)
    return pl.pallas_call(
        functools.partial(row_kernel, makings),
        in_specs=[whole] * len(arrays),
        out_specs=[whole] * len(makings),
        out_shape=[jax.ShapeDtypeStruct((rows(making), width), low) for making in makings],
        compiler_params=params,
        cost_estimate=brief,
    )(*arrays)


def shared_out(blocks, axes):
    return lax.all_to_all(blocks, axes, 0, 0, tiled=True)


def shown_to_all(mine, axes):
    return shared_out(jnp.broadcast_to(mine, (lax.axis_size(axes),) + mine.shape), axes)


def normalize(values, gain_vec):
    inv_rms = lax.rsqrt(jnp.mean(values * values, axis=-1, keepdims=True) + epsilon)
    return (values * inv_rms * gain_vec, inv_rms)


def norm_back(values, inv_rms, gain_vec, upstream):
    scaled = values * inv_rms
    weighted = upstream * gain_vec
    inner_mean = jnp.mean(weighted * scaled, axis=-1, keepdims=True)
    return inv_rms * (weighted - scaled * inner_mean)


def dot(left, right, dims):
    return lax.dot_general(left, right, (dims, ((), ())), preferred_element_type=full)


def hidden_terms(gate_pre, up_pre, activation_grad):
    sigmoid_gate = jax.nn.sigmoid(gate_pre)
    swish_gate = gate_pre * sigmoid_gate
    gate_grad = activation_grad * up_pre * sigmoid_gate * (1.0 + gate_pre * (1.0 - sigmoid_gate))
    return (
        (swish_gate * up_pre).astype(low),
        gate_grad.astype(low),
        (activation_grad * swish_gate).astype(low),
    )


def both_ways_kernel(
    x_ref, own_ref, after_ref, pair_ref, down_ref, act_ref, grad_ref, grad_sum, c_ref
):
    step = pl.program_id(0)
    own = own_ref.shape[0]

    @pl.when(step == 0)
    def _():
        grad_sum[...] = jnp.zeros_like(grad_sum)
        c_ref[:own] = own_ref[...]
        c_ref[own:] = after_ref[...]

    activation, gate_grad, up_grad = hidden_terms(
        dot(x_ref[...], pair_ref[0], plain),
        dot(x_ref[...], pair_ref[1], plain),
        dot(c_ref[...], down_ref[...], flipped),
    )
    act_ref[...] = activation
    grad_sum[...] += dot(gate_grad, pair_ref[0], flipped) + dot(up_grad, pair_ref[1], flipped)

    @pl.when(step == pl.num_programs(0) - 1)
    def _():
        grad_ref[...] = grad_sum[...].astype(low)


def both_ways(normed, upstream, after, pair, down):
    rows, width = normed.shape
    hidden = down.shape[0]
    tile = min(512, hidden)
    whole = pl.BlockSpec((rows, width), lambda i: (0, 0))
    return pl.pallas_call(
        both_ways_kernel,
        grid=(hidden // tile,),
        in_specs=[
            whole,
            pl.BlockSpec(upstream.shape, lambda i: (0, 0)),
            pl.BlockSpec(after.shape, lambda i: (0, 0)),
            pl.BlockSpec((2, width, tile), lambda i: (0, 0, i)),
            pl.BlockSpec((tile, width), lambda i: (i, 0)),
        ],
        out_specs=[pl.BlockSpec((rows, tile), lambda i: (0, i)), whole],
        out_shape=[
            jax.ShapeDtypeStruct((rows, hidden), low),
            jax.ShapeDtypeStruct((rows, width), low),
        ],
        scratch_shapes=[pltpu.VMEM((rows, width), full), pltpu.VMEM((rows, width), low)],
        compiler_params=params,
        cost_estimate=brief,
    )(normed, upstream, after, pair, down)


def copy_kernel(place_ref, from_ref, to_ref):
    to_ref[...] = from_ref[...]


def own_columns(pair, place, part, group):
    _, width, _ = pair.shape
    return pl.pallas_call(
        copy_kernel,
        grid_spec=pltpu.PrefetchScalarGridSpec(
            num_scalar_prefetch=1,
            grid=(2,),
            in_specs=[pl.BlockSpec((1, width, part), lambda k, p: (k, 0, 8 * group + p[0]))],
            out_specs=pl.BlockSpec((1, width, part), lambda k, p: (k, 0, 0)),
        ),
        out_shape=jax.ShapeDtypeStruct((2, width, part), low),
        compiler_params=params,
        cost_estimate=brief,
    )(place, pair)


def write_terms(hidden, x, c, arrived, out_ref):
    two = 2 * hidden.shape[0] // 3
    shard = out_ref.shape[2]
    pair = dot(hidden[:two], x, plain)
    single = dot(hidden[two:], c, plain)
    for j in range(out_ref.shape[0]):
        columns = slice(j * shard, (j + 1) * shard)
        for rows, term in ((slice(0, two), pair), (slice(two, None), single)):
            total = term[:, columns]
            for ref in arrived:
                total = total + ref[j, rows].astype(full)
            out_ref[j, rows] = total.astype(low)


def write_hidden(x, c, weights, place):
    for core, (gate_ref, up_ref, down_ref) in enumerate(weights):
        part = down_ref.shape[1]
        activation, gate_grad, up_grad = hidden_terms(
            dot(x, gate_ref[0], plain),
            dot(x, up_ref[0], plain),
            dot(c, down_ref[0], flipped),
        )
        for n, term in enumerate((gate_grad, up_grad, activation)):
            place(core, slice(n * part, (n + 1) * part), term.T)


def threes(refs):
    return [refs[start : start + 3] for start in range(0, len(refs), 3)]


def first_hidden_kernel(counts, spots, unit, cores, *refs):
    pieces = refs[: counts[0]], refs[counts[0] : sum(counts)]
    refs = refs[sum(counts) :]
    weights, refs = refs[: 3 * cores], refs[3 * cores :]
    hidden_ref, x_out, c_out = refs[:3]
    terms, (x_all, c_all, other_rows, arrivals, leaving) = refs[3:-5], refs[-5:]
    both = (x_all, x_out), (c_all, c_out)
    count = len(spots[0])
    block = hidden_ref.shape[2]
    together = block // unit
    step = pl.program_id(0)

    def coming(index):
        rows = pl.ds(index * unit, unit)
        copies = []
        for n in range(2):
            piece, start = spots[n][index]
            source = pieces[n][piece].at[pl.ds(start, unit)]
            copies.append(
                pltpu.make_async_copy(source, both[n][0].at[rows], arrivals.at[n, index])
            )
        return copies

    def going(index):
        rows = pl.ds(index * block, block)
        return [
            pltpu.make_async_copy(here.at[rows], there.at[rows], leaving.at[n, index])
            for n, (here, there) in enumerate(both)
        ]

    @pl.when(step == 0)
    def _():
        for index in range(count):
            for copy in coming(index):
                copy.start()

    for index in range(count // together):

        @pl.when(step == index)
        def _(index=index):
            for piece in range(index * together, (index + 1) * together):
                for copy in coming(piece):
                    copy.wait()
            for copy in going(index):
                copy.start()

    rows = pl.ds(pl.multiple_of(step * block, block), block)

    def place(core, span, value):
        if core == 0:
            hidden_ref[0, span] = value
        else:
            other_rows[core - 1, span, rows] = value

    write_hidden(x_all[rows], c_all[rows], threes(weights), place)

    @pl.when(step == pl.num_programs(0) - 1)
    def _():
        width, wide = x_all.shape[1], 512
        for core, out_ref in enumerate(terms):
            shard = out_ref.shape[2]
            for start in range(0, width, wide):
                columns = slice(start, start + wide)
                write_terms(
                    other_rows[core],
                    x_all[:, columns],
                    c_all[:, columns],
                    (),
                    out_ref.at[pl.ds(start // shard, wide // shard)],
                )
        for index in range(count // together):
            for copy in going(index):
                copy.wait()


def next_hidden_kernel(x_ref, c_ref, *refs):
    def place(core, span, value):
        refs[-1][core, span] = value

    write_hidden(x_ref[...], c_ref[...], threes(refs[:-1]), place)


def weight_operands(pairs, downs, index):
    _, width, part = pairs[0].shape
    specs, arrays = [], []
    for pair, down in zip(pairs, downs):
        specs += [
            pl.BlockSpec((1, width, part), lambda i, k=k: (k, 0, 0)) for k in range(2)
        ]
        specs.append(pl.BlockSpec((1, part, width), lambda i: (index, 0, 0)))
        arrays += [pair, pair, down]
    return specs, arrays


def first_hidden(x_pieces, c_pieces, unit, pairs, downs, shard):
    width = downs[0].shape[2]
    arrays, spots = [], []
    for row in (x_pieces, c_pieces):
        known = []
        for array, _ in row:
            if not any(array is other for other in known):
                known.append(array)
        arrays.append(known)
        spots.append(
            [
                (next(n for n, other in enumerate(known) if other is array), start)
                for array, start in row
            ]
        )
    counts = tuple(len(known) for known in arrays)
    count, own, cores = len(x_pieces), downs[0].shape[1], len(downs)
    block, rows = max(1, 384 // unit) * unit, count * unit
    anywhere = pl.BlockSpec(memory_space=pl.ANY)
    row_shape = jax.ShapeDtypeStruct((rows, width), low)
    specs, weights = weight_operands(pairs, downs, 0)
    terms_shape = jax.ShapeDtypeStruct((width // shard, 3 * own, shard), low)
    return pl.pallas_call(
        functools.partial(first_hidden_kernel, counts, spots, unit, cores),
        grid=(rows // block,),
        in_specs=[anywhere] * sum(counts) + specs,
        out_specs=[
            pl.BlockSpec((1, 3 * own, block), lambda i: (0, 0, i)),
            anywhere,
            anywhere,
        ]
        + [pl.BlockSpec(terms_shape.shape, lambda i: (0, 0, 0))] * (cores - 1),
        scratch_shapes=[
            pltpu.VMEM((rows, width), low),
            pltpu.VMEM((rows, width), low),
            pltpu.VMEM((cores - 1, 3 * own, rows), low),
            pltpu.SemaphoreType.DMA((2, count)),
            pltpu.SemaphoreType.DMA((2, rows // block)),
        ],
        out_shape=[
            jax.ShapeDtypeStruct((1, 3 * own, rows), low),
            row_shape,
            row_shape,
        ]
        + [terms_shape] * (cores - 1),
        compiler_params=params,
        cost_estimate=brief,
    )(*arrays[0], *arrays[1], *weights)


def next_hidden(x_all, c_all, pairs, downs, index):
    rows, width = x_all.shape
    own, cores = downs[0].shape[1], len(downs)
    block = min(384, rows)
    tokens = pl.BlockSpec((block, width), lambda i: (i, 0))
    specs, weights = weight_operands(pairs, downs, index)
    return pl.pallas_call(
        next_hidden_kernel,
        grid=(rows // block,),
        in_specs=[tokens, tokens] + specs,
        out_specs=pl.BlockSpec((cores, 3 * own, block), lambda i: (0, 0, i)),
        out_shape=jax.ShapeDtypeStruct((cores, 3 * own, rows), low),
        compiler_params=params,
        cost_estimate=brief,
    )(x_all, c_all, *weights)


def weight_kernel(hidden_ref, x_ref, c_ref, *refs):
    write_terms(hidden_ref[0], x_ref[...], c_ref[...], refs[:-1], refs[-1])


def weight_terms(hidden, normed, upstream, shard, core, arrived=()):
    three, rows = hidden.shape[1:]
    width = normed.shape[1]
    tile = max(512, shard)
    columns = pl.BlockSpec((rows, tile), lambda i: (0, i))
    out_block = pl.BlockSpec((tile // shard, three, shard), lambda i: (i, 0, 0))
    return pl.pallas_call(
        weight_kernel,
        grid=(width // tile,),
        in_specs=[pl.BlockSpec((1, three, rows), lambda i: (core, 0, 0)), columns, columns]
        + [out_block] * len(arrived),
        out_specs=out_block,
        out_shape=jax.ShapeDtypeStruct((width // shard, three, shard), low),
        compiler_params=params,
        cost_estimate=brief,
    )(hidden, normed, upstream, *arrived)


def mixing_kernel(facts, x_ref, weight_ref, taps_ref, mixed_ref, kept_ref, line):
    seqs, length, gap = facts
    own, side = seqs * length, 2 * seqs
    x = x_ref[...]
    b_gate, c_gate, values = (dot(x, weight_ref[k], plain) for k in range(3))
    product = b_gate * values
    conv_out = [None] * (2 * seqs)
    for seq in range(seqs):
        before, after = own + side + 2 * seq, own + 2 * seq
        line[seq, 0:2] = product[before : before + 2]
        line[seq, 2 : length + 2] = product[seq * length : (seq + 1) * length]
        line[seq, length + 2 : length + 4] = product[after : after + 2]
        conv = sum(taps_ref[tap] * line[seq, tap : tap + length + 2] for tap in range(3))
        kept_ref[3, seq * length : (seq + 1) * length] = conv[:length]
        kept_ref[3, after : after + 2] = conv[length:]
    kept_ref[3, own + side :] = jnp.zeros_like(product[own + side :])
    kept_ref[0], kept_ref[1], kept_ref[2] = b_gate, c_gate, values
    mixed_ref[...] = (c_gate * kept_ref[3]).astype(low)


def mixing(normed, weight, taps, seqs, length):
    rows, width = normed.shape
    channels = weight.shape[2]
    tile = channels // 4
    return pl.pallas_call(
        functools.partial(mixing_kernel, (seqs, length, 0)),
        grid=(4,),
        in_specs=[
            pl.BlockSpec((rows, width), lambda i: (0, 0)),
            pl.BlockSpec((3, width, tile), lambda i: (0, 0, i)),
            pl.BlockSpec((3, tile), lambda i: (0, i)),
        ],
        out_specs=[
            pl.BlockSpec((rows, tile), lambda i: (0, i)),
            pl.BlockSpec((4, rows, tile), lambda i: (0, 0, i)),
        ],
        out_shape=[
            jax.ShapeDtypeStruct((rows, channels), low),
            jax.ShapeDtypeStruct((4, rows, channels), full),
        ],
        scratch_shapes=[pltpu.VMEM((seqs, length + 8, tile), full)],
        compiler_params=params,
        cost_estimate=brief,
    )(normed, weight, taps)


def unmixing_kernel(facts, spot_ref, grad_ref, weight_ref, kept_ref, taps_ref, *refs):
    *sent, sums_ref, line, past = refs
    seqs, length, deep, shard = facts
    own, side = seqs * length, 2 * seqs
    tile = weight_ref.shape[0]
    mixed_grad = dot(grad_ref[...], weight_ref[...], flipped)
    conv_grad = mixed_grad * kept_ref[1]
    blocks = []
    for seq in range(seqs):
        rows = slice(seq * length, (seq + 1) * length)
        before, after = own + side + 2 * seq, own + 2 * seq
        line[seq, 0:length] = conv_grad[rows]
        line[seq, length : length + 2] = conv_grad[after : after + 2]
        product_grad = sum(taps_ref[2 - tap] * line[seq, tap : tap + length] for tap in range(3))
        b_gate, values = kept_ref[0, rows], kept_ref[2, rows]
        grads = (product_grad * values, mixed_grad[rows] * kept_ref[3, rows], product_grad * b_gate)
        blocks.append((rows, [grad.astype(low) for grad in grads]))
        past[seq, 0:2] = kept_ref[0, before : before + 2] * kept_ref[2, before : before + 2]
        past[seq, 2 : length + 2] = b_gate * values
    for tap in range(3):
        sums_ref[tap : tap + 1] = sum(
            jnp.sum(line[seq, 0:length] * past[seq, tap : tap + length], axis=0, keepdims=True)
            for seq in range(seqs)
        )
    for mask, sent_ref in enumerate(sent):

        @pl.when(pl.program_id(0) == mask)
        def _(mask=mask, sent_ref=sent_ref):
            for rows, grads in blocks:
                for k, grad in enumerate(grads):
                    sent_ref[rows, k * tile : (k + 1) * tile] = grad
            for part in range(4):

                @pl.when(spot_ref[0] == part ^ mask)
                def _(part=part):
                    for far in range(deep):
                        start = (far * 4 + part) * shard
                        to = 3 * tile + far * shard
                        sent_ref[:, to : to + shard] = grad_ref[0:own, start : start + shard]


def unmixing(grad, weight, kept, taps, seqs, length, shard, spot):
    rows, width = grad.shape
    channels = weight.shape[0]
    tile, deep = channels // 4, width // (4 * shard)
    wide = 3 * tile + deep * shard
    block = pl.BlockSpec((seqs * length, wide), lambda i, p: (0, 0))
    return pl.pallas_call(
        functools.partial(unmixing_kernel, (seqs, length, deep, shard)),
        grid_spec=pltpu.PrefetchScalarGridSpec(
            num_scalar_prefetch=1,
            grid=(4,),
            in_specs=[
                pl.BlockSpec((rows, width), lambda i, p: (0, 0)),
                pl.BlockSpec((tile, width), lambda i, p: (i ^ p[0], 0)),
                pl.BlockSpec((4, rows, tile), lambda i, p: (0, 0, i ^ p[0])),
                pl.BlockSpec((3, tile), lambda i, p: (0, i ^ p[0])),
            ],
            out_specs=[block] * 4 + [pl.BlockSpec((3, tile), lambda i, p: (0, i ^ p[0]))],
            scratch_shapes=[pltpu.VMEM((seqs, length + 8, tile), full)] * 2,
        ),
        out_shape=[jax.ShapeDtypeStruct((seqs * length, wide), low)] * 4
        + [jax.ShapeDtypeStruct((3, channels), full)],
        compiler_params=params,
        cost_estimate=brief,
    )(spot, grad, weight, kept, taps)


def unprojected_kernel(spot_ref, *refs):
    *sent, weight_ref, out_ref, total = refs
    step = pl.program_id(0)
    tile = weight_ref.shape[2]
    for mask, sent_ref in enumerate(sent):

        @pl.when(step == mask)
        def _(mask=mask, sent_ref=sent_ref):
            term = sum(
                dot(sent_ref[:, k * tile : (k + 1) * tile], weight_ref[k], flipped)
                for k in range(3)
            )
            total[...] = term if mask == 0 else total[...] + term

    @pl.when(step == len(sent) - 1)
    def _():
        out_ref[...] = total[...].astype(low)


def unprojected(sent, weight, spot):
    rows = sent[0].shape[0]
    width, channels = weight.shape[1:]
    tile = channels // 4
    return pl.pallas_call(
        unprojected_kernel,
        grid_spec=pltpu.PrefetchScalarGridSpec(
            num_scalar_prefetch=1,
            grid=(4,),
            in_specs=[pl.BlockSpec((rows, 3 * tile), lambda i, p: (0, 0))] * 4
            + [pl.BlockSpec((3, width, tile), lambda i, p: (0, 0, i ^ p[0]))],
            out_specs=pl.BlockSpec((rows, width), lambda i, p: (0, 0)),
            scratch_shapes=[pltpu.VMEM((rows, width), full)],
        ),
        out_shape=jax.ShapeDtypeStruct((rows, width), low),
        compiler_params=params,
        cost_estimate=brief,
    )(spot, *sent, weight)


def in_terms_kernel(cores, facts_ref, *refs):
    sent, rights, (out_ref, gathered, turned_rows) = refs[:4], refs[4 : 4 + cores], refs[4 + cores :]
    chips, count, shard = out_ref.shape
    rows = sent[0].shape[0]
    share = rows // cores

    @pl.when(pl.program_id(0) == 0)
    def _():
        for index in range(cores):
            core = lax.rem(facts_ref[1] + cores - index, cores)
            start = pl.multiple_of(core * share, 16)
            for mask, ref in enumerate(sent):
                place = pl.multiple_of((facts_ref[0] ^ mask) * share, 16)
                gathered[pl.ds(place, share)] = ref[pl.ds(start, share), :]
            turned_rows[index] = gathered[...].T

    total = sum(
        dot(turned_rows[index], rights[index][...].reshape(chips * share, chips * shard), plain)
        for index in range(cores)
    )
    for j in range(chips):
        out_ref[j] = total[:, j * shard : (j + 1) * shard].astype(low)


def in_weight_terms(sent, count, rights, shard, spot):
    rows = sent[0].shape[0]
    cores = len(rights)
    chips, _, share, half = rights[0].shape
    tile = chips * shard
    tiles = half // tile
    facts = jnp.concatenate([spot, lax.axis_index("mp").astype(jnp.int32).reshape(1)])
    right = pl.BlockSpec((chips, 1, share, tile), lambda i, p: (0, i // tiles, 0, i % tiles))
    return pl.pallas_call(
        functools.partial(in_terms_kernel, cores),
        grid_spec=pltpu.PrefetchScalarGridSpec(
            num_scalar_prefetch=1,
            grid=(2 * tiles,),
            in_specs=[pl.BlockSpec((rows, count), lambda i, p: (0, 0))] * chips + [right] * cores,
            out_specs=pl.BlockSpec((chips, count, shard), lambda i, p: (i, 0, 0)),
            scratch_shapes=[
                pltpu.VMEM((chips * share, count), low),
                pltpu.VMEM((cores, count, chips * share), low),
            ],
        ),
        out_shape=jax.ShapeDtypeStruct((2 * tiles * chips, count, shard), low),
        compiler_params=params,
        cost_estimate=brief,
    )(facts, *sent, *rights)


def out_terms_kernel(facts_ref, *refs):
    *sent, mixed_ref, out_ref, columns = refs
    chips, rows, channels = mixed_ref.shape
    shard = out_ref.shape[2]
    deep = out_ref.shape[0]
    first = sent[0].shape[1] - deep * shard
    for mask, ref in enumerate(sent):
        place = pl.multiple_of((facts_ref[0] ^ mask) * rows, 16)
        columns[pl.ds(place, rows)] = ref[:, first:]
    total = dot(mixed_ref[...].reshape(chips * rows, channels).T, columns[...], plain)
    for far in range(deep):
        out_ref[far] = total[:, far * shard : (far + 1) * shard].astype(low)


def out_weight_terms(sent, count, shown, channels, shard, spot):
    rows, wide = sent[0].shape
    chips = shown.shape[0]
    deep = (wide - count) // shard
    return pl.pallas_call(
        out_terms_kernel,
        grid_spec=pltpu.PrefetchScalarGridSpec(
            num_scalar_prefetch=1,
            grid=(1,),
            in_specs=[pl.BlockSpec((rows, wide), lambda i, p: (0, 0))] * chips
            + [pl.BlockSpec((chips, rows, channels), lambda i, p: (0, 0, 0))],
            out_specs=pl.BlockSpec((deep, channels, shard), lambda i, p: (0, 0, 0)),
            scratch_shapes=[pltpu.VMEM((chips * rows, deep * shard), low)],
        ),
        out_shape=jax.ShapeDtypeStruct((deep, channels, shard), low),
        compiler_params=params,
        cost_estimate=brief,
    )(spot, *sent, shown)


def placing_kernel(parts, *refs):
    placed_ref, pair_ref, down_ref = refs[0], refs[-2], refs[-1]
    chips, three, _ = placed_ref.shape
    chips //= parts
    own = three // 3
    for chip in range(chips):
        block = sum(placed_ref[part * chips + chip].astype(full) for part in range(parts))
        rows = slice(chip * own, (chip + 1) * own)
        pair_ref[:, 0, rows] = block[:own].T
        pair_ref[:, 1, rows] = block[own : 2 * own].T
        down_ref[rows] = block[2 * own :]


def put_in_place(placed, parts, index, groups, before):
    chips, three, shard = placed.shape
    columns = chips // parts * three // 3
    return pl.pallas_call(
        functools.partial(placing_kernel, parts),
        grid=(1,),
        in_specs=[pl.BlockSpec(placed.shape, lambda i: (0, 0, 0))]
        + [pl.BlockSpec(memory_space=pl.ANY)] * len(before),
        out_specs=[
            pl.BlockSpec((shard, 2, columns), lambda i: (0, 0, index)),
            pl.BlockSpec((columns, shard), lambda i: (index, 0)),
        ],
        out_shape=[
            jax.ShapeDtypeStruct((shard, 2, groups * columns), full),
            jax.ShapeDtypeStruct((groups * columns, shard), full),
        ],
        input_output_aliases={1 + n: n for n in range(len(before))},
        compiler_params=params,
        cost_estimate=brief,
    )(placed, *before)


def product_kernel(left_ref, right_ref, out_ref, total):
    step = pl.program_id(0)
    term = dot(left_ref[...], right_ref[...], plain)

    @pl.when(step == 0)
    def _():
        total[...] = term

    @pl.when(step > 0)
    def _():
        total[...] += term

    @pl.when(step == pl.num_programs(0) - 1)
    def _():
        out_ref[...] = total[...].astype(low)


def product_of(left, right):
    rows, depth = left.shape
    width = right.shape[1]
    tile = min(1024, depth)
    return pl.pallas_call(
        product_kernel,
        grid=(depth // tile,),
        in_specs=[
            pl.BlockSpec((rows, tile), lambda i: (0, i)),
            pl.BlockSpec((tile, width), lambda i: (i, 0)),
        ],
        out_specs=pl.BlockSpec((rows, width), lambda i: (0, 0)),
        out_shape=jax.ShapeDtypeStruct((rows, width), low),
        scratch_shapes=[pltpu.VMEM((rows, width), full)],
        compiler_params=params,
        cost_estimate=brief,
    )(left, right)


def tokens_grad_kernel(core_ref, values_ref, inv_ref, gain_ref, inner_ref, *refs):
    parts, (out_ref, sums_ref) = refs[:-2], refs[-2:]
    upstream = sum(ref[...].astype(full) for ref in parts)
    scaled = values_ref[...] * inv_ref[...]
    weighted = upstream * gain_ref[...]
    inner_mean = jnp.mean(weighted * scaled, axis=-1, keepdims=True)
    out_ref[...] = (inner_ref[...] + inv_ref[...] * (weighted - scaled * inner_mean)).astype(low)

    @pl.when(pl.program_id(0) == core_ref[0])
    def _():
        sums_ref[...] = jnp.sum(upstream * scaled, axis=0, keepdims=True)


def tokens_grad_of(values, inv_rms, gain_vec, inner_grad, parts, rows, cores):
    width = values.shape[1]
    share = rows // cores
    core = lax.axis_index("mp").astype(jnp.int32).reshape(1)
    block = pl.BlockSpec((share, width), lambda i, p: (i, 0))
    line = pl.BlockSpec((1, width), lambda i, p: (0, 0))
    return pl.pallas_call(
        tokens_grad_kernel,
        grid_spec=pltpu.PrefetchScalarGridSpec(
            num_scalar_prefetch=1,
            grid=(cores,),
            in_specs=[block, pl.BlockSpec((share, 1), lambda i, p: (i, 0)), line, block]
            + [block] * len(parts),
            out_specs=[block, line],
        ),
        out_shape=[
            jax.ShapeDtypeStruct((rows, width), low),
            jax.ShapeDtypeStruct((1, width), full),
        ],
        compiler_params=params,
        cost_estimate=brief,
    )(core, values, inv_rms, gain_vec.reshape(1, -1), inner_grad, *parts)


def local(
    tokens,
    norm1_gain,
    in_weight,
    conv_weight,
    out_weight,
    norm2_gain,
    gate_up,
    down_weight,
    cotangent,
):
    seq_count, local_len, width = tokens.shape
    row_total = seq_count * local_len
    channels = in_weight.shape[2]
    hidden = gate_up.shape[2]
    parts = lax.axis_size("a")
    cores = lax.axis_size("mp")
    shard = width // (parts * 8)
    deep = width // (4 * shard)
    quarter = channels // 4
    cube, plane, column = ("b", "c", "d"), ("c", "d"), ("a", "b")
    place = lax.axis_index(cube).astype(jnp.int32).reshape(1)
    own = hidden // 8
    in_parts = jnp.transpose(in_weight, (1, 0, 2))

    after = passed_along(
        jnp.stack([tokens[:, :2], cotangent[:, :2]]), column + plane, -1
    ).reshape(2, -1, width)
    before = passed_along(tokens[:, local_len - 2 :], column + plane, 1).reshape(-1, width)
    side = before.shape[0]
    padding = jnp.zeros((2 * side + (-2 * side) % 16, width), low)
    before, upstream_mine = tied(before, share_of(cotangent.reshape(row_total, width)))
    inputs = jnp.concatenate(
        [tokens.reshape(row_total, width), after[0], before, padding[2 * side :]]
    ).astype(full)
    upstream_own = cotangent.reshape(row_total, width)
    upstream_after = jnp.concatenate([after[1], padding[side:]])
    upstream_grad = jnp.concatenate([upstream_own, upstream_after]).astype(full)
    normed_full_one, inv_rms_one = normalize(inputs, norm1_gain)
    normed_one = normed_full_one.astype(low)
    upstream_opposite = opposite(upstream_mine)
    mixed, mixer_state = mixing(normed_one, in_parts, conv_weight, seq_count, local_len)
    mixed, upstream_opposite = tied(mixed, upstream_opposite)
    inner_sum = inputs + summed(dot(mixed, out_weight, plain))
    normed_full_two, inv_rms_two = normalize(inner_sum, norm2_gain)
    normed_two = normed_full_two.astype(low)

    groups = 2 if own > 256 else 1
    half_width = width // 2
    part = own // groups
    unit = row_total // cores
    normed_mine = share_of(normed_two[:row_total])
    together = in_rows([normed_mine, upstream_mine], [(0, 1)])[0]
    from_near = near(together)
    firsts = [(index * 8 + place[0]) * part for index in range(groups)]
    down_own = jnp.stack(
        [lax.dynamic_slice_in_dim(down_weight, first, part, 0) for first in firsts]
    )
    downs = [down_own] + others(down_own, "mp")
    gate_up, together = tied(gate_up, together)
    pair_weight = lax.optimization_barrier(jnp.transpose(gate_up, (1, 0, 2)))
    pair_weight, normed_mine, *arrived = tied(
        pair_weight, normed_mine, *from_near, *downs[1:]
    )
    from_near, downs[1:] = arrived[:3], arrived[3:]
    from_beyond = beyond(from_near, "cdb")
    normed_opposite = opposite(normed_mine)
    pairs = [own_columns(pair_weight, place, part, 0)]
    pairs[0] = [pairs[0]] + others(pairs[0], "mp")
    pair_weight, pairs[0][0] = tied(pair_weight, pairs[0][0])
    activation, normed_two_part = both_ways(
        normed_two, upstream_own, upstream_after, pair_weight, down_weight
    )
    activation, normed_two_part, normed_opposite, *arrived = tied(
        activation, normed_two_part, normed_opposite, *from_beyond, *pairs[0][1:]
    )
    from_beyond, pairs[0][1:] = arrived[:3], arrived[3:]
    latest = []

    def in_turn(*values):
        values = tied(*values, *latest)[: len(values)]
        return values if len(values) > 1 else values[0]

    def over(*values):
        latest[:] = values

    over(normed_two_part, activation)
    normed_one, mixed = in_turn(normed_one, mixed)
    one_mine = share_of(normed_one[:row_total])
    shown = jnp.stack([one_mine[:, :half_width], one_mine[:, half_width:]])
    spare = ((0, 0), (0, half_width - channels))
    shown = jnp.concatenate([jnp.pad(mixed[:row_total], spare), shown.reshape(-1, half_width)])
    shown = lax.all_gather(in_turn(shown), plane)
    normed_two_grad = summed(normed_two_part)

    gathered = [together] + from_near + from_beyond
    hidden_rows, normed_all, upstream_all, *blocks = first_hidden(
        [(rows, 0) for rows in gathered] + [(normed_opposite, 0)],
        [(rows, unit) for rows in gathered] + [(upstream_opposite, 0)],
        unit,
        [in_turn(pairs[0][0])] + pairs[0][1:],
        downs,
        shard,
    )
    def of_others(rows):
        blocks = []
        for core in range(1, cores):
            blocks.append(weight_terms(in_turn(rows), normed_all, upstream_all, shard, core))
            over(blocks[-1])
        return [turned(block, "mp", -core - 1) for core, block in enumerate(blocks)]

    def of_mine(rows, received):
        block = weight_terms(in_turn(rows), normed_all, upstream_all, shard, 0, received)
        over(block)
        return block

    over(hidden_rows)
    received = [turned(block, "mp", -core - 1) for core, block in enumerate(blocks)]
    normed_two_grad = in_turn(normed_two_grad)
    inner_grad = upstream_grad + norm_back(inner_sum, inv_rms_two, norm2_gain, normed_two_grad)
    branch_grad = inner_grad.astype(low)
    over(branch_grad)
    block = of_mine(hidden_rows, received)
    placed = shared_out(block, column + plane)
    if groups > 1:
        next_pair = own_columns(in_turn(pair_weight), place, part, 1)
        over(next_pair)
        pairs.append([next_pair] + others(next_pair, "mp"))
    if groups > 1:
        next_rows = next_hidden(in_turn(normed_all), upstream_all, pairs[1], downs, 1)
        over(next_rows)
        received = of_others(next_rows)
    spot = lax.axis_index(plane).astype(jnp.int32).reshape(1)
    *sent, taps_grad = unmixing(
        in_turn(branch_grad), out_weight, mixer_state, conv_weight, seq_count, local_len, shard, spot
    )
    over(*sent)
    seen = [sent[0], swapped(in_turn(sent[1]), "d"), swapped(in_turn(sent[2]), "c")]
    if groups > 1:
        next_block = of_mine(next_rows, received)
    over(*latest, *seen, shown, placed)
    if groups > 1:
        next_placed = shared_out(in_turn(next_block), column + plane)
    one_all = [in_turn(shown)[:, row_total:].reshape(4, 2, unit, half_width)]
    one_all += others(one_all[0], "mp")
    seen.append(lax.ppermute(in_turn(sent[3]), plane, [(i, 3 - i) for i in range(4)]))
    normed_one_part = unprojected([in_turn(sent[0])] + sent[1:], in_parts, spot)
    over(normed_one_part, *one_all[1:], seen[3])
    seen[0] = in_turn(seen[0])
    in_terms = in_weight_terms(seen, 3 * quarter, one_all, shard, spot)
    over(in_terms)
    if groups > 1:
        over(in_terms, next_placed)
    in_total = shared_out(in_turn(in_terms), column + plane)
    out_terms = out_weight_terms(
        [in_turn(seen[0])] + seen[1:], 3 * quarter, shown, channels, shard, spot
    )
    over(out_terms)
    out_total = lax.psum_scatter(out_terms, column, scatter_dimension=0).astype(full)
    totals = put_in_place(placed, parts, 0, groups, ())
    if groups > 1:
        totals = put_in_place(next_placed, parts, 1, groups, totals)
    gate_up_total, down_total = totals
    parts_one = both_parts(in_turn(normed_one_part))
    tokens_grad, gain_one = tokens_grad_of(
        inputs, inv_rms_one, norm1_gain, inner_grad, parts_one, row_total, cores
    )
    gain_two = jnp.sum(
        share_of((normed_two_grad * inner_sum * inv_rms_two)[:row_total]), axis=0
    )
    channel_start = lax.axis_index("mp") * channels
    taps_full = lax.dynamic_update_slice_in_dim(
        jnp.zeros((3, width), full), taps_grad, channel_start, 1
    )
    small = jnp.concatenate([gain_one, gain_two[None], taps_full], axis=0)
    for axes in (("mp",), plane, column):
        if lax.axis_size(axes) <= 4:
            small = over_all(small, axes)
        else:
            small = lax.psum(small, axes)
    output_part = product_of(in_turn(activation), down_weight)
    output = (inner_sum + summed(output_part))[:row_total].astype(low)
    in_total = (
        jnp.sum(in_total.astype(full).reshape(-1, 4, 3, quarter, shard), axis=0)
        .transpose(3, 1, 0, 2)
        .reshape(shard, 3, channels)
    )
    taps_total = lax.dynamic_slice_in_dim(small[2:], channel_start, channels, 1)
    return (
        output.reshape(seq_count, local_len, width),
        tokens_grad.reshape(seq_count, local_len, width),
        small[0],
        in_total,
        taps_total,
        out_total,
        small[1],
        gate_up_total,
        down_total,
    )


def solution(mesh):
    seq, mp = mesh.shape["seq"], mesh.shape["mp"]
    fine = Mesh(mesh.devices.reshape(seq // 8, 2, 2, 2, mp), ("a", "b", "c", "d", "mp"))
    by_seq = ("a", "b", "c", "d")
    return jax.shard_map(
        local,
        mesh=fine,
        in_specs=(
            P(None, by_seq, None),
            P(),
            P(None, None, "mp"),
            P(None, "mp"),
            P("mp", None),
            P(),
            P(None, None, "mp"),
            P("mp", None),
            P(None, by_seq, None),
        ),
        out_specs=(
            P(None, by_seq, None),
            P(None, by_seq, None),
            P(),
            P(by_seq, None, "mp"),
            P(None, "mp"),
            P("mp", by_seq),
            P(),
            P(by_seq, None, "mp"),
            P("mp", by_seq),
        ),
        check_vma=False,
    )
```

```python
import functools

import jax
import jax.numpy as jnp
from jax import lax
from jax.experimental import pallas as pl
from jax.experimental.pallas import tpu as pltpu
from jax.sharding import Mesh, PartitionSpec as P

epsilon = 1e-05
low = jnp.bfloat16
full = jnp.float32
plain = ((1,), (0,))
flipped = ((1,), (1,))
params = pltpu.CompilerParams(vmem_limit_bytes=56 * 2**20)


brief = pl.CostEstimate(flops=1000, bytes_accessed=1000, transcendentals=0)


def swapped(block, axis):
    return lax.ppermute(block, axis, [(0, 1), (1, 0)])


def passed_along(block, axis, distance):
    devices = range(lax.axis_size(axis))
    route = [(i - distance, i) for i in devices if i - distance in devices]
    return lax.ppermute(block, axis, route)


def turned(block, axis, distance):
    count = lax.axis_size(axis)
    return lax.ppermute(block, axis, [(i, (i + distance) % count) for i in range(count)])


def others(block, axis):
    return [turned(block, axis, step) for step in range(1, lax.axis_size(axis))]


def both_parts(partial):
    if lax.axis_size("mp") == 2:
        return [partial, swapped(partial, "mp")]
    return [lax.psum(partial, "mp")]


def summed(partial):
    return sum(part.astype(full) for part in both_parts(partial.astype(low)))


def over_all(values, axes):
    count = lax.axis_size(axes)
    near_by, *rest = [
        lax.ppermute(values, axes, [(i, i ^ mask) for i in range(count)]) for mask in range(1, count)
    ]
    total = values + near_by
    return total + (rest[0] + rest[1]) if rest else total


def share_of(rows):
    count = rows.shape[0] // lax.axis_size("mp")
    return lax.dynamic_slice_in_dim(rows, lax.axis_index("mp") * count, count, 0)


def tied(*values):
    return lax.optimization_barrier(values)


def near(mine):
    return [swapped(mine, axis) for axis in "bcd"]


def beyond(from_near, axes="cdb"):
    return [swapped(piece, axis) for piece, axis in zip(from_near, axes)]


def opposite(mine):
    return lax.ppermute(mine, ("b", "c", "d"), [(i, 7 - i) for i in range(8)])


def row_kernel(makings, *refs):
    for place, making in enumerate(makings):
        out_ref, row = refs[len(refs) - len(makings) + place], 0
        for part in making:
            index, start, rows = part if isinstance(part, tuple) else (part, 0, None)
            rows = refs[index].shape[0] if rows is None else rows
            out_ref[row : row + rows] = refs[index][start : start + rows]
            row += rows


def in_rows(arrays, makings):
    width = arrays[0].shape[1]

    def rows(making):
        return sum(
            part[2] if isinstance(part, tuple) else arrays[part].shape[0] for part in making
        )

    whole = pl.BlockSpec(memory_space=pltpu.VMEM)
    return pl.pallas_call(
        functools.partial(row_kernel, makings),
        in_specs=[whole] * len(arrays),
        out_specs=[whole] * len(makings),
        out_shape=[jax.ShapeDtypeStruct((rows(making), width), low) for making in makings],
        compiler_params=params,
        cost_estimate=brief,
    )(*arrays)


def shared_out(blocks, axes):
    return lax.all_to_all(blocks, axes, 0, 0, tiled=True)


def shown_to_all(mine, axes):
    return shared_out(jnp.broadcast_to(mine, (lax.axis_size(axes),) + mine.shape), axes)


def normalize(values, gain_vec):
    inv_rms = lax.rsqrt(jnp.mean(values * values, axis=-1, keepdims=True) + epsilon)
    return (values * inv_rms * gain_vec, inv_rms)


def norm_back(values, inv_rms, gain_vec, upstream):
    scaled = values * inv_rms
    weighted = upstream * gain_vec
    inner_mean = jnp.mean(weighted * scaled, axis=-1, keepdims=True)
    return inv_rms * (weighted - scaled * inner_mean)


def dot(left, right, dims):
    return lax.dot_general(left, right, (dims, ((), ())), preferred_element_type=full)


def hidden_terms(gate_pre, up_pre, activation_grad):
    sigmoid_gate = jax.nn.sigmoid(gate_pre)
    swish_gate = gate_pre * sigmoid_gate
    gate_grad = activation_grad * up_pre * sigmoid_gate * (1.0 + gate_pre * (1.0 - sigmoid_gate))
    return (
        (swish_gate * up_pre).astype(low),
        gate_grad.astype(low),
        (activation_grad * swish_gate).astype(low),
    )


def both_ways_kernel(
    x_ref, own_ref, after_ref, pair_ref, down_ref, act_ref, grad_ref, grad_sum, c_ref
):
    step = pl.program_id(0)
    own = own_ref.shape[0]

    @pl.when(step == 0)
    def _():
        grad_sum[...] = jnp.zeros_like(grad_sum)
        c_ref[:own] = own_ref[...]
        c_ref[own:] = after_ref[...]

    activation, gate_grad, up_grad = hidden_terms(
        dot(x_ref[...], pair_ref[0], plain),
        dot(x_ref[...], pair_ref[1], plain),
        dot(c_ref[...], down_ref[...], flipped),
    )
    act_ref[...] = activation
    grad_sum[...] += dot(gate_grad, pair_ref[0], flipped) + dot(up_grad, pair_ref[1], flipped)

    @pl.when(step == pl.num_programs(0) - 1)
    def _():
        grad_ref[...] = grad_sum[...].astype(low)


def both_ways(normed, upstream, after, pair, down):
    rows, width = normed.shape
    hidden = down.shape[0]
    tile = min(512, hidden)
    whole = pl.BlockSpec((rows, width), lambda i: (0, 0))
    return pl.pallas_call(
        both_ways_kernel,
        grid=(hidden // tile,),
        in_specs=[
            whole,
            pl.BlockSpec(upstream.shape, lambda i: (0, 0)),
            pl.BlockSpec(after.shape, lambda i: (0, 0)),
            pl.BlockSpec((2, width, tile), lambda i: (0, 0, i)),
            pl.BlockSpec((tile, width), lambda i: (i, 0)),
        ],
        out_specs=[pl.BlockSpec((rows, tile), lambda i: (0, i)), whole],
        out_shape=[
            jax.ShapeDtypeStruct((rows, hidden), low),
            jax.ShapeDtypeStruct((rows, width), low),
        ],
        scratch_shapes=[pltpu.VMEM((rows, width), full), pltpu.VMEM((rows, width), low)],
        compiler_params=params,
        cost_estimate=brief,
    )(normed, upstream, after, pair, down)


def copy_kernel(place_ref, from_ref, to_ref):
    to_ref[...] = from_ref[...]


def own_columns(pair, place, part, group):
    _, width, _ = pair.shape
    return pl.pallas_call(
        copy_kernel,
        grid_spec=pltpu.PrefetchScalarGridSpec(
            num_scalar_prefetch=1,
            grid=(2,),
            in_specs=[pl.BlockSpec((1, width, part), lambda k, p: (k, 0, 8 * group + p[0]))],
            out_specs=pl.BlockSpec((1, width, part), lambda k, p: (k, 0, 0)),
        ),
        out_shape=jax.ShapeDtypeStruct((2, width, part), low),
        compiler_params=params,
        cost_estimate=brief,
    )(place, pair)


def write_terms(hidden, x, c, arrived, out_ref):
    two = 2 * hidden.shape[0] // 3
    shard = out_ref.shape[2]
    pair = dot(hidden[:two], x, plain)
    single = dot(hidden[two:], c, plain)
    for j in range(out_ref.shape[0]):
        columns = slice(j * shard, (j + 1) * shard)
        for rows, term in ((slice(0, two), pair), (slice(two, None), single)):
            total = term[:, columns]
            for ref in arrived:
                total = total + ref[j, rows].astype(full)
            out_ref[j, rows] = total.astype(low)


def write_hidden(x, c, weights, place):
    for core, (gate_ref, up_ref, down_ref) in enumerate(weights):
        part = down_ref.shape[1]
        activation, gate_grad, up_grad = hidden_terms(
            dot(x, gate_ref[0], plain),
            dot(x, up_ref[0], plain),
            dot(c, down_ref[0], flipped),
        )
        for n, term in enumerate((gate_grad, up_grad, activation)):
            place(core, slice(n * part, (n + 1) * part), term.T)


def threes(refs):
    return [refs[start : start + 3] for start in range(0, len(refs), 3)]


def first_hidden_kernel(counts, spots, unit, cores, *refs):
    pieces = refs[: counts[0]], refs[counts[0] : sum(counts)]
    refs = refs[sum(counts) :]
    weights, refs = refs[: 3 * cores], refs[3 * cores :]
    x_out, c_out = refs[:2]
    terms, (x_all, c_all, other_rows, arrivals, leaving) = refs[2:-5], refs[-5:]
    both = (x_all, x_out), (c_all, c_out)
    count = len(spots[0])
    block = max(1, 384 // unit) * unit
    together = block // unit
    step = pl.program_id(0)

    def coming(index):
        rows = pl.ds(index * unit, unit)
        copies = []
        for n in range(2):
            piece, start = spots[n][index]
            source = pieces[n][piece].at[pl.ds(start, unit)]
            copies.append(
                pltpu.make_async_copy(source, both[n][0].at[rows], arrivals.at[n, index])
            )
        return copies

    def going(index):
        rows = pl.ds(index * block, block)
        return [
            pltpu.make_async_copy(here.at[rows], there.at[rows], leaving.at[n, index])
            for n, (here, there) in enumerate(both)
        ]

    @pl.when(step == 0)
    def _():
        for index in range(count):
            for copy in coming(index):
                copy.start()

    for index in range(count // together):

        @pl.when(step == index)
        def _(index=index):
            for piece in range(index * together, (index + 1) * together):
                for copy in coming(piece):
                    copy.wait()
            for copy in going(index):
                copy.start()

    rows = pl.ds(pl.multiple_of(step * block, block), block)

    def place(core, span, value):
        other_rows[core, span, rows] = value

    write_hidden(x_all[rows], c_all[rows], threes(weights), place)

    @pl.when(step == pl.num_programs(0) - 1)
    def _():
        width, wide = x_all.shape[1], 512
        for core, out_ref in enumerate(terms):
            shard = out_ref.shape[2]
            for start in range(0, width, wide):
                columns = slice(start, start + wide)
                write_terms(
                    other_rows[core],
                    x_all[:, columns],
                    c_all[:, columns],
                    (),
                    out_ref.at[pl.ds(start // shard, wide // shard)],
                )
        for index in range(count // together):
            for copy in going(index):
                copy.wait()


def next_hidden_kernel(x_ref, c_ref, *refs):
    def place(core, span, value):
        refs[-1][core, span] = value

    write_hidden(x_ref[...], c_ref[...], threes(refs[:-1]), place)


def weight_operands(pairs, downs, index):
    _, width, part = pairs[0].shape
    specs, arrays = [], []
    for pair, down in zip(pairs, downs):
        specs += [
            pl.BlockSpec((1, width, part), lambda i, k=k: (k, 0, 0)) for k in range(2)
        ]
        specs.append(pl.BlockSpec((1, part, width), lambda i: (index, 0, 0)))
        arrays += [pair, pair, down]
    return specs, arrays


def first_hidden(x_pieces, c_pieces, unit, pairs, downs, shard):
    width = downs[0].shape[2]
    arrays, spots = [], []
    for row in (x_pieces, c_pieces):
        known = []
        for array, _ in row:
            if not any(array is other for other in known):
                known.append(array)
        arrays.append(known)
        spots.append(
            [
                (next(n for n, other in enumerate(known) if other is array), start)
                for array, start in row
            ]
        )
    counts = tuple(len(known) for known in arrays)
    count, own, cores = len(x_pieces), downs[0].shape[1], len(downs)
    block, rows = max(1, 384 // unit) * unit, count * unit
    anywhere = pl.BlockSpec(memory_space=pl.ANY)
    row_shape = jax.ShapeDtypeStruct((rows, width), low)
    specs, weights = weight_operands(pairs, downs, 0)
    terms_shape = jax.ShapeDtypeStruct((width // shard, 3 * own, shard), low)
    return pl.pallas_call(
        functools.partial(first_hidden_kernel, counts, spots, unit, cores),
        grid=(rows // block,),
        in_specs=[anywhere] * sum(counts) + specs,
        out_specs=[
            anywhere,
            anywhere,
        ]
        + [pl.BlockSpec(terms_shape.shape, lambda i: (0, 0, 0))] * cores,
        scratch_shapes=[
            pltpu.VMEM((rows, width), low),
            pltpu.VMEM((rows, width), low),
            pltpu.VMEM((cores, 3 * own, rows), low),
            pltpu.SemaphoreType.DMA((2, count)),
            pltpu.SemaphoreType.DMA((2, rows // block)),
        ],
        out_shape=[
            row_shape,
            row_shape,
        ]
        + [terms_shape] * cores,
        compiler_params=params,
        cost_estimate=brief,
    )(*arrays[0], *arrays[1], *weights)


def next_hidden(x_all, c_all, pairs, downs, index):
    rows, width = x_all.shape
    own, cores = downs[0].shape[1], len(downs)
    block = min(384, rows)
    tokens = pl.BlockSpec((block, width), lambda i: (i, 0))
    specs, weights = weight_operands(pairs, downs, index)
    return pl.pallas_call(
        next_hidden_kernel,
        grid=(rows // block,),
        in_specs=[tokens, tokens] + specs,
        out_specs=pl.BlockSpec((cores, 3 * own, block), lambda i: (0, 0, i)),
        out_shape=jax.ShapeDtypeStruct((cores, 3 * own, rows), low),
        compiler_params=params,
        cost_estimate=brief,
    )(x_all, c_all, *weights)


def weight_kernel(hidden_ref, x_ref, c_ref, *refs):
    write_terms(hidden_ref[0], x_ref[...], c_ref[...], refs[:-1], refs[-1])


def weight_terms(hidden, normed, upstream, shard, core, arrived=()):
    three, rows = hidden.shape[1:]
    width = normed.shape[1]
    tile = max(512, shard)
    columns = pl.BlockSpec((rows, tile), lambda i: (0, i))
    out_block = pl.BlockSpec((tile // shard, three, shard), lambda i: (i, 0, 0))
    return pl.pallas_call(
        weight_kernel,
        grid=(width // tile,),
        in_specs=[pl.BlockSpec((1, three, rows), lambda i: (core, 0, 0)), columns, columns]
        + [out_block] * len(arrived),
        out_specs=out_block,
        out_shape=jax.ShapeDtypeStruct((width // shard, three, shard), low),
        compiler_params=params,
        cost_estimate=brief,
    )(hidden, normed, upstream, *arrived)


def mixing_kernel(facts, x_ref, weight_ref, taps_ref, mixed_ref, kept_ref, line):
    seqs, length, gap = facts
    own, side = seqs * length, 2 * seqs
    x = x_ref[...]
    b_gate, c_gate, values = (dot(x, weight_ref[k], plain) for k in range(3))
    product = b_gate * values
    conv_out = [None] * (2 * seqs)
    for seq in range(seqs):
        before, after = own + side + 2 * seq, own + 2 * seq
        line[seq, 0:2] = product[before : before + 2]
        line[seq, 2 : length + 2] = product[seq * length : (seq + 1) * length]
        line[seq, length + 2 : length + 4] = product[after : after + 2]
        conv = sum(taps_ref[tap] * line[seq, tap : tap + length + 2] for tap in range(3))
        kept_ref[3, seq * length : (seq + 1) * length] = conv[:length]
        kept_ref[3, after : after + 2] = conv[length:]
    kept_ref[3, own + side :] = jnp.zeros_like(product[own + side :])
    kept_ref[0], kept_ref[1], kept_ref[2] = b_gate, c_gate, values
    mixed_ref[...] = (c_gate * kept_ref[3]).astype(low)


def mixing(normed, weight, taps, seqs, length):
    rows, width = normed.shape
    channels = weight.shape[2]
    tile = channels // 4
    return pl.pallas_call(
        functools.partial(mixing_kernel, (seqs, length, 0)),
        grid=(4,),
        in_specs=[
            pl.BlockSpec((rows, width), lambda i: (0, 0)),
            pl.BlockSpec((3, width, tile), lambda i: (0, 0, i)),
            pl.BlockSpec((3, tile), lambda i: (0, i)),
        ],
        out_specs=[
            pl.BlockSpec((rows, tile), lambda i: (0, i)),
            pl.BlockSpec((4, rows, tile), lambda i: (0, 0, i)),
        ],
        out_shape=[
            jax.ShapeDtypeStruct((rows, channels), low),
            jax.ShapeDtypeStruct((4, rows, channels), full),
        ],
        scratch_shapes=[pltpu.VMEM((seqs, length + 8, tile), full)],
        compiler_params=params,
        cost_estimate=brief,
    )(normed, weight, taps)


def unmixing_kernel(facts, spot_ref, grad_ref, weight_ref, kept_ref, taps_ref, *refs):
    *sent, sums_ref, line, past = refs
    seqs, length, deep, shard = facts
    own, side = seqs * length, 2 * seqs
    tile = weight_ref.shape[0]
    mixed_grad = dot(grad_ref[...], weight_ref[...], flipped)
    conv_grad = mixed_grad * kept_ref[1]
    blocks = []
    for seq in range(seqs):
        rows = slice(seq * length, (seq + 1) * length)
        before, after = own + side + 2 * seq, own + 2 * seq
        line[seq, 0:length] = conv_grad[rows]
        line[seq, length : length + 2] = conv_grad[after : after + 2]
        product_grad = sum(taps_ref[2 - tap] * line[seq, tap : tap + length] for tap in range(3))
        b_gate, values = kept_ref[0, rows], kept_ref[2, rows]
        grads = (product_grad * values, mixed_grad[rows] * kept_ref[3, rows], product_grad * b_gate)
        blocks.append((rows, [grad.astype(low) for grad in grads]))
        past[seq, 0:2] = kept_ref[0, before : before + 2] * kept_ref[2, before : before + 2]
        past[seq, 2 : length + 2] = b_gate * values
    for tap in range(3):
        sums_ref[tap : tap + 1] = sum(
            jnp.sum(line[seq, 0:length] * past[seq, tap : tap + length], axis=0, keepdims=True)
            for seq in range(seqs)
        )
    for mask, sent_ref in enumerate(sent):

        @pl.when(pl.program_id(0) == mask)
        def _(mask=mask, sent_ref=sent_ref):
            for rows, grads in blocks:
                for k, grad in enumerate(grads):
                    sent_ref[rows, k * tile : (k + 1) * tile] = grad
            for part in range(4):

                @pl.when(spot_ref[0] == part ^ mask)
                def _(part=part):
                    for far in range(deep):
                        start = (far * 4 + part) * shard
                        to = 3 * tile + far * shard
                        sent_ref[:, to : to + shard] = grad_ref[0:own, start : start + shard]


def unmixing(grad, weight, kept, taps, seqs, length, shard, spot):
    rows, width = grad.shape
    channels = weight.shape[0]
    tile, deep = channels // 4, width // (4 * shard)
    wide = 3 * tile + deep * shard
    block = pl.BlockSpec((seqs * length, wide), lambda i, p: (0, 0))
    return pl.pallas_call(
        functools.partial(unmixing_kernel, (seqs, length, deep, shard)),
        grid_spec=pltpu.PrefetchScalarGridSpec(
            num_scalar_prefetch=1,
            grid=(4,),
            in_specs=[
                pl.BlockSpec((rows, width), lambda i, p: (0, 0)),
                pl.BlockSpec((tile, width), lambda i, p: (i ^ p[0], 0)),
                pl.BlockSpec((4, rows, tile), lambda i, p: (0, 0, i ^ p[0])),
                pl.BlockSpec((3, tile), lambda i, p: (0, i ^ p[0])),
            ],
            out_specs=[block] * 4 + [pl.BlockSpec((3, tile), lambda i, p: (0, i ^ p[0]))],
            scratch_shapes=[pltpu.VMEM((seqs, length + 8, tile), full)] * 2,
        ),
        out_shape=[jax.ShapeDtypeStruct((seqs * length, wide), low)] * 4
        + [jax.ShapeDtypeStruct((3, channels), full)],
        compiler_params=params,
        cost_estimate=brief,
    )(spot, grad, weight, kept, taps)


def unprojected_kernel(spot_ref, *refs):
    *sent, weight_ref, out_ref, total = refs
    step = pl.program_id(0)
    tile = weight_ref.shape[2]
    for mask, sent_ref in enumerate(sent):

        @pl.when(step == mask)
        def _(mask=mask, sent_ref=sent_ref):
            term = sum(
                dot(sent_ref[:, k * tile : (k + 1) * tile], weight_ref[k], flipped)
                for k in range(3)
            )
            total[...] = term if mask == 0 else total[...] + term

    @pl.when(step == len(sent) - 1)
    def _():
        out_ref[...] = total[...].astype(low)


def unprojected(sent, weight, spot):
    rows = sent[0].shape[0]
    width, channels = weight.shape[1:]
    tile = channels // 4
    return pl.pallas_call(
        unprojected_kernel,
        grid_spec=pltpu.PrefetchScalarGridSpec(
            num_scalar_prefetch=1,
            grid=(4,),
            in_specs=[pl.BlockSpec((rows, 3 * tile), lambda i, p: (0, 0))] * 4
            + [pl.BlockSpec((3, width, tile), lambda i, p: (0, 0, i ^ p[0]))],
            out_specs=pl.BlockSpec((rows, width), lambda i, p: (0, 0)),
            scratch_shapes=[pltpu.VMEM((rows, width), full)],
        ),
        out_shape=jax.ShapeDtypeStruct((rows, width), low),
        compiler_params=params,
        cost_estimate=brief,
    )(spot, *sent, weight)


def in_terms_kernel(cores, facts_ref, *refs):
    sent, rights, (out_ref, gathered, turned_rows) = refs[:4], refs[4 : 4 + cores], refs[4 + cores :]
    chips, count, shard = out_ref.shape
    rows = sent[0].shape[0]
    share = rows // cores

    @pl.when(pl.program_id(0) == 0)
    def _():
        for index in range(cores):
            core = lax.rem(facts_ref[1] + cores - index, cores)
            start = pl.multiple_of(core * share, 16)
            for mask, ref in enumerate(sent):
                place = pl.multiple_of((facts_ref[0] ^ mask) * share, 16)
                gathered[pl.ds(place, share)] = ref[pl.ds(start, share), :]
            turned_rows[index] = gathered[...].T

    total = sum(
        dot(turned_rows[index], rights[index][...].reshape(chips * share, chips * shard), plain)
        for index in range(cores)
    )
    for j in range(chips):
        out_ref[j] = total[:, j * shard : (j + 1) * shard].astype(low)


def in_weight_terms(sent, count, rights, shard, spot):
    rows = sent[0].shape[0]
    cores = len(rights)
    chips, _, share, half = rights[0].shape
    tile = chips * shard
    tiles = half // tile
    facts = jnp.concatenate([spot, lax.axis_index("mp").astype(jnp.int32).reshape(1)])
    right = pl.BlockSpec((chips, 1, share, tile), lambda i, p: (0, i // tiles, 0, i % tiles))
    return pl.pallas_call(
        functools.partial(in_terms_kernel, cores),
        grid_spec=pltpu.PrefetchScalarGridSpec(
            num_scalar_prefetch=1,
            grid=(2 * tiles,),
            in_specs=[pl.BlockSpec((rows, count), lambda i, p: (0, 0))] * chips + [right] * cores,
            out_specs=pl.BlockSpec((chips, count, shard), lambda i, p: (i, 0, 0)),
            scratch_shapes=[
                pltpu.VMEM((chips * share, count), low),
                pltpu.VMEM((cores, count, chips * share), low),
            ],
        ),
        out_shape=jax.ShapeDtypeStruct((2 * tiles * chips, count, shard), low),
        compiler_params=params,
        cost_estimate=brief,
    )(facts, *sent, *rights)


def out_terms_kernel(facts_ref, *refs):
    *sent, mixed_ref, out_ref, columns = refs
    chips, rows, channels = mixed_ref.shape
    shard = out_ref.shape[2]
    deep = out_ref.shape[0]
    first = sent[0].shape[1] - deep * shard
    for mask, ref in enumerate(sent):
        place = pl.multiple_of((facts_ref[0] ^ mask) * rows, 16)
        columns[pl.ds(place, rows)] = ref[:, first:]
    total = dot(mixed_ref[...].reshape(chips * rows, channels).T, columns[...], plain)
    for far in range(deep):
        out_ref[far] = total[:, far * shard : (far + 1) * shard].astype(low)


def out_weight_terms(sent, count, shown, channels, shard, spot):
    rows, wide = sent[0].shape
    chips = shown.shape[0]
    deep = (wide - count) // shard
    return pl.pallas_call(
        out_terms_kernel,
        grid_spec=pltpu.PrefetchScalarGridSpec(
            num_scalar_prefetch=1,
            grid=(1,),
            in_specs=[pl.BlockSpec((rows, wide), lambda i, p: (0, 0))] * chips
            + [pl.BlockSpec((chips, rows, channels), lambda i, p: (0, 0, 0))],
            out_specs=pl.BlockSpec((deep, channels, shard), lambda i, p: (0, 0, 0)),
            scratch_shapes=[pltpu.VMEM((chips * rows, deep * shard), low)],
        ),
        out_shape=jax.ShapeDtypeStruct((deep, channels, shard), low),
        compiler_params=params,
        cost_estimate=brief,
    )(spot, *sent, shown)


def placing_kernel(parts, *refs):
    placed_ref, pair_ref, down_ref = refs[0], refs[-2], refs[-1]
    chips, three, _ = placed_ref.shape
    chips //= parts
    own = three // 3
    for chip in range(chips):
        block = sum(placed_ref[part * chips + chip].astype(full) for part in range(parts))
        rows = slice(chip * own, (chip + 1) * own)
        pair_ref[:, 0, rows] = block[:own].T
        pair_ref[:, 1, rows] = block[own : 2 * own].T
        down_ref[rows] = block[2 * own :]


def put_in_place(placed, parts, index, groups, before):
    chips, three, shard = placed.shape
    columns = chips // parts * three // 3
    return pl.pallas_call(
        functools.partial(placing_kernel, parts),
        grid=(1,),
        in_specs=[pl.BlockSpec(placed.shape, lambda i: (0, 0, 0))]
        + [pl.BlockSpec(memory_space=pl.ANY)] * len(before),
        out_specs=[
            pl.BlockSpec((shard, 2, columns), lambda i: (0, 0, index)),
            pl.BlockSpec((columns, shard), lambda i: (index, 0)),
        ],
        out_shape=[
            jax.ShapeDtypeStruct((shard, 2, groups * columns), full),
            jax.ShapeDtypeStruct((groups * columns, shard), full),
        ],
        input_output_aliases={1 + n: n for n in range(len(before))},
        compiler_params=params,
        cost_estimate=brief,
    )(placed, *before)


def product_kernel(left_ref, right_ref, out_ref, total):
    step = pl.program_id(0)
    term = dot(left_ref[...], right_ref[...], plain)

    @pl.when(step == 0)
    def _():
        total[...] = term

    @pl.when(step > 0)
    def _():
        total[...] += term

    @pl.when(step == pl.num_programs(0) - 1)
    def _():
        out_ref[...] = total[...].astype(low)


def product_of(left, right):
    rows, depth = left.shape
    width = right.shape[1]
    tile = min(1024, depth)
    return pl.pallas_call(
        product_kernel,
        grid=(depth // tile,),
        in_specs=[
            pl.BlockSpec((rows, tile), lambda i: (0, i)),
            pl.BlockSpec((tile, width), lambda i: (i, 0)),
        ],
        out_specs=pl.BlockSpec((rows, width), lambda i: (0, 0)),
        out_shape=jax.ShapeDtypeStruct((rows, width), low),
        scratch_shapes=[pltpu.VMEM((rows, width), full)],
        compiler_params=params,
        cost_estimate=brief,
    )(left, right)


def tokens_grad_kernel(core_ref, values_ref, inv_ref, gain_ref, inner_ref, *refs):
    parts, (out_ref, sums_ref) = refs[:-2], refs[-2:]
    upstream = sum(ref[...].astype(full) for ref in parts)
    scaled = values_ref[...] * inv_ref[...]
    weighted = upstream * gain_ref[...]
    inner_mean = jnp.mean(weighted * scaled, axis=-1, keepdims=True)
    out_ref[...] = (inner_ref[...] + inv_ref[...] * (weighted - scaled * inner_mean)).astype(low)

    @pl.when(pl.program_id(0) == core_ref[0])
    def _():
        sums_ref[...] = jnp.sum(upstream * scaled, axis=0, keepdims=True)


def tokens_grad_of(values, inv_rms, gain_vec, inner_grad, parts, rows, cores):
    width = values.shape[1]
    share = rows // cores
    core = lax.axis_index("mp").astype(jnp.int32).reshape(1)
    block = pl.BlockSpec((share, width), lambda i, p: (i, 0))
    line = pl.BlockSpec((1, width), lambda i, p: (0, 0))
    return pl.pallas_call(
        tokens_grad_kernel,
        grid_spec=pltpu.PrefetchScalarGridSpec(
            num_scalar_prefetch=1,
            grid=(cores,),
            in_specs=[block, pl.BlockSpec((share, 1), lambda i, p: (i, 0)), line, block]
            + [block] * len(parts),
            out_specs=[block, line],
        ),
        out_shape=[
            jax.ShapeDtypeStruct((rows, width), low),
            jax.ShapeDtypeStruct((1, width), full),
        ],
        compiler_params=params,
        cost_estimate=brief,
    )(core, values, inv_rms, gain_vec.reshape(1, -1), inner_grad, *parts)


def local(
    tokens,
    norm1_gain,
    in_weight,
    conv_weight,
    out_weight,
    norm2_gain,
    gate_up,
    down_weight,
    cotangent,
):
    seq_count, local_len, width = tokens.shape
    row_total = seq_count * local_len
    channels = in_weight.shape[2]
    hidden = gate_up.shape[2]
    parts = lax.axis_size("a")
    cores = lax.axis_size("mp")
    shard = width // (parts * 8)
    deep = width // (4 * shard)
    quarter = channels // 4
    cube, plane, column = ("b", "c", "d"), ("c", "d"), ("a", "b")
    place = lax.axis_index(cube).astype(jnp.int32).reshape(1)
    own = hidden // 8
    in_parts = jnp.transpose(in_weight, (1, 0, 2))

    after = passed_along(
        jnp.stack([tokens[:, :2], cotangent[:, :2]]), column + plane, -1
    ).reshape(2, -1, width)
    before = passed_along(tokens[:, local_len - 2 :], column + plane, 1).reshape(-1, width)
    side = before.shape[0]
    padding = jnp.zeros((2 * side + (-2 * side) % 16, width), low)
    before, upstream_mine = tied(before, share_of(cotangent.reshape(row_total, width)))
    inputs = jnp.concatenate(
        [tokens.reshape(row_total, width), after[0], before, padding[2 * side :]]
    ).astype(full)
    upstream_own = cotangent.reshape(row_total, width)
    upstream_after = jnp.concatenate([after[1], padding[side:]])
    upstream_grad = jnp.concatenate([upstream_own, upstream_after]).astype(full)
    normed_full_one, inv_rms_one = normalize(inputs, norm1_gain)
    normed_one = normed_full_one.astype(low)
    upstream_opposite = opposite(upstream_mine)
    mixed, mixer_state = mixing(normed_one, in_parts, conv_weight, seq_count, local_len)
    mixed, upstream_opposite = tied(mixed, upstream_opposite)
    inner_sum = inputs + summed(dot(mixed, out_weight, plain))
    normed_full_two, inv_rms_two = normalize(inner_sum, norm2_gain)
    normed_two = normed_full_two.astype(low)

    groups = 2 if own > 256 else 1
    half_width = width // 2
    part = own // groups
    unit = row_total // cores
    normed_mine = share_of(normed_two[:row_total])
    together = in_rows([normed_mine, upstream_mine], [(0, 1)])[0]
    from_near = near(together)
    firsts = [(index * 8 + place[0]) * part for index in range(groups)]
    down_own = jnp.stack(
        [lax.dynamic_slice_in_dim(down_weight, first, part, 0) for first in firsts]
    )
    downs = [down_own] + others(down_own, "mp")
    gate_up, together = tied(gate_up, together)
    pair_weight = lax.optimization_barrier(jnp.transpose(gate_up, (1, 0, 2)))
    pair_weight, normed_mine, *arrived = tied(
        pair_weight, normed_mine, *from_near, *downs[1:]
    )
    from_near, downs[1:] = arrived[:3], arrived[3:]
    from_beyond = beyond(from_near, "cdb")
    normed_opposite = opposite(normed_mine)
    pairs = [own_columns(pair_weight, place, part, 0)]
    pairs[0] = [pairs[0]] + others(pairs[0], "mp")
    pair_weight, pairs[0][0] = tied(pair_weight, pairs[0][0])
    activation, normed_two_part = both_ways(
        normed_two, upstream_own, upstream_after, pair_weight, down_weight
    )
    activation, normed_two_part, normed_opposite, *arrived = tied(
        activation, normed_two_part, normed_opposite, *from_beyond, *pairs[0][1:]
    )
    from_beyond, pairs[0][1:] = arrived[:3], arrived[3:]
    latest = []

    def in_turn(*values):
        values = tied(*values, *latest)[: len(values)]
        return values if len(values) > 1 else values[0]

    def over(*values):
        latest[:] = values

    over(normed_two_part, activation)
    normed_one, mixed = in_turn(normed_one, mixed)
    one_mine = share_of(normed_one[:row_total])
    shown = jnp.stack([one_mine[:, :half_width], one_mine[:, half_width:]])
    spare = ((0, 0), (0, half_width - channels))
    shown = jnp.concatenate([jnp.pad(mixed[:row_total], spare), shown.reshape(-1, half_width)])
    shown = lax.all_gather(in_turn(shown), plane)
    normed_two_grad = summed(normed_two_part)

    gathered = [together] + from_near + from_beyond
    normed_all, upstream_all, *blocks = first_hidden(
        [(rows, 0) for rows in gathered] + [(normed_opposite, 0)],
        [(rows, unit) for rows in gathered] + [(upstream_opposite, 0)],
        unit,
        [in_turn(pairs[0][1])] + pairs[0][2:],
        downs[1:],
        shard,
    )

    def of_others(rows):
        blocks = []
        for core in range(1, cores):
            blocks.append(weight_terms(in_turn(rows), normed_all, upstream_all, shard, core))
            over(blocks[-1])
        return [turned(block, "mp", -core - 1) for core, block in enumerate(blocks)]

    def of_mine(rows, received):
        block = weight_terms(in_turn(rows), normed_all, upstream_all, shard, 0, received)
        over(block)
        return block

    over(*blocks)
    received = [turned(block, "mp", -core - 1) for core, block in enumerate(blocks)]
    hidden_rows = next_hidden(in_turn(normed_all), upstream_all, pairs[0][:1], downs[:1], 0)
    over(hidden_rows)
    block = of_mine(hidden_rows, received)
    placed = shared_out(block, column + plane)
    if groups > 1:
        next_pair = own_columns(in_turn(pair_weight), place, part, 1)
        over(next_pair)
        pairs.append([next_pair] + others(next_pair, "mp"))
    normed_two_grad = in_turn(normed_two_grad)
    inner_grad = upstream_grad + norm_back(inner_sum, inv_rms_two, norm2_gain, normed_two_grad)
    branch_grad = inner_grad.astype(low)
    over(branch_grad)
    if groups > 1:
        next_rows = next_hidden(in_turn(normed_all), upstream_all, pairs[1], downs, 1)
        over(next_rows)
        received = of_others(next_rows)
    spot = lax.axis_index(plane).astype(jnp.int32).reshape(1)
    *sent, taps_grad = unmixing(
        in_turn(branch_grad), out_weight, mixer_state, conv_weight, seq_count, local_len, shard, spot
    )
    over(*sent)
    seen = [sent[0], swapped(in_turn(sent[1]), "d"), swapped(in_turn(sent[2]), "c")]
    if groups > 1:
        next_block = of_mine(next_rows, received)
    over(*latest, *seen, shown, placed)
    if groups > 1:
        next_placed = shared_out(in_turn(next_block), column + plane)
    one_all = [in_turn(shown)[:, row_total:].reshape(4, 2, unit, half_width)]
    one_all += others(one_all[0], "mp")
    seen.append(lax.ppermute(in_turn(sent[3]), plane, [(i, 3 - i) for i in range(4)]))
    normed_one_part = unprojected([in_turn(sent[0])] + sent[1:], in_parts, spot)
    over(normed_one_part, *one_all[1:], seen[3])
    seen[0] = in_turn(seen[0])
    in_terms = in_weight_terms(seen, 3 * quarter, one_all, shard, spot)
    over(in_terms)
    if groups > 1:
        over(in_terms, next_placed)
    in_total = shared_out(in_turn(in_terms), column + plane)
    out_terms = out_weight_terms(
        [in_turn(seen[0])] + seen[1:], 3 * quarter, shown, channels, shard, spot
    )
    over(out_terms)
    out_total = lax.psum_scatter(out_terms, column, scatter_dimension=0).astype(full)
    totals = put_in_place(placed, parts, 0, groups, ())
    if groups > 1:
        totals = put_in_place(next_placed, parts, 1, groups, totals)
    gate_up_total, down_total = totals
    parts_one = both_parts(in_turn(normed_one_part))
    tokens_grad, gain_one = tokens_grad_of(
        inputs, inv_rms_one, norm1_gain, inner_grad, parts_one, row_total, cores
    )
    gain_two = jnp.sum(
        share_of((normed_two_grad * inner_sum * inv_rms_two)[:row_total]), axis=0
    )
    channel_start = lax.axis_index("mp") * channels
    taps_full = lax.dynamic_update_slice_in_dim(
        jnp.zeros((3, width), full), taps_grad, channel_start, 1
    )
    small = jnp.concatenate([gain_one, gain_two[None], taps_full], axis=0)
    for axes in (("mp",), plane, column):
        if lax.axis_size(axes) <= 4:
            small = over_all(small, axes)
        else:
            small = lax.psum(small, axes)
    output_part = product_of(in_turn(activation), down_weight)
    output = (inner_sum + summed(output_part))[:row_total].astype(low)
    in_total = (
        jnp.sum(in_total.astype(full).reshape(-1, 4, 3, quarter, shard), axis=0)
        .transpose(3, 1, 0, 2)
        .reshape(shard, 3, channels)
    )
    taps_total = lax.dynamic_slice_in_dim(small[2:], channel_start, channels, 1)
    return (
        output.reshape(seq_count, local_len, width),
        tokens_grad.reshape(seq_count, local_len, width),
        small[0],
        in_total,
        taps_total,
        out_total,
        small[1],
        gate_up_total,
        down_total,
    )


def solution(mesh):
    seq, mp = mesh.shape["seq"], mesh.shape["mp"]
    fine = Mesh(mesh.devices.reshape(seq // 8, 2, 2, 2, mp), ("a", "b", "c", "d", "mp"))
    by_seq = ("a", "b", "c", "d")
    return jax.shard_map(
        local,
        mesh=fine,
        in_specs=(
            P(None, by_seq, None),
            P(),
            P(None, None, "mp"),
            P(None, "mp"),
            P("mp", None),
            P(),
            P(None, None, "mp"),
            P("mp", None),
            P(None, by_seq, None),
        ),
        out_specs=(
            P(None, by_seq, None),
            P(None, by_seq, None),
            P(),
            P(by_seq, None, "mp"),
            P(None, "mp"),
            P("mp", by_seq),
            P(),
            P(by_seq, None, "mp"),
            P("mp", by_seq),
        ),
        check_vma=False,
    )
```

```python
import functools

import jax
import jax.numpy as jnp
from jax import lax
from jax.experimental import pallas as pl
from jax.experimental.pallas import tpu as pltpu
from jax.sharding import Mesh, PartitionSpec as P

epsilon = 1e-05
low = jnp.bfloat16
full = jnp.float32
plain = ((1,), (0,))
flipped = ((1,), (1,))
params = pltpu.CompilerParams(vmem_limit_bytes=56 * 2**20)


brief = pl.CostEstimate(flops=1000, bytes_accessed=1000, transcendentals=0)


def swapped(block, axis):
    return lax.ppermute(block, axis, [(0, 1), (1, 0)])


def passed_along(block, axis, distance):
    devices = range(lax.axis_size(axis))
    route = [(i - distance, i) for i in devices if i - distance in devices]
    return lax.ppermute(block, axis, route)


def turned(block, axis, distance):
    count = lax.axis_size(axis)
    return lax.ppermute(block, axis, [(i, (i + distance) % count) for i in range(count)])


def others(block, axis):
    return [turned(block, axis, step) for step in range(1, lax.axis_size(axis))]


def both_parts(partial):
    if lax.axis_size("mp") == 2:
        return [partial, swapped(partial, "mp")]
    return [lax.psum(partial, "mp")]


def summed(partial):
    return sum(part.astype(full) for part in both_parts(partial.astype(low)))


def over_all(values, axes):
    count = lax.axis_size(axes)
    near_by, *rest = [
        lax.ppermute(values, axes, [(i, i ^ mask) for i in range(count)]) for mask in range(1, count)
    ]
    total = values + near_by
    return total + (rest[0] + rest[1]) if rest else total


def share_of(rows):
    count = rows.shape[0] // lax.axis_size("mp")
    return lax.dynamic_slice_in_dim(rows, lax.axis_index("mp") * count, count, 0)


def tied(*values):
    return lax.optimization_barrier(values)


def near(mine):
    return [swapped(mine, axis) for axis in "bcd"]


def beyond(from_near, axes="cdb"):
    return [swapped(piece, axis) for piece, axis in zip(from_near, axes)]


def opposite(mine):
    return lax.ppermute(mine, ("b", "c", "d"), [(i, 7 - i) for i in range(8)])


def row_kernel(makings, *refs):
    for place, making in enumerate(makings):
        out_ref, row = refs[len(refs) - len(makings) + place], 0
        for part in making:
            index, start, rows = part if isinstance(part, tuple) else (part, 0, None)
            rows = refs[index].shape[0] if rows is None else rows
            out_ref[row : row + rows] = refs[index][start : start + rows]
            row += rows


def in_rows(arrays, makings):
    width = arrays[0].shape[1]

    def rows(making):
        return sum(
            part[2] if isinstance(part, tuple) else arrays[part].shape[0] for part in making
        )

    whole = pl.BlockSpec(memory_space=pltpu.VMEM)
    return pl.pallas_call(
        functools.partial(row_kernel, makings),
        in_specs=[whole] * len(arrays),
        out_specs=[whole] * len(makings),
        out_shape=[jax.ShapeDtypeStruct((rows(making), width), low) for making in makings],
        compiler_params=params,
        cost_estimate=brief,
    )(*arrays)


def shared_out(blocks, axes):
    return lax.all_to_all(blocks, axes, 0, 0, tiled=True)


def shown_to_all(mine, axes):
    return shared_out(jnp.broadcast_to(mine, (lax.axis_size(axes),) + mine.shape), axes)


def normalize(values, gain_vec):
    inv_rms = lax.rsqrt(jnp.mean(values * values, axis=-1, keepdims=True) + epsilon)
    return (values * inv_rms * gain_vec, inv_rms)


def norm_back(values, inv_rms, gain_vec, upstream):
    scaled = values * inv_rms
    weighted = upstream * gain_vec
    inner_mean = jnp.mean(weighted * scaled, axis=-1, keepdims=True)
    return inv_rms * (weighted - scaled * inner_mean)


def dot(left, right, dims):
    return lax.dot_general(left, right, (dims, ((), ())), preferred_element_type=full)


def hidden_terms(gate_pre, up_pre, activation_grad):
    sigmoid_gate = jax.nn.sigmoid(gate_pre)
    swish_gate = gate_pre * sigmoid_gate
    gate_grad = activation_grad * up_pre * sigmoid_gate * (1.0 + gate_pre * (1.0 - sigmoid_gate))
    return (
        (swish_gate * up_pre).astype(low),
        gate_grad.astype(low),
        (activation_grad * swish_gate).astype(low),
    )


def both_ways_kernel(
    x_ref, own_ref, after_ref, pair_ref, down_ref, act_ref, grad_ref, grad_sum, c_ref
):
    step = pl.program_id(0)
    own = own_ref.shape[0]

    @pl.when(step == 0)
    def _():
        grad_sum[...] = jnp.zeros_like(grad_sum)
        c_ref[:own] = own_ref[...]
        c_ref[own:] = after_ref[...]

    activation, gate_grad, up_grad = hidden_terms(
        dot(x_ref[...], pair_ref[0], plain),
        dot(x_ref[...], pair_ref[1], plain),
        dot(c_ref[...], down_ref[...], flipped),
    )
    act_ref[...] = activation
    grad_sum[...] += dot(gate_grad, pair_ref[0], flipped) + dot(up_grad, pair_ref[1], flipped)

    @pl.when(step == pl.num_programs(0) - 1)
    def _():
        grad_ref[...] = grad_sum[...].astype(low)


def both_ways(normed, upstream, after, pair, down):
    rows, width = normed.shape
    hidden = down.shape[0]
    tile = min(512, hidden)
    whole = pl.BlockSpec((rows, width), lambda i: (0, 0))
    return pl.pallas_call(
        both_ways_kernel,
        grid=(hidden // tile,),
        in_specs=[
            whole,
            pl.BlockSpec(upstream.shape, lambda i: (0, 0)),
            pl.BlockSpec(after.shape, lambda i: (0, 0)),
            pl.BlockSpec((2, width, tile), lambda i: (0, 0, i)),
            pl.BlockSpec((tile, width), lambda i: (i, 0)),
        ],
        out_specs=[pl.BlockSpec((rows, tile), lambda i: (0, i)), whole],
        out_shape=[
            jax.ShapeDtypeStruct((rows, hidden), low),
            jax.ShapeDtypeStruct((rows, width), low),
        ],
        scratch_shapes=[pltpu.VMEM((rows, width), full), pltpu.VMEM((rows, width), low)],
        compiler_params=params,
        cost_estimate=brief,
    )(normed, upstream, after, pair, down)


def copy_kernel(place_ref, from_ref, to_ref):
    to_ref[...] = from_ref[...]


def own_columns(pair, place, part, group):
    _, width, _ = pair.shape
    return pl.pallas_call(
        copy_kernel,
        grid_spec=pltpu.PrefetchScalarGridSpec(
            num_scalar_prefetch=1,
            grid=(2,),
            in_specs=[pl.BlockSpec((1, width, part), lambda k, p: (k, 0, 8 * group + p[0]))],
            out_specs=pl.BlockSpec((1, width, part), lambda k, p: (k, 0, 0)),
        ),
        out_shape=jax.ShapeDtypeStruct((2, width, part), low),
        compiler_params=params,
        cost_estimate=brief,
    )(place, pair)


def write_terms(hidden, x, c, arrived, out_ref):
    two = 2 * hidden.shape[0] // 3
    shard = out_ref.shape[2]
    pair = dot(hidden[:two], x, plain)
    single = dot(hidden[two:], c, plain)
    for j in range(out_ref.shape[0]):
        columns = slice(j * shard, (j + 1) * shard)
        for rows, term in ((slice(0, two), pair), (slice(two, None), single)):
            total = term[:, columns]
            for ref in arrived:
                total = total + ref[j, rows].astype(full)
            out_ref[j, rows] = total.astype(low)


def write_hidden(x, c, weights, place):
    for core, (gate_ref, up_ref, down_ref) in enumerate(weights):
        part = down_ref.shape[1]
        activation, gate_grad, up_grad = hidden_terms(
            dot(x, gate_ref[0], plain),
            dot(x, up_ref[0], plain),
            dot(c, down_ref[0], flipped),
        )
        for n, term in enumerate((gate_grad, up_grad, activation)):
            place(core, slice(n * part, (n + 1) * part), term.T)


def threes(refs):
    return [refs[start : start + 3] for start in range(0, len(refs), 3)]


def first_hidden_kernel(counts, spots, unit, cores, *refs):
    pieces = refs[: counts[0]], refs[counts[0] : sum(counts)]
    refs = refs[sum(counts) :]
    weights, refs = refs[: 3 * cores], refs[3 * cores :]
    x_out, c_out = refs[:2]
    terms, (x_all, c_all, other_rows, arrivals, leaving) = refs[2:-5], refs[-5:]
    both = (x_all, x_out), (c_all, c_out)
    count = len(spots[0])
    block = max(1, 384 // unit) * unit
    together = block // unit
    step = pl.program_id(0)

    def coming(index):
        rows = pl.ds(index * unit, unit)
        copies = []
        for n in range(2):
            piece, start = spots[n][index]
            source = pieces[n][piece].at[pl.ds(start, unit)]
            copies.append(
                pltpu.make_async_copy(source, both[n][0].at[rows], arrivals.at[n, index])
            )
        return copies

    def going(index):
        rows = pl.ds(index * block, block)
        return [
            pltpu.make_async_copy(here.at[rows], there.at[rows], leaving.at[n, index])
            for n, (here, there) in enumerate(both)
        ]

    @pl.when(step == 0)
    def _():
        for index in range(count):
            for copy in coming(index):
                copy.start()

    for index in range(count // together):

        @pl.when(step == index)
        def _(index=index):
            for piece in range(index * together, (index + 1) * together):
                for copy in coming(piece):
                    copy.wait()
            for copy in going(index):
                copy.start()

    rows = pl.ds(pl.multiple_of(step * block, block), block)

    def place(core, span, value):
        other_rows[core, span, rows] = value

    write_hidden(x_all[rows], c_all[rows], threes(weights), place)

    @pl.when(step == pl.num_programs(0) - 1)
    def _():
        width, wide = x_all.shape[1], 512
        for core, out_ref in enumerate(terms):
            shard = out_ref.shape[2]
            for start in range(0, width, wide):
                columns = slice(start, start + wide)
                write_terms(
                    other_rows[core],
                    x_all[:, columns],
                    c_all[:, columns],
                    (),
                    out_ref.at[pl.ds(start // shard, wide // shard)],
                )
        for index in range(count // together):
            for copy in going(index):
                copy.wait()


def next_hidden_kernel(x_ref, c_ref, *refs):
    def place(core, span, value):
        refs[-1][core, span] = value

    write_hidden(x_ref[...], c_ref[...], threes(refs[:-1]), place)


def weight_operands(pairs, downs, index):
    _, width, part = pairs[0].shape
    specs, arrays = [], []
    for pair, down in zip(pairs, downs):
        specs += [
            pl.BlockSpec((1, width, part), lambda i, k=k: (k, 0, 0)) for k in range(2)
        ]
        specs.append(pl.BlockSpec((1, part, width), lambda i: (index, 0, 0)))
        arrays += [pair, pair, down]
    return specs, arrays


def first_hidden(x_pieces, c_pieces, unit, pairs, downs, shard):
    width = downs[0].shape[2]
    arrays, spots = [], []
    for row in (x_pieces, c_pieces):
        known = []
        for array, _ in row:
            if not any(array is other for other in known):
                known.append(array)
        arrays.append(known)
        spots.append(
            [
                (next(n for n, other in enumerate(known) if other is array), start)
                for array, start in row
            ]
        )
    counts = tuple(len(known) for known in arrays)
    count, own, cores = len(x_pieces), downs[0].shape[1], len(downs)
    block, rows = max(1, 384 // unit) * unit, count * unit
    anywhere = pl.BlockSpec(memory_space=pl.ANY)
    row_shape = jax.ShapeDtypeStruct((rows, width), low)
    specs, weights = weight_operands(pairs, downs, 0)
    terms_shape = jax.ShapeDtypeStruct((width // shard, 3 * own, shard), low)
    return pl.pallas_call(
        functools.partial(first_hidden_kernel, counts, spots, unit, cores),
        grid=(rows // block,),
        in_specs=[anywhere] * sum(counts) + specs,
        out_specs=[
            anywhere,
            anywhere,
        ]
        + [pl.BlockSpec(terms_shape.shape, lambda i: (0, 0, 0))] * cores,
        scratch_shapes=[
            pltpu.VMEM((rows, width), low),
            pltpu.VMEM((rows, width), low),
            pltpu.VMEM((cores, 3 * own, rows), low),
            pltpu.SemaphoreType.DMA((2, count)),
            pltpu.SemaphoreType.DMA((2, rows // block)),
        ],
        out_shape=[
            row_shape,
            row_shape,
        ]
        + [terms_shape] * cores,
        compiler_params=params,
        cost_estimate=brief,
    )(*arrays[0], *arrays[1], *weights)


def next_hidden(x_all, c_all, pairs, downs, index):
    rows, width = x_all.shape
    own, cores = downs[0].shape[1], len(downs)
    block = min(384, rows)
    tokens = pl.BlockSpec((block, width), lambda i: (i, 0))
    specs, weights = weight_operands(pairs, downs, index)
    return pl.pallas_call(
        next_hidden_kernel,
        grid=(rows // block,),
        in_specs=[tokens, tokens] + specs,
        out_specs=pl.BlockSpec((cores, 3 * own, block), lambda i: (0, 0, i)),
        out_shape=jax.ShapeDtypeStruct((cores, 3 * own, rows), low),
        compiler_params=params,
        cost_estimate=brief,
    )(x_all, c_all, *weights)


def weight_kernel(hidden_ref, x_ref, c_ref, *refs):
    write_terms(hidden_ref[0], x_ref[...], c_ref[...], refs[:-1], refs[-1])


def weight_terms(hidden, normed, upstream, shard, core, arrived=()):
    three, rows = hidden.shape[1:]
    width = normed.shape[1]
    tile = max(512, shard)
    columns = pl.BlockSpec((rows, tile), lambda i: (0, i))
    out_block = pl.BlockSpec((tile // shard, three, shard), lambda i: (i, 0, 0))
    return pl.pallas_call(
        weight_kernel,
        grid=(width // tile,),
        in_specs=[pl.BlockSpec((1, three, rows), lambda i: (core, 0, 0)), columns, columns]
        + [out_block] * len(arrived),
        out_specs=out_block,
        out_shape=jax.ShapeDtypeStruct((width // shard, three, shard), low),
        compiler_params=params,
        cost_estimate=brief,
    )(hidden, normed, upstream, *arrived)


def mixing_kernel(facts, x_ref, weight_ref, taps_ref, mixed_ref, kept_ref, line):
    seqs, length, gap = facts
    own, side = seqs * length, 2 * seqs
    x = x_ref[...]
    b_gate, c_gate, values = (dot(x, weight_ref[k], plain) for k in range(3))
    product = b_gate * values
    conv_out = [None] * (2 * seqs)
    for seq in range(seqs):
        before, after = own + side + 2 * seq, own + 2 * seq
        line[seq, 0:2] = product[before : before + 2]
        line[seq, 2 : length + 2] = product[seq * length : (seq + 1) * length]
        line[seq, length + 2 : length + 4] = product[after : after + 2]
        conv = sum(taps_ref[tap] * line[seq, tap : tap + length + 2] for tap in range(3))
        kept_ref[3, seq * length : (seq + 1) * length] = conv[:length]
        kept_ref[3, after : after + 2] = conv[length:]
    kept_ref[3, own + side :] = jnp.zeros_like(product[own + side :])
    kept_ref[0], kept_ref[1], kept_ref[2] = b_gate, c_gate, values
    mixed_ref[...] = (c_gate * kept_ref[3]).astype(low)


def mixing(normed, weight, taps, seqs, length):
    rows, width = normed.shape
    channels = weight.shape[2]
    tile = channels // 4
    return pl.pallas_call(
        functools.partial(mixing_kernel, (seqs, length, 0)),
        grid=(4,),
        in_specs=[
            pl.BlockSpec((rows, width), lambda i: (0, 0)),
            pl.BlockSpec((3, width, tile), lambda i: (0, 0, i)),
            pl.BlockSpec((3, tile), lambda i: (0, i)),
        ],
        out_specs=[
            pl.BlockSpec((rows, tile), lambda i: (0, i)),
            pl.BlockSpec((4, rows, tile), lambda i: (0, 0, i)),
        ],
        out_shape=[
            jax.ShapeDtypeStruct((rows, channels), low),
            jax.ShapeDtypeStruct((4, rows, channels), full),
        ],
        scratch_shapes=[pltpu.VMEM((seqs, length + 8, tile), full)],
        compiler_params=params,
        cost_estimate=brief,
    )(normed, weight, taps)


def unmixing_kernel(facts, spot_ref, grad_ref, weight_ref, kept_ref, taps_ref, *refs):
    *sent, sums_ref, line, past = refs
    seqs, length, deep, shard = facts
    own, side = seqs * length, 2 * seqs
    tile = weight_ref.shape[0]
    mixed_grad = dot(grad_ref[...], weight_ref[...], flipped)
    conv_grad = mixed_grad * kept_ref[1]
    blocks = []
    for seq in range(seqs):
        rows = slice(seq * length, (seq + 1) * length)
        before, after = own + side + 2 * seq, own + 2 * seq
        line[seq, 0:length] = conv_grad[rows]
        line[seq, length : length + 2] = conv_grad[after : after + 2]
        product_grad = sum(taps_ref[2 - tap] * line[seq, tap : tap + length] for tap in range(3))
        b_gate, values = kept_ref[0, rows], kept_ref[2, rows]
        grads = (product_grad * values, mixed_grad[rows] * kept_ref[3, rows], product_grad * b_gate)
        blocks.append((rows, [grad.astype(low) for grad in grads]))
        past[seq, 0:2] = kept_ref[0, before : before + 2] * kept_ref[2, before : before + 2]
        past[seq, 2 : length + 2] = b_gate * values
    for tap in range(3):
        sums_ref[tap : tap + 1] = sum(
            jnp.sum(line[seq, 0:length] * past[seq, tap : tap + length], axis=0, keepdims=True)
            for seq in range(seqs)
        )
    for mask, sent_ref in enumerate(sent):

        @pl.when(pl.program_id(0) == mask)
        def _(mask=mask, sent_ref=sent_ref):
            for rows, grads in blocks:
                for k, grad in enumerate(grads):
                    sent_ref[rows, k * tile : (k + 1) * tile] = grad
            for part in range(4):

                @pl.when(spot_ref[0] == part ^ mask)
                def _(part=part):
                    for far in range(deep):
                        start = (far * 4 + part) * shard
                        to = 3 * tile + far * shard
                        sent_ref[:, to : to + shard] = grad_ref[0:own, start : start + shard]


def unmixing(grad, weight, kept, taps, seqs, length, shard, spot):
    rows, width = grad.shape
    channels = weight.shape[0]
    tile, deep = channels // 4, width // (4 * shard)
    wide = 3 * tile + deep * shard
    block = pl.BlockSpec((seqs * length, wide), lambda i, p: (0, 0))
    return pl.pallas_call(
        functools.partial(unmixing_kernel, (seqs, length, deep, shard)),
        grid_spec=pltpu.PrefetchScalarGridSpec(
            num_scalar_prefetch=1,
            grid=(4,),
            in_specs=[
                pl.BlockSpec((rows, width), lambda i, p: (0, 0)),
                pl.BlockSpec((tile, width), lambda i, p: (i ^ p[0], 0)),
                pl.BlockSpec((4, rows, tile), lambda i, p: (0, 0, i ^ p[0])),
                pl.BlockSpec((3, tile), lambda i, p: (0, i ^ p[0])),
            ],
            out_specs=[block] * 4 + [pl.BlockSpec((3, tile), lambda i, p: (0, i ^ p[0]))],
            scratch_shapes=[pltpu.VMEM((seqs, length + 8, tile), full)] * 2,
        ),
        out_shape=[jax.ShapeDtypeStruct((seqs * length, wide), low)] * 4
        + [jax.ShapeDtypeStruct((3, channels), full)],
        compiler_params=params,
        cost_estimate=brief,
    )(spot, grad, weight, kept, taps)


def unprojected_kernel(spot_ref, *refs):
    *sent, weight_ref, out_ref, total = refs
    step = pl.program_id(0)
    tile = weight_ref.shape[2]
    for mask, sent_ref in enumerate(sent):

        @pl.when(step == mask)
        def _(mask=mask, sent_ref=sent_ref):
            term = sum(
                dot(sent_ref[:, k * tile : (k + 1) * tile], weight_ref[k], flipped)
                for k in range(3)
            )
            total[...] = term if mask == 0 else total[...] + term

    @pl.when(step == len(sent) - 1)
    def _():
        out_ref[...] = total[...].astype(low)


def unprojected(sent, weight, spot):
    rows = sent[0].shape[0]
    width, channels = weight.shape[1:]
    tile = channels // 4
    return pl.pallas_call(
        unprojected_kernel,
        grid_spec=pltpu.PrefetchScalarGridSpec(
            num_scalar_prefetch=1,
            grid=(4,),
            in_specs=[pl.BlockSpec((rows, 3 * tile), lambda i, p: (0, 0))] * 4
            + [pl.BlockSpec((3, width, tile), lambda i, p: (0, 0, i ^ p[0]))],
            out_specs=pl.BlockSpec((rows, width), lambda i, p: (0, 0)),
            scratch_shapes=[pltpu.VMEM((rows, width), full)],
        ),
        out_shape=jax.ShapeDtypeStruct((rows, width), low),
        compiler_params=params,
        cost_estimate=brief,
    )(spot, *sent, weight)


def in_terms_kernel(cores, facts_ref, *refs):
    sent, rights, (out_ref, gathered, turned_rows) = refs[:4], refs[4 : 4 + cores], refs[4 + cores :]
    chips, count, shard = out_ref.shape
    rows = sent[0].shape[0]
    share = rows // cores

    @pl.when(pl.program_id(0) == 0)
    def _():
        for index in range(cores):
            core = lax.rem(facts_ref[1] + cores - index, cores)
            start = pl.multiple_of(core * share, 16)
            for mask, ref in enumerate(sent):
                place = pl.multiple_of((facts_ref[0] ^ mask) * share, 16)
                gathered[pl.ds(place, share)] = ref[pl.ds(start, share), :]
            turned_rows[index] = gathered[...].T

    total = sum(
        dot(turned_rows[index], rights[index][...].reshape(chips * share, chips * shard), plain)
        for index in range(cores)
    )
    for j in range(chips):
        out_ref[j] = total[:, j * shard : (j + 1) * shard].astype(low)


def in_weight_terms(sent, count, rights, shard, spot):
    rows = sent[0].shape[0]
    cores = len(rights)
    chips, _, share, half = rights[0].shape
    tile = chips * shard
    tiles = half // tile
    facts = jnp.concatenate([spot, lax.axis_index("mp").astype(jnp.int32).reshape(1)])
    right = pl.BlockSpec((chips, 1, share, tile), lambda i, p: (0, i // tiles, 0, i % tiles))
    return pl.pallas_call(
        functools.partial(in_terms_kernel, cores),
        grid_spec=pltpu.PrefetchScalarGridSpec(
            num_scalar_prefetch=1,
            grid=(2 * tiles,),
            in_specs=[pl.BlockSpec((rows, count), lambda i, p: (0, 0))] * chips + [right] * cores,
            out_specs=pl.BlockSpec((chips, count, shard), lambda i, p: (i, 0, 0)),
            scratch_shapes=[
                pltpu.VMEM((chips * share, count), low),
                pltpu.VMEM((cores, count, chips * share), low),
            ],
        ),
        out_shape=jax.ShapeDtypeStruct((2 * tiles * chips, count, shard), low),
        compiler_params=params,
        cost_estimate=brief,
    )(facts, *sent, *rights)


def out_terms_kernel(facts_ref, *refs):
    *sent, mixed_ref, out_ref, columns = refs
    chips, rows, channels = mixed_ref.shape
    shard = out_ref.shape[2]
    deep = out_ref.shape[0]
    first = sent[0].shape[1] - deep * shard
    for mask, ref in enumerate(sent):
        place = pl.multiple_of((facts_ref[0] ^ mask) * rows, 16)
        columns[pl.ds(place, rows)] = ref[:, first:]
    total = dot(mixed_ref[...].reshape(chips * rows, channels).T, columns[...], plain)
    for far in range(deep):
        out_ref[far] = total[:, far * shard : (far + 1) * shard].astype(low)


def out_weight_terms(sent, count, shown, channels, shard, spot):
    rows, wide = sent[0].shape
    chips = shown.shape[0]
    deep = (wide - count) // shard
    return pl.pallas_call(
        out_terms_kernel,
        grid_spec=pltpu.PrefetchScalarGridSpec(
            num_scalar_prefetch=1,
            grid=(1,),
            in_specs=[pl.BlockSpec((rows, wide), lambda i, p: (0, 0))] * chips
            + [pl.BlockSpec((chips, rows, channels), lambda i, p: (0, 0, 0))],
            out_specs=pl.BlockSpec((deep, channels, shard), lambda i, p: (0, 0, 0)),
            scratch_shapes=[pltpu.VMEM((chips * rows, deep * shard), low)],
        ),
        out_shape=jax.ShapeDtypeStruct((deep, channels, shard), low),
        compiler_params=params,
        cost_estimate=brief,
    )(spot, *sent, shown)


def placing_kernel(parts, *refs):
    placed_ref, pair_ref, down_ref = refs[0], refs[-2], refs[-1]
    chips, three, _ = placed_ref.shape
    chips //= parts
    own = three // 3
    for chip in range(chips):
        block = sum(placed_ref[part * chips + chip].astype(full) for part in range(parts))
        rows = slice(chip * own, (chip + 1) * own)
        pair_ref[:, 0, rows] = block[:own].T
        pair_ref[:, 1, rows] = block[own : 2 * own].T
        down_ref[rows] = block[2 * own :]


def put_in_place(placed, parts, index, groups, before):
    chips, three, shard = placed.shape
    columns = chips // parts * three // 3
    return pl.pallas_call(
        functools.partial(placing_kernel, parts),
        grid=(1,),
        in_specs=[pl.BlockSpec(placed.shape, lambda i: (0, 0, 0))]
        + [pl.BlockSpec(memory_space=pl.ANY)] * len(before),
        out_specs=[
            pl.BlockSpec((shard, 2, columns), lambda i: (0, 0, index)),
            pl.BlockSpec((columns, shard), lambda i: (index, 0)),
        ],
        out_shape=[
            jax.ShapeDtypeStruct((shard, 2, groups * columns), full),
            jax.ShapeDtypeStruct((groups * columns, shard), full),
        ],
        input_output_aliases={1 + n: n for n in range(len(before))},
        compiler_params=params,
        cost_estimate=brief,
    )(placed, *before)


def product_kernel(left_ref, right_ref, out_ref, total):
    step = pl.program_id(0)
    term = dot(left_ref[...], right_ref[...], plain)

    @pl.when(step == 0)
    def _():
        total[...] = term

    @pl.when(step > 0)
    def _():
        total[...] += term

    @pl.when(step == pl.num_programs(0) - 1)
    def _():
        out_ref[...] = total[...].astype(low)


def product_of(left, right):
    rows, depth = left.shape
    width = right.shape[1]
    tile = min(1024, depth)
    return pl.pallas_call(
        product_kernel,
        grid=(depth // tile,),
        in_specs=[
            pl.BlockSpec((rows, tile), lambda i: (0, i)),
            pl.BlockSpec((tile, width), lambda i: (i, 0)),
        ],
        out_specs=pl.BlockSpec((rows, width), lambda i: (0, 0)),
        out_shape=jax.ShapeDtypeStruct((rows, width), low),
        scratch_shapes=[pltpu.VMEM((rows, width), full)],
        compiler_params=params,
        cost_estimate=brief,
    )(left, right)


def tokens_grad_kernel(core_ref, values_ref, inv_ref, gain_ref, inner_ref, *refs):
    parts, (out_ref, sums_ref) = refs[:-2], refs[-2:]
    upstream = sum(ref[...].astype(full) for ref in parts)
    scaled = values_ref[...] * inv_ref[...]
    weighted = upstream * gain_ref[...]
    inner_mean = jnp.mean(weighted * scaled, axis=-1, keepdims=True)
    out_ref[...] = (inner_ref[...] + inv_ref[...] * (weighted - scaled * inner_mean)).astype(low)

    @pl.when(pl.program_id(0) == core_ref[0])
    def _():
        sums_ref[...] = jnp.sum(upstream * scaled, axis=0, keepdims=True)


def tokens_grad_of(values, inv_rms, gain_vec, inner_grad, parts, rows, cores):
    width = values.shape[1]
    share = rows // cores
    core = lax.axis_index("mp").astype(jnp.int32).reshape(1)
    block = pl.BlockSpec((share, width), lambda i, p: (i, 0))
    line = pl.BlockSpec((1, width), lambda i, p: (0, 0))
    return pl.pallas_call(
        tokens_grad_kernel,
        grid_spec=pltpu.PrefetchScalarGridSpec(
            num_scalar_prefetch=1,
            grid=(cores,),
            in_specs=[block, pl.BlockSpec((share, 1), lambda i, p: (i, 0)), line, block]
            + [block] * len(parts),
            out_specs=[block, line],
        ),
        out_shape=[
            jax.ShapeDtypeStruct((rows, width), low),
            jax.ShapeDtypeStruct((1, width), full),
        ],
        compiler_params=params,
        cost_estimate=brief,
    )(core, values, inv_rms, gain_vec.reshape(1, -1), inner_grad, *parts)


def local(
    tokens,
    norm1_gain,
    in_weight,
    conv_weight,
    out_weight,
    norm2_gain,
    gate_up,
    down_weight,
    cotangent,
):
    seq_count, local_len, width = tokens.shape
    row_total = seq_count * local_len
    channels = in_weight.shape[2]
    hidden = gate_up.shape[2]
    parts = lax.axis_size("a")
    cores = lax.axis_size("mp")
    shard = width // (parts * 8)
    deep = width // (4 * shard)
    quarter = channels // 4
    cube, plane, column = ("b", "c", "d"), ("c", "d"), ("a", "b")
    place = lax.axis_index(cube).astype(jnp.int32).reshape(1)
    own = hidden // 8
    in_parts = jnp.transpose(in_weight, (1, 0, 2))

    after = passed_along(
        jnp.stack([tokens[:, :2], cotangent[:, :2]]), column + plane, -1
    ).reshape(2, -1, width)
    before = passed_along(tokens[:, local_len - 2 :], column + plane, 1).reshape(-1, width)
    side = before.shape[0]
    padding = jnp.zeros((2 * side + (-2 * side) % 16, width), low)
    before, upstream_mine = tied(before, share_of(cotangent.reshape(row_total, width)))
    inputs = jnp.concatenate(
        [tokens.reshape(row_total, width), after[0], before, padding[2 * side :]]
    ).astype(full)
    upstream_own = cotangent.reshape(row_total, width)
    upstream_after = jnp.concatenate([after[1], padding[side:]])
    upstream_grad = jnp.concatenate([upstream_own, upstream_after]).astype(full)
    normed_full_one, inv_rms_one = normalize(inputs, norm1_gain)
    normed_one = normed_full_one.astype(low)
    upstream_opposite = opposite(upstream_mine)
    mixed, mixer_state = mixing(normed_one, in_parts, conv_weight, seq_count, local_len)
    mixed, upstream_opposite = tied(mixed, upstream_opposite)
    inner_sum = inputs + summed(dot(mixed, out_weight, plain))
    normed_full_two, inv_rms_two = normalize(inner_sum, norm2_gain)
    normed_two = normed_full_two.astype(low)

    groups = 2 if own > 256 else 1
    half_width = width // 2
    part = own // groups
    unit = row_total // cores
    normed_mine = share_of(normed_two[:row_total])
    together = in_rows([normed_mine, upstream_mine], [(0, 1)])[0]
    from_near = near(together)
    firsts = [(index * 8 + place[0]) * part for index in range(groups)]
    down_own = jnp.stack(
        [lax.dynamic_slice_in_dim(down_weight, first, part, 0) for first in firsts]
    )
    downs = [down_own] + others(down_own, "mp")
    gate_up, together = tied(gate_up, together)
    pair_weight = lax.optimization_barrier(jnp.transpose(gate_up, (1, 0, 2)))
    pair_weight, normed_mine, *arrived = tied(
        pair_weight, normed_mine, *from_near, *downs[1:]
    )
    from_near, downs[1:] = arrived[:3], arrived[3:]
    from_beyond = beyond(from_near, "cdb")
    normed_opposite = opposite(normed_mine)
    pairs = [own_columns(pair_weight, place, part, 0)]
    pairs[0] = [pairs[0]] + others(pairs[0], "mp")
    pair_weight, pairs[0][0] = tied(pair_weight, pairs[0][0])
    activation, normed_two_part = both_ways(
        normed_two, upstream_own, upstream_after, pair_weight, down_weight
    )
    activation, normed_two_part, normed_opposite, *arrived = tied(
        activation, normed_two_part, normed_opposite, *from_beyond, *pairs[0][1:]
    )
    from_beyond, pairs[0][1:] = arrived[:3], arrived[3:]
    latest = []

    def in_turn(*values):
        values = tied(*values, *latest)[: len(values)]
        return values if len(values) > 1 else values[0]

    def over(*values):
        latest[:] = values

    over(normed_two_part, activation)
    normed_one, mixed = in_turn(normed_one, mixed)
    one_mine = share_of(normed_one[:row_total])
    shown = jnp.stack([one_mine[:, :half_width], one_mine[:, half_width:]])
    spare = ((0, 0), (0, half_width - channels))
    shown = jnp.concatenate([jnp.pad(mixed[:row_total], spare), shown.reshape(-1, half_width)])
    shown = lax.all_gather(in_turn(shown), plane)
    normed_two_grad = summed(normed_two_part)

    gathered = [together] + from_near + from_beyond
    normed_all, upstream_all, *blocks = first_hidden(
        [(rows, 0) for rows in gathered] + [(normed_opposite, 0)],
        [(rows, unit) for rows in gathered] + [(upstream_opposite, 0)],
        unit,
        [in_turn(pairs[0][1])] + pairs[0][2:],
        downs[1:],
        shard,
    )

    def of_others(rows):
        blocks = []
        for core in range(1, cores):
            blocks.append(weight_terms(in_turn(rows), normed_all, upstream_all, shard, core))
            over(blocks[-1])
        return [turned(block, "mp", -core - 1) for core, block in enumerate(blocks)]

    def of_mine(rows, received):
        block = weight_terms(in_turn(rows), normed_all, upstream_all, shard, 0, received)
        over(block)
        return block

    over(*blocks)
    received = [turned(block, "mp", -core - 1) for core, block in enumerate(blocks)]
    hidden_rows = next_hidden(in_turn(normed_all), upstream_all, pairs[0][:1], downs[:1], 0)
    over(hidden_rows)
    block = of_mine(hidden_rows, received)
    placed = shared_out(block, column + plane)
    if groups > 1:
        next_pair = own_columns(in_turn(pair_weight), place, part, 1)
        over(next_pair)
        pairs.append([next_pair] + others(next_pair, "mp"))
    normed_two_grad = in_turn(normed_two_grad)
    inner_grad = upstream_grad + norm_back(inner_sum, inv_rms_two, norm2_gain, normed_two_grad)
    branch_grad = inner_grad.astype(low)
    over(branch_grad)
    if groups > 1:
        next_rows = next_hidden(in_turn(normed_all), upstream_all, pairs[1], downs, 1)
        over(next_rows)
        received = of_others(next_rows)
    spot = lax.axis_index(plane).astype(jnp.int32).reshape(1)
    *sent, taps_grad = unmixing(
        in_turn(branch_grad), out_weight, mixer_state, conv_weight, seq_count, local_len, shard, spot
    )
    over(*sent)
    seen = [sent[0], swapped(in_turn(sent[1]), "d"), swapped(in_turn(sent[2]), "c")]
    if groups > 1:
        next_block = of_mine(next_rows, received)
    one_all = [in_turn(shown)[:, row_total:].reshape(4, 2, unit, half_width)]
    over(*latest, *seen, one_all[0], placed)
    if groups > 1:
        next_placed = shared_out(in_turn(next_block), column + plane)
    one_all += others(one_all[0], "mp")
    seen.append(lax.ppermute(in_turn(sent[3]), plane, [(i, 3 - i) for i in range(4)]))
    normed_one_part = unprojected([in_turn(sent[0])] + sent[1:], in_parts, spot)
    over(normed_one_part, *one_all[1:], seen[3])
    seen[0] = in_turn(seen[0])
    in_terms = in_weight_terms(seen, 3 * quarter, one_all, shard, spot)
    over(in_terms)
    if groups > 1:
        over(in_terms, next_placed)
    in_total = shared_out(in_turn(in_terms), column + plane)
    out_terms = out_weight_terms(
        [in_turn(seen[0])] + seen[1:], 3 * quarter, shown, channels, shard, spot
    )
    over(out_terms)
    out_total = lax.psum_scatter(out_terms, column, scatter_dimension=0).astype(full)
    totals = put_in_place(placed, parts, 0, groups, ())
    if groups > 1:
        totals = put_in_place(next_placed, parts, 1, groups, totals)
    gate_up_total, down_total = totals
    parts_one = both_parts(in_turn(normed_one_part))
    tokens_grad, gain_one = tokens_grad_of(
        inputs, inv_rms_one, norm1_gain, inner_grad, parts_one, row_total, cores
    )
    gain_two = jnp.sum(
        share_of((normed_two_grad * inner_sum * inv_rms_two)[:row_total]), axis=0
    )
    channel_start = lax.axis_index("mp") * channels
    taps_full = lax.dynamic_update_slice_in_dim(
        jnp.zeros((3, width), full), taps_grad, channel_start, 1
    )
    small = jnp.concatenate([gain_one, gain_two[None], taps_full], axis=0)
    for axes in (("mp",), plane, column):
        if lax.axis_size(axes) <= 4:
            small = over_all(small, axes)
        else:
            small = lax.psum(small, axes)
    output_part = product_of(in_turn(activation), down_weight)
    output = (inner_sum + summed(output_part))[:row_total].astype(low)
    in_total = (
        jnp.sum(in_total.astype(full).reshape(-1, 4, 3, quarter, shard), axis=0)
        .transpose(3, 1, 0, 2)
        .reshape(shard, 3, channels)
    )
    taps_total = lax.dynamic_slice_in_dim(small[2:], channel_start, channels, 1)
    return (
        output.reshape(seq_count, local_len, width),
        tokens_grad.reshape(seq_count, local_len, width),
        small[0],
        in_total,
        taps_total,
        out_total,
        small[1],
        gate_up_total,
        down_total,
    )


def solution(mesh):
    seq, mp = mesh.shape["seq"], mesh.shape["mp"]
    fine = Mesh(mesh.devices.reshape(seq // 8, 2, 2, 2, mp), ("a", "b", "c", "d", "mp"))
    by_seq = ("a", "b", "c", "d")
    return jax.shard_map(
        local,
        mesh=fine,
        in_specs=(
            P(None, by_seq, None),
            P(),
            P(None, None, "mp"),
            P(None, "mp"),
            P("mp", None),
            P(),
            P(None, None, "mp"),
            P("mp", None),
            P(None, by_seq, None),
        ),
        out_specs=(
            P(None, by_seq, None),
            P(None, by_seq, None),
            P(),
            P(by_seq, None, "mp"),
            P(None, "mp"),
            P("mp", by_seq),
            P(),
            P(by_seq, None, "mp"),
            P("mp", by_seq),
        ),
        check_vma=False,
    )
```
